32 devices in a mesh: dp: 16 (over z, y, x), rep: 2 (over core).
Axes of the slice: x: 2, y: 2, z: 4, core: 2. Of those that a mesh axis runs over, the one named last changes fastest.
Arguments:
- tokens: bfloat16 [16384, 1024], P(('dp', 'rep')), may hold values from -6 to 6
- kept_patch: int32 [16384], P(('dp', 'rep')), may hold values from 0 to 195
- image_lengths: int32 [32, 16], P(('dp', 'rep')), may hold values from 0 to 64, as said below
- ground_distance: int32 [32, 16], P(('dp', 'rep')), may hold values from 1 to 30
- cotangent: bfloat16 [16384, 1024], P(('dp', 'rep')), may hold values from -6 to 6
- norm_one_gain: bfloat16 [1024], P('dp'), may hold values from 0.5 to 1.5
- norm_one_bias: bfloat16 [1024], P('dp'), may hold values from -1.5 to 1.5
- joint_weight: bfloat16 [1024, 3072], P('dp'), may hold values from -0.1875 to 0.1875
- joint_bias: bfloat16 [3072], P('dp'), may hold values from -1.5 to 1.5
- merge_weight: bfloat16 [1024, 1024], P('dp'), may hold values from -0.5 to 0.5
- merge_bias: bfloat16 [1024], P('dp'), may hold values from -1.5 to 1.5
- norm_two_gain: bfloat16 [1024], P('dp'), may hold values from 0.5 to 1.5
- norm_two_bias: bfloat16 [1024], P('dp'), may hold values from -1.5 to 1.5
- expand_weight: bfloat16 [1024, 4096], P('dp'), may hold values from -0.1875 to 0.1875
- expand_bias: bfloat16 [4096], P('dp'), may hold values from -1.5 to 1.5
- shrink_weight: bfloat16 [4096, 1024], P('dp'), may hold values from -0.125 to 0.125
- shrink_bias: bfloat16 [1024], P('dp'), may hold values from -1.5 to 1.5
Outputs:
- output: bfloat16 [16384, 1024], P(('dp', 'rep'))
- grad_tokens: float32 [16384, 1024], P(('dp', 'rep'))
- grad_norm_one_gain: float32 [1024], P('dp')
- grad_norm_one_bias: float32 [1024], P('dp')
- grad_joint_weight: float32 [1024, 3072], P('dp')
- grad_joint_bias: float32 [3072], P('dp')
- grad_merge_weight: float32 [1024, 1024], P('dp')
- grad_merge_bias: float32 [1024], P('dp')
- grad_norm_two_gain: float32 [1024], P('dp')
- grad_norm_two_bias: float32 [1024], P('dp')
- grad_expand_weight: float32 [1024, 4096], P('dp')
- grad_expand_bias: float32 [4096], P('dp')
- grad_shrink_weight: float32 [4096, 1024], P('dp')
- grad_shrink_bias: float32 [1024], P('dp')
The draws below stay inside these ranges and needn't reach their ends.
Inputs may be any that keep to these rules, and one draw needn't show every extreme that they name: In each row of image_lengths the slots are filled in order until 512 rows or fewer are used, the last image may be cut, later slots are 0 and the remaining rows are padding; some device has no padding rows and some slot holds 64 patches.
All inputs are finite; a program needn't handle non-finite values.
Results may differ from the reference program's by a relative error of at most 0.014.
Values may be sent and summed in bfloat16 or wider, within the bound.
A program may use at most 192 MiB of HBM per device.

```python
from functools import partial
import jax
import jax.numpy as jnp
from jax import lax

D = 1024
FF = 4096
HD = 64
TOK_DEV = 512
MOST = 64
MIN_VIS = 34
IMG_DEV = 16
TOKENS = 16384
N_DP = 16
N_REP = 2


def draw_image_lengths(key, part):
    key = jax.random.fold_in(key, 11)
    devices = N_DP * N_REP
    first_key, second_key, third_key = jax.random.split(key, 3)
    full_lengths = jax.random.randint(first_key, (devices, IMG_DEV), MIN_VIS, MOST + 1)
    live_count = jax.random.randint(second_key, (devices,), TOK_DEV - TOK_DEV // 4, TOK_DEV + 1)
    chosen = jax.random.randint(third_key, (), 0, devices)
    device_ids = jnp.arange(devices)
    live_count = jnp.where(device_ids == chosen, TOK_DEV, live_count)
    full_lengths = full_lengths.at[chosen, 0].set(MOST)
    starts = jnp.cumsum(full_lengths, axis=1) - full_lengths
    cut = jnp.clip(live_count[:, None] - starts, 0, full_lengths)
    return cut.astype(jnp.int32)


def touch_ends(drawn, stream_key, low, largest):
    place = [jax.random.randint(jax.random.fold_in(stream_key, axis), (), 0, length) for axis, length in enumerate(drawn.shape)]
    widest = drawn.shape.index(max(drawn.shape))
    beside = place[:widest] + [(place[widest] + 1) % drawn.shape[widest]] + place[widest + 1:]
    return drawn.at[tuple(place)].set(low).at[tuple(beside)].set(largest)


def raised(drawn, own_key, source, target, shards_of, factor):
    def block_of(dim):
        return (jnp.arange(drawn.shape[dim]) // (drawn.shape[dim] // shards_of)).reshape((-1,) + (1,) * (drawn.ndim - 1 - dim))

    near = jax.random.permutation(own_key, shards_of)[block_of(target)]
    other_side = (block_of(target) + shards_of // 2) % shards_of
    return jnp.where((block_of(source) == near) | (block_of(source) == other_side), factor * drawn, drawn)


def level_of(key, dims, cuts, least, top_value):
    level, own = 1.0, jax.random.fold_in(key, 6)
    for dim, shards_of in cuts:
        draws = jnp.exp(jax.random.uniform(jax.random.fold_in(own, dim), (shards_of,), jnp.float32, least / len(cuts), top_value / len(cuts)))
        level = level * jnp.repeat(draws, dims[dim] // shards_of).reshape([-1 if axis == dim else 1 for axis in range(len(dims))])
    return level


def normal_values(rng, extent, deviation, bound, shards=(), held_as=jnp.bfloat16):
    loudness = level_of(rng, extent, shards, -0.22, 0.18) if shards else 1.0
    values = jax.random.normal(rng, extent, jnp.float32) * deviation * loudness
    return jnp.minimum(jnp.maximum(values, -bound), bound).astype(held_as)


def noise_with(own_key, extent, scale, reach, cuts, heavy, kind=jnp.bfloat16):
    drawn = scale * jax.random.normal(own_key, extent, jnp.float32)
    if cuts:
        drawn = drawn * level_of(own_key, extent, cuts, -0.22, 0.18)
    return jnp.clip(raised(drawn, jax.random.fold_in(own_key, 3), *heavy), -reach, reach).astype(kind)


def setup_inputs(seed: int = 0) -> dict:
    seeds = jax.random.split(jax.random.key(seed), 18)
    tokens = noise_with(seeds[0], (TOKENS, D), 1.0, 6.0, ((0, 32),), (0, 1, 32, 2.75))
    kept_patch = touch_ends(jax.random.randint(seeds[1], (TOKENS,), 0, 196), jax.random.fold_in(seeds[1], 1), 0, 195).astype(jnp.int32)
    image_lengths = draw_image_lengths(jax.random.fold_in(seeds[17], 71), 0)
    ground_distance = touch_ends(jax.random.randint(seeds[3], (N_DP * N_REP, IMG_DEV), 1, 31), jax.random.fold_in(seeds[3], 1), 1, 30).astype(jnp.int32)
    cotangent = noise_with(seeds[4], (TOKENS, D), 1.0, 6.0, ((0, 32),), (0, 1, 32, 2.75))
    norm_one_gain = jnp.clip(1.0 + 0.1 * jax.random.normal(seeds[5], (D,), jnp.float32), 0.5, 1.5).astype(jnp.bfloat16)
    norm_one_bias = normal_values(seeds[6], (D,), 0.3, 1.5, ((0, 16),))
    joint_weight = normal_values(seeds[7], (D, 3 * D), D ** -0.5, 0.1875, ((0, 16),))
    joint_bias = normal_values(seeds[8], (3 * D,), 0.3, 1.5, ((0, 16),))
    merge_weight = normal_values(seeds[9], (D, D), (D // 8) ** -0.5, 0.5, ((0, 16),))
    merge_bias = normal_values(seeds[10], (D,), 0.3, 1.5, ((0, 16),))
    norm_two_gain = jnp.clip(1.0 + 0.1 * jax.random.normal(seeds[11], (D,), jnp.float32), 0.5, 1.5).astype(jnp.bfloat16)
    norm_two_bias = normal_values(seeds[12], (D,), 0.3, 1.5, ((0, 16),))
    expand_weight = normal_values(seeds[13], (D, FF), D ** -0.5, 0.1875, ((0, 16),))
    expand_bias = normal_values(seeds[14], (FF,), 0.3, 1.5, ((0, 16),))
    shrink_weight = normal_values(seeds[15], (FF, D), (FF // 2) ** -0.5, 0.125, ((0, 16),))
    shrink_bias = normal_values(seeds[16], (D,), 0.3, 1.5, ((0, 16),))
    return dict(tokens=tokens, kept_patch=kept_patch, image_lengths=image_lengths, ground_distance=ground_distance, cotangent=cotangent, norm_one_gain=norm_one_gain, norm_one_bias=norm_one_bias, joint_weight=joint_weight, joint_bias=joint_bias, merge_weight=merge_weight, merge_bias=merge_bias, norm_two_gain=norm_two_gain, norm_two_bias=norm_two_bias, expand_weight=expand_weight, expand_bias=expand_bias, shrink_weight=shrink_weight, shrink_bias=shrink_bias)


highest = lax.Precision.HIGHEST

@jax.custom_vjp
def low(v):
    return lax.optimization_barrier(v.astype(jnp.bfloat16)).astype(jnp.float32)

@jax.custom_vjp
def low_back(v):
    return v

def low_keep(v):
    return (low(v), None)

def low_pass(kept, grad):
    return (grad,)

def back_keep(v):
    return (v, None)

def back_low(kept, grad):
    return (low(grad),)
low.defvjp(low_keep, low_pass)
low_back.defvjp(back_keep, back_low)

def packing(lengths, row_count):
    image_ends = jnp.cumsum(lengths).astype(jnp.int32)
    row_ids = jnp.arange(row_count, dtype=jnp.int32)
    segment = lax.optimization_barrier(jnp.sum((image_ends[None, :] <= row_ids[:, None]).astype(jnp.int32), axis=1))
    live_rows = (row_ids < image_ends[-1]).astype(jnp.float32)
    return (segment, live_rows)

def row_distance(segment, distances):
    slots = jnp.arange(distances.shape[-1], dtype=jnp.int32)
    onehot = (segment[:, None] == slots[None, :]).astype(jnp.float32)
    return lax.optimization_barrier(jnp.sum(onehot * distances[None, :].astype(jnp.float32), axis=1))

def positions(patch_index, ground_rows, model_width):
    quarter = model_width // 4
    frequency = 1.0 / 10000.0 ** (jnp.arange(quarter, dtype=jnp.float32) / quarter)
    factor = ground_rows / 10.0
    across_rows = ((patch_index // 14).astype(jnp.float32) * factor)[..., None] * frequency
    along_rows = ((patch_index % 14).astype(jnp.float32) * factor)[..., None] * frequency
    return jnp.concatenate([jnp.sin(across_rows), jnp.cos(across_rows), jnp.sin(along_rows), jnp.cos(along_rows)], axis=-1)

def norm_rows(hidden, scaling, offset):
    center = hidden - lax.optimization_barrier(jnp.mean(hidden, axis=-1, keepdims=True))
    spread = lax.optimization_barrier(jnp.mean(center * center, axis=-1, keepdims=True))
    return center * lax.rsqrt(spread + 1e-06) * scaling + offset

def matmul(left, right):
    return jnp.dot(left, right, precision=highest)

def device_layer(params, device_item):
    gain_one, bias_one, joint_matrix, joint_offset, merge_matrix, merge_offset, gain_two, bias_two, expand_matrix, expand_offset, shrink_matrix, shrink_offset = params
    tokens_rows, pos_rows, segment, live_rows = device_item
    row_count = tokens_rows.shape[0]
    model_width = tokens_rows.shape[1]
    head_count = model_width // HD
    residual_in = tokens_rows + pos_rows
    normed = low(norm_rows(residual_in, gain_one, bias_one))
    projected = low_back(low(matmul(normed, joint_matrix) + joint_offset))
    queries = projected[:, :model_width].reshape(row_count, head_count, HD)
    key_rows = projected[:, model_width:2 * model_width].reshape(row_count, head_count, HD)
    value_rows = projected[:, 2 * model_width:].reshape(row_count, head_count, HD)
    scores = low_back(jnp.einsum('qhd,khd->hqk', queries, key_rows, precision=highest)) * HD ** (-0.5)
    same_image = segment[:, None] == segment[None, :]
    scores = jnp.where(same_image[None], scores, -1000000000.0)
    softmax_rows = low(jax.nn.softmax(scores, axis=-1))
    attended = jnp.einsum('hqk,khd->qhd', softmax_rows, value_rows, precision=highest).reshape(row_count, model_width)
    attended = low_back(low(attended))
    branch = low_back(matmul(attended, merge_matrix) + merge_offset)
    middle = residual_in + branch
    second = low(norm_rows(middle, gain_two, bias_two))
    hidden_pre = low_back(matmul(second, expand_matrix) + expand_offset)
    active = low(jax.nn.gelu(hidden_pre, approximate=False))
    branch_mlp = low_back(matmul(active, shrink_matrix) + shrink_offset)
    return (middle + branch_mlp) * live_rows[:, None]

def reference(tokens, kept_patch, image_lengths, ground_distance, cotangent, norm_one_gain, norm_one_bias, joint_weight, joint_bias, merge_weight, merge_bias, norm_two_gain, norm_two_bias, expand_weight, expand_bias, shrink_weight, shrink_bias):
    devices = N_DP * N_REP
    segment, live_rows = jax.vmap(partial(packing, row_count=TOK_DEV))(image_lengths)
    ground_rows = jax.vmap(row_distance)(segment, ground_distance)
    pos_rows = positions(kept_patch.reshape(devices, TOK_DEV), ground_rows, D)
    params = tuple((item.astype(jnp.float32) for item in (norm_one_gain, norm_one_bias, joint_weight, joint_bias, merge_weight, merge_bias, norm_two_gain, norm_two_bias, expand_weight, expand_bias, shrink_weight, shrink_bias)))

    def forward(inputs, weights):
        blocks = inputs.reshape(devices, TOK_DEV, D)

        def one_device(device_item):
            return device_layer(weights, device_item)
        result = lax.map(jax.checkpoint(one_device), (blocks, pos_rows, segment, live_rows))
        return result.reshape(devices * TOK_DEV, D)
    output, pullback = jax.vjp(forward, tokens.astype(jnp.float32), params)
    grad_tokens, grads = pullback(cotangent.astype(jnp.float32))
    return (output.astype(jnp.bfloat16), grad_tokens, grads[0], grads[1], grads[2], grads[3], grads[4], grads[5], grads[6], grads[7], grads[8], grads[9], grads[10], grads[11])
```

```python
import functools

import jax
import jax.numpy as jnp
from jax import lax
from jax.experimental import pallas as pl
from jax.experimental.pallas import tpu as pltpu
from jax.sharding import PartitionSpec as P

HD = 64
MESH = pl.DeviceIdType.MESH
F32 = jnp.float32
BF16 = jnp.bfloat16
NEVER = -1000000000.0
VMEM_BYTES = 127 * 2**19
LAST = (((1,), (1,)), ((), ()))
FIRST = (((0,), (0,)), ((), ()))

def packing(lengths, row_count):
    image_ends = jnp.cumsum(lengths)
    row_ids = jnp.arange(row_count, dtype=jnp.int32)
    segment = jnp.sum((image_ends[None, :] <= row_ids[:, None]).astype(jnp.int32), axis=1)
    live_rows = (row_ids < image_ends[-1]).astype(jnp.float32)
    return (segment, live_rows)


def row_distance(segment, distances):
    slots = jnp.arange(distances.shape[-1], dtype=jnp.int32)
    onehot = (segment[:, None] == slots[None, :]).astype(jnp.float32)
    return jnp.sum(onehot * distances[None, :].astype(jnp.float32), axis=1)


def positions(patch_index, ground_rows, model_width):
    quarter = model_width // 4
    frequency = 1.0 / 10000.0 ** (jnp.arange(quarter, dtype=jnp.float32) / quarter)
    factor = ground_rows / 10.0
    across_rows = ((patch_index // 14).astype(jnp.float32) * factor)[..., None] * frequency
    along_rows = ((patch_index % 14).astype(jnp.float32) * factor)[..., None] * frequency
    return jnp.concatenate(
        [jnp.sin(across_rows), jnp.cos(across_rows), jnp.sin(along_rows), jnp.cos(along_rows)],
        axis=-1,
    )


def norm_forward(hidden, scaling, offset):
    center = hidden - jnp.mean(hidden, axis=-1, keepdims=True)
    inverse = lax.rsqrt(jnp.mean(center * center, axis=-1, keepdims=True) + 1e-06)
    scaled = center * inverse
    return (scaled * scaling.astype(jnp.float32) + offset.astype(jnp.float32), scaled, inverse)


def norm_backward(incoming, scaled, inverse, scaling):
    grad_scaled = incoming * scaling.astype(jnp.float32)
    centered_grad = grad_scaled - jnp.mean(grad_scaled, axis=-1, keepdims=True)
    centered_grad = centered_grad - scaled * jnp.mean(grad_scaled * scaled, axis=-1, keepdims=True)
    return (centered_grad * inverse, jnp.sum(incoming * scaled, axis=0), jnp.sum(incoming, axis=0))


def gelu_slope(hidden_pre):
    normal_cdf = 0.5 * (1.0 + jax.scipy.special.erf(hidden_pre * 0.7071067811865476))
    density = jnp.exp(-0.5 * hidden_pre * hidden_pre) * 0.3989422804014327
    return normal_cdf + hidden_pre * density


def general_layer(
    tokens,
    kept_patch,
    image_lengths,
    ground_distance,
    cotangent,
    norm_one_gain,
    norm_one_bias,
    joint_weight,
    joint_bias,
    merge_weight,
    merge_bias,
    norm_two_gain,
    norm_two_bias,
    expand_weight,
    expand_bias,
    shrink_weight,
    shrink_bias,
):
    full = (
        lax.all_gather(norm_one_gain, "dp", axis=0, tiled=True),
        lax.all_gather(norm_one_bias, "dp", axis=0, tiled=True),
        lax.all_gather(joint_weight, "dp", axis=0, tiled=True),
        lax.all_gather(joint_bias, "dp", axis=0, tiled=True),
        lax.all_gather(merge_weight, "dp", axis=0, tiled=True),
        lax.all_gather(merge_bias, "dp", axis=0, tiled=True),
        lax.all_gather(norm_two_gain, "dp", axis=0, tiled=True),
        lax.all_gather(norm_two_bias, "dp", axis=0, tiled=True),
        lax.all_gather(expand_weight, "dp", axis=0, tiled=True),
        lax.all_gather(expand_bias, "dp", axis=0, tiled=True),
        lax.all_gather(shrink_weight, "dp", axis=0, tiled=True),
        lax.all_gather(shrink_bias, "dp", axis=0, tiled=True),
    )
    row_count = tokens.shape[0]
    model_width = tokens.shape[1]
    head_count = model_width // HD
    segment, live_rows = packing(image_lengths[0], row_count)
    ground_rows = row_distance(segment, ground_distance[0])
    residual_in = tokens.astype(jnp.float32) + positions(kept_patch, ground_rows, model_width)
    first, scaled_one, inverse_one = norm_forward(residual_in, full[0], full[1])
    first_low = first.astype(jnp.bfloat16)
    projected = (
        jnp.dot(first_low, full[2], preferred_element_type=jnp.float32)
        + full[3].astype(jnp.float32)
    ).astype(jnp.bfloat16)
    queries = projected[:, :model_width].reshape(row_count, head_count, HD)
    key_rows = projected[:, model_width : 2 * model_width].reshape(row_count, head_count, HD)
    value_rows = projected[:, 2 * model_width :].reshape(row_count, head_count, HD)
    score_scale = HD ** (-0.5)

    def block_scores():
        raw_scores = (
            jnp.einsum("qhd,khd->hqk", queries, key_rows, preferred_element_type=jnp.float32)
            * score_scale
        )
        same_image = segment[:, None] == segment[None, :]
        return jnp.where(same_image[None], raw_scores, -1000000000.0)

    scores = block_scores()
    highest_score = jnp.max(scores, axis=-1, keepdims=True)
    exponent = jnp.exp(scores - highest_score)
    row_total = jnp.sum(exponent, axis=-1, keepdims=True)
    softmax_rows = exponent / row_total
    log_totals = highest_score + jnp.log(row_total)
    attended_parts = jnp.einsum(
        "hqk,khd->qhd",
        softmax_rows.astype(jnp.bfloat16),
        value_rows,
        preferred_element_type=jnp.float32,
    )
    attended = attended_parts.reshape(row_count, model_width).astype(jnp.bfloat16)
    branch = jnp.dot(attended, full[4], preferred_element_type=jnp.float32) + full[5].astype(
        jnp.float32
    )
    middle = residual_in + branch
    second, scaled_two, inverse_two = norm_forward(middle, full[6], full[7])
    second_low = second.astype(jnp.bfloat16)
    hidden_pre = jnp.dot(second_low, full[8], preferred_element_type=jnp.float32) + full[9].astype(
        jnp.float32
    )
    active_low = jax.nn.gelu(hidden_pre, approximate=False).astype(jnp.bfloat16)
    branch_mlp = jnp.dot(active_low, full[10], preferred_element_type=jnp.float32) + full[
        11
    ].astype(jnp.float32)
    output = ((middle + branch_mlp) * live_rows[:, None]).astype(jnp.bfloat16)
    again = (
        lax.all_gather(norm_one_gain, "dp", axis=0, tiled=True),
        lax.all_gather(norm_one_bias, "dp", axis=0, tiled=True),
        lax.all_gather(joint_weight, "dp", axis=0, tiled=True),
        lax.all_gather(joint_bias, "dp", axis=0, tiled=True),
        lax.all_gather(merge_weight, "dp", axis=0, tiled=True),
        lax.all_gather(merge_bias, "dp", axis=0, tiled=True),
        lax.all_gather(norm_two_gain, "dp", axis=0, tiled=True),
        lax.all_gather(norm_two_bias, "dp", axis=0, tiled=True),
        lax.all_gather(expand_weight, "dp", axis=0, tiled=True),
        lax.all_gather(expand_bias, "dp", axis=0, tiled=True),
        lax.all_gather(shrink_weight, "dp", axis=0, tiled=True),
        lax.all_gather(shrink_bias, "dp", axis=0, tiled=True),
    )
    incoming = cotangent.astype(jnp.float32) * live_rows[:, None]
    incoming_low = incoming.astype(jnp.bfloat16)
    grad_shrink = jnp.einsum(
        "tf,to->fo", active_low, incoming_low, preferred_element_type=jnp.float32
    )
    grad_shrink_offset = jnp.sum(incoming_low.astype(jnp.float32), axis=0)
    grad_active = jnp.einsum(
        "to,fo->tf", incoming_low, again[10], preferred_element_type=jnp.float32
    )
    grad_hidden = (grad_active * gelu_slope(hidden_pre)).astype(jnp.bfloat16)
    grad_expand = jnp.einsum(
        "td,tf->df", second_low, grad_hidden, preferred_element_type=jnp.float32
    )
    grad_expand_offset = jnp.sum(grad_hidden.astype(jnp.float32), axis=0)
    grad_second = jnp.einsum("tf,df->td", grad_hidden, again[8], preferred_element_type=jnp.float32)
    back_two, grad_gain_two, grad_bias_two = norm_backward(
        grad_second, scaled_two, inverse_two, again[6]
    )
    grad_middle = incoming + back_two
    middle_low = grad_middle.astype(jnp.bfloat16)
    grad_merge = jnp.einsum("ti,to->io", attended, middle_low, preferred_element_type=jnp.float32)
    grad_merge_offset = jnp.sum(middle_low.astype(jnp.float32), axis=0)
    grad_attended = jnp.einsum(
        "to,io->ti", middle_low, again[4], preferred_element_type=jnp.float32
    )
    grad_attended = grad_attended.astype(jnp.bfloat16).reshape(row_count, head_count, HD)
    softmax_rows = jnp.exp(block_scores() - log_totals)
    grad_softmax = jnp.einsum(
        "qhd,khd->hqk", grad_attended, value_rows, preferred_element_type=jnp.float32
    )
    row_delta = jnp.sum(softmax_rows * grad_softmax, axis=-1, keepdims=True)
    grad_scores = (softmax_rows * (grad_softmax - row_delta) * score_scale).astype(jnp.bfloat16)
    grad_query_parts = jnp.einsum(
        "hqk,khd->qhd", grad_scores, key_rows, preferred_element_type=jnp.float32
    )
    grad_keys = jnp.einsum("hqk,qhd->khd", grad_scores, queries, preferred_element_type=jnp.float32)
    grad_values = jnp.einsum(
        "hqk,qhd->khd",
        softmax_rows.astype(jnp.bfloat16),
        grad_attended,
        preferred_element_type=jnp.float32,
    )
    grad_joint = jnp.concatenate(
        [
            grad_query_parts.reshape(row_count, model_width),
            grad_keys.reshape(row_count, model_width),
            grad_values.reshape(row_count, model_width),
        ],
        axis=1,
    ).astype(jnp.bfloat16)
    grad_joint_matrix = jnp.einsum(
        "td,tj->dj", first_low, grad_joint, preferred_element_type=jnp.float32
    )
    grad_joint_offset = jnp.sum(grad_joint.astype(jnp.float32), axis=0)
    grad_first = jnp.einsum("tj,dj->td", grad_joint, again[2], preferred_element_type=jnp.float32)
    back_one, grad_gain_one, grad_bias_one = norm_backward(
        grad_first, scaled_one, inverse_one, again[0]
    )
    grad_tokens = grad_middle + back_one
    grads_full = (
        grad_gain_one,
        grad_bias_one,
        grad_joint_matrix,
        grad_joint_offset,
        grad_merge,
        grad_merge_offset,
        grad_gain_two,
        grad_bias_two,
        grad_expand,
        grad_expand_offset,
        grad_shrink,
        grad_shrink_offset,
    )
    shares = (
        lax.psum_scatter(grads_full[0], "dp", scatter_dimension=0, tiled=True),
        lax.psum_scatter(grads_full[1], "dp", scatter_dimension=0, tiled=True),
        lax.psum_scatter(grads_full[2], "dp", scatter_dimension=0, tiled=True),
        lax.psum_scatter(grads_full[3], "dp", scatter_dimension=0, tiled=True),
        lax.psum_scatter(grads_full[4], "dp", scatter_dimension=0, tiled=True),
        lax.psum_scatter(grads_full[5], "dp", scatter_dimension=0, tiled=True),
        lax.psum_scatter(grads_full[6], "dp", scatter_dimension=0, tiled=True),
        lax.psum_scatter(grads_full[7], "dp", scatter_dimension=0, tiled=True),
        lax.psum_scatter(grads_full[8], "dp", scatter_dimension=0, tiled=True),
        lax.psum_scatter(grads_full[9], "dp", scatter_dimension=0, tiled=True),
        lax.psum_scatter(grads_full[10], "dp", scatter_dimension=0, tiled=True),
        lax.psum_scatter(grads_full[11], "dp", scatter_dimension=0, tiled=True),
    )
    totals = (
        lax.psum(shares[0].astype(jnp.bfloat16), "rep").astype(jnp.float32),
        lax.psum(shares[1].astype(jnp.bfloat16), "rep").astype(jnp.float32),
        lax.psum(shares[2].astype(jnp.bfloat16), "rep").astype(jnp.float32),
        lax.psum(shares[3].astype(jnp.bfloat16), "rep").astype(jnp.float32),
        lax.psum(shares[4].astype(jnp.bfloat16), "rep").astype(jnp.float32),
        lax.psum(shares[5].astype(jnp.bfloat16), "rep").astype(jnp.float32),
        lax.psum(shares[6].astype(jnp.bfloat16), "rep").astype(jnp.float32),
        lax.psum(shares[7].astype(jnp.bfloat16), "rep").astype(jnp.float32),
        lax.psum(shares[8].astype(jnp.bfloat16), "rep").astype(jnp.float32),
        lax.psum(shares[9].astype(jnp.bfloat16), "rep").astype(jnp.float32),
        lax.psum(shares[10].astype(jnp.bfloat16), "rep").astype(jnp.float32),
        lax.psum(shares[11].astype(jnp.bfloat16), "rep").astype(jnp.float32),
    )
    return (
        output,
        grad_tokens,
        totals[0],
        totals[1],
        totals[2],
        totals[3],
        totals[4],
        totals[5],
        totals[6],
        totals[7],
        totals[8],
        totals[9],
        totals[10],
        totals[11],
    )


def contract(a, b, dims):
    return lax.dot_general(a, b, dims, preferred_element_type=F32)


def matmul(a, b):
    return jnp.dot(a, b, preferred_element_type=F32)


def span(start, size):
    return pl.ds(start if isinstance(start, int) else pl.multiple_of(start, size), size)


def layer_kernel(dims, names, *args):
    r = dict(zip(names, args, strict=True))
    Z, Y, X = dims
    h0, live, seg, vec, cot = (r[k] for k in ("h0", "live", "seg", "vec", "cot"))
    N1, QKV, OA, H1, N2, G, DU, EB = (r[k] for k in ("N1", "QKV", "OA", "H1", "N2", "G", "DU", "EB"))
    SEG, L, V, XS, XR, OUTB, DA, VG = (
        r[k] for k in ("SEG", "L", "V", "XS", "XR", "OUTB", "DA", "VG")
    )
    R, D = h0.shape
    half_heads = D // HD // 2
    HW = half_heads * HD
    FC = DU.shape[1]
    me = lax.axis_index("dp")
    c = lax.axis_index("rep")
    o = 1 - c
    x = lax.rem(me, X)
    y = lax.rem(me // X, Y)
    z = me // (X * Y)
    OS = XS.at[:, 0:HW]
    own = span(c * R, R)
    sib = span(o * R, R)

    def at(zz, yy, xx):
        return (zz * (Y * X) + yy * X + xx, c)

    def zplus(d):
        return lax.rem(z + d, Z)

    def zminus(d):
        return lax.rem(z + Z - d, Z)

    to_x, to_y, to_o = at(z, y, 1 - x), at(z, 1 - y, x), (me, o)
    to_z = [None] + [at(zplus(d), y, x) for d in range(1, Z)]

    def remote(src, dst, ssem, rsem, to):
        return pltpu.make_async_remote_copy(
            src_ref=src, dst_ref=dst, send_sem=ssem, recv_sem=rsem, device_id=to, device_id_type=MESH
        )

    barrier = pltpu.get_barrier_semaphore()
    for to in to_z[1:] + [to_x, to_y, to_o]:
        pl.semaphore_signal(barrier, inc=1, device_id=to, device_id_type=MESH)
    pl.semaphore_wait(barrier, Z - 1 + 3)

    pair_sems = iter(range(r["ps"].shape[0]))

    def to_pair(src, dst):
        k = next(pair_sems)
        cp = remote(src, dst, r["ps"].at[k], r["pr"].at[k], to_o)
        cp.start()
        return cp

    W = {k: r["W" + k] for k in "jmxs"}
    rows = {k: W[k].shape[3] for k in W}
    wid = {"j": W["j"].shape[4] // 2, "m": HW // 2, "x": W["x"].shape[4] // 2, "s": W["s"].shape[4] // 2}

    def wcols(k, p):
        if k == "m":
            return span(c * HW + p * wid[k], wid[k])
        return pl.ds(p * wid[k], wid[k])

    def piece(k, p, zz, yy, xx):
        return W[k].at[zz, yy, xx, :, wcols(k, p)]

    order = "jmxs"
    num = {(k, p): 2 * i + p for i, k in enumerate(order) for p in (0, 1)}

    def send_piece(k, p, zz, yy, xx, ssem, rsem, to):
        remote(piece(k, p, zz, yy, xx), piece(k, p, zz, yy, xx), ssem, rsem, to).start()

    def vec_send(src, slot, to, sems):
        cp = remote(src, r["VR"].at[slot], sems[0].at[slot], sems[1].at[slot], to)
        cp.start()
        return cp

    vcps = [vec_send(vec, d - 1, to_z[d], (r["vs"], r["vr"])) for d in range(1, Z)]
    segcp = to_pair(seg, SEG.at[c])
    SEG[c] = seg[...]

    lsem = r["ls"]
    local = {k: [] for k in "jmxse"}

    def local_copy(k, src, dst):
        pltpu.make_async_copy(src, dst, lsem.at["jmxse".index(k)]).start()

    for i in range(3):
        local_copy("j", r["wj"].at[:, span(i * D + c * HW, HW)], W["j"].at[z, y, x, :, pl.ds(i * HW, HW)])
    local_copy("m", r["wm"].at[:, span(c * HW, HW)], W["m"].at[z, y, x, :, span(c * HW, HW)])
    blk = rows["s"]
    for i in range(FC // blk):
        local_copy("x", r["wx"].at[:, span(2 * blk * i + blk * c, blk)], W["x"].at[z, y, x, :, pl.ds(i * blk, blk)])
    local_copy("s", r["ws"].at[span(c * blk, blk), :], W["s"].at[z, y, x])
    local_copy("e", cot, EB.at[own, :])

    def local_wait(k, ref):
        pltpu.make_async_copy(ref, ref, lsem.at["jmxse".index(k)]).wait()

    own_ref = {
        "j": W["j"].at[z, y, x],
        "m": W["m"].at[z, y, x, :, span(c * HW, HW)],
        "x": W["x"].at[z, y, x],
        "s": W["s"].at[z, y, x],
    }
    for k in order:
        local_wait(k, own_ref[k])
        for d in range(1, Z):
            for p in (0, 1):
                n = num[k, p]
                send_piece(k, p, z, y, x, r["as1"].at[n], r["ar1"].at[n, d - 1], to_z[d])

    def forward_z(k, d):
        zs = zminus(d)
        for p in (0, 1):
            n = num[k, p]
            if d:
                cp = remote(piece(k, p, zs, y, x), piece(k, p, zs, y, x), r["as1"].at[n], r["ar1"].at[n, d - 1], to_z[d])
                cp.wait_recv()
            a, b = (to_y, to_x) if p == 0 else (to_x, to_y)
            send_piece(k, p, zs, y, x, r["as2"].at[n], r["ar2"].at[n, d], a)
            send_piece(k, p, zs, y, x, r["as3"].at[n], r["ar3"].at[n], b)

    def forward_2(k, d):
        zs = zminus(d)
        for p in (0, 1):
            n = num[k, p]
            yy, xx, a, b = (1 - y, x, to_y, to_x) if p == 0 else (y, 1 - x, to_x, to_y)
            remote(piece(k, p, zs, yy, xx), piece(k, p, zs, yy, xx), r["as2"].at[n], r["ar2"].at[n, d], a).wait_recv()
            send_piece(k, p, zs, yy, xx, r["as3"].at[n], r["ar3"].at[n], b)

    def gather_wait(k):
        for p in (0, 1):
            n = num[k, p]
            ref = W[k].at[:, :, 0, :, wcols(k, p)] if p == 0 else W[k].at[:, 0, :, :, wcols(k, p)]
            remote(ref, ref, r["as3"].at[n], r["ar3"].at[n], to_x if p == 0 else to_y).wait_recv()

    def gather_done(k):
        for p in (0, 1):
            n = num[k, p]
            for ref, s in (
                (W[k].at[pl.ds(0, Z - 1), 0, 0, :, wcols(k, p)], "as1"),
                (W[k].at[:, 0, 0, :, wcols(k, p)], "as2"),
                (W[k].at[:, :, 0, :, wcols(k, p)], "as3"),
            ):
                remote(ref, ref, r[s].at[n], r["ar3"].at[n], to_x).wait_send()

    events = []
    for k in order:
        events += [functools.partial(forward_z, k, d) for d in range(Z)]
        events += [functools.partial(forward_2, k, d) for d in range(Z)]
    events = events[::-1]

    def pump(n):
        for _ in range(n):
            if events:
                events.pop()()

    per = 2 * Z

    pump(1)
    for d in range(1, Z):
        vcps[d - 1].wait()
    acc = vec[...].astype(F32)
    for d in range(1, Z):
        acc = acc + r["VR"][d - 1].astype(F32)
    r["VT"][0] = acc.astype(BF16)
    cp = vec_send(r["VT"].at[0], Z - 1, to_y, (r["vs"], r["vr"]))
    cp.wait()
    acc = acc + r["VR"][Z - 1].astype(F32)
    r["VT"][1] = acc.astype(BF16)
    cp = vec_send(r["VT"].at[1], Z, to_x, (r["vs"], r["vr"]))
    cp.wait()
    V[...] = acc + r["VR"][Z].astype(F32)
    VG[...] = jnp.zeros_like(VG)

    local_wait("e", EB.at[own, :])
    def mask_rows(i, _):
        rr = span(c * R + i * 128, 128)
        EB[rr, :] = (EB[rr, :].astype(F32) * live[span(i * 128, 128), :]).astype(BF16)
        VG[5:6, :] += jnp.sum(EB[rr, :].astype(F32), axis=0, keepdims=True)
        return 0

    lax.fori_loop(0, R // 128, mask_rows, 0)

    def normed(h):
        center = h - jnp.mean(h, axis=-1, keepdims=True)
        inverse = lax.rsqrt(jnp.mean(center * center, axis=-1, keepdims=True) + 1e-06)
        return center * inverse, inverse

    def norm_one(i, _):
        scaled, _i = normed(h0[span(i * 128, 128), :])
        N1[span(c * R + i * 128, 128), :] = (scaled * V[0:1, :] + V[1:2, :]).astype(BF16)
        return 0

    lax.fori_loop(0, R // 128, norm_one, 0)
    n1cp = to_pair(N1.at[own, :], N1.at[own, :])
    ebcp = to_pair(EB.at[own, :], EB.at[own, :])
    segcp.wait()
    pump(per - 1)
    n1cp.wait()
    ebcp.wait()
    pump(2)
    gather_wait("j")

    TQ = 256
    for t in range(3 * HW // TQ):
        w = W["j"][:, :, :, :, t * TQ : (t + 1) * TQ].reshape(D, TQ)
        f = t * TQ
        b = V[6 + f // D : 7 + f // D, f % D : f % D + TQ]
        QKV[:, t * TQ : (t + 1) * TQ] = (matmul(N1[...], w) + b).astype(BF16)
        pump(1)

    lane = lax.broadcasted_iota(jnp.int32, (1, 2 * HD), 1) // HD

    def same_image(g):
        row = SEG[g, 0:1, :]
        col = jnp.transpose(SEG[g])[:, 0:1]
        return col == row

    def attend(g, hp):
        rr = span(g * R, R)
        q = QKV[rr, span(hp * 2 * HD, 2 * HD)]
        k = QKV[rr, span(HW + hp * 2 * HD, 2 * HD)]
        v = QKV[rr, span(2 * HW + hp * 2 * HD, 2 * HD)]
        same = same_image(g)
        res = []
        for i in (0, 1):
            qi = jnp.where(lane == i, q.astype(F32) * HD**-0.5, 0.0).astype(BF16)
            s = jnp.where(same, contract(k, qi, LAST), NEVER)
            top = jnp.max(s, axis=0, keepdims=True)
            e = jnp.exp(s - top)
            tot = jnp.sum(e, axis=0, keepdims=True)
            L[g * half_heads + 2 * hp + i] = top + jnp.log(tot)
            pb = (e * (1.0 / tot)).astype(BF16)
            res.append(contract(v, pb, FIRST)[i * HD : (i + 1) * HD])
        return jnp.transpose(jnp.concatenate(res, axis=0)).astype(BF16)

    for hp in range(half_heads // 2):
        OS[:, 2 * HD * hp : 2 * HD * (hp + 1)] = attend(o, hp)
        pump(1)
    ocp = to_pair(OS, OA.at[:, span(c * HW, HW)])
    for hp in range(half_heads // 2):
        OA[:, span(c * HW + 2 * HD * hp, 2 * HD)] = attend(c, hp)
        pump(1)
    pump(max(0, len(events) - 2 * per + 2))
    gather_wait("m")
    wmcp = to_pair(W["m"].at[:, :, :, :, span(c * HW, HW)], W["m"].at[:, :, :, :, span(c * HW, HW)])
    ocp.wait()
    wmcp.wait()
    pump(1)

    TR = 256
    for t in range(R // TR):
        rr = pl.ds(t * TR, TR)
        h1 = h0[rr, :] + matmul(OA[rr, :], W["m"][...].reshape(D, D)) + V[2:3, :]
        H1[rr, :] = h1
        scaled, _i = normed(h1)
        N2[span(c * R + t * TR, TR), :] = (scaled * V[3:4, :] + V[4:5, :]).astype(BF16)
    n2cp = to_pair(N2.at[own, :], N2.at[own, :])
    pump(max(0, len(events) - per + 1))
    n2cp.wait()
    gather_wait("x")

    for t in range(FC // TQ):
        cc = slice(t * TQ, (t + 1) * TQ)
        b = V[8 + t * TQ // D : 9 + t * TQ // D, t * TQ % D : t * TQ % D + TQ]
        for h in range(2):
            rr = slice(h * R, (h + 1) * R)
            u = matmul(N2[rr, :], W["x"][:, :, :, :, cc].reshape(D, TQ)) + b
            cdf = 0.5 * (1.0 + lax.erf(u * 0.7071067811865476))
            G[rr, cc] = (u * cdf).astype(BF16)
            DU[rr, cc] = (cdf + u * (jnp.exp(-0.5 * u * u) * 0.3989422804014327)).astype(BF16)
        pump(1)

    GS, GM, GX, GJ = r["GS"], r["GM"], W["s"], W["x"]
    grad = {"s": GS, "x": GX, "m": GM, "j": GJ}
    gorder = "sxmj"
    gnum = {(k, p): 2 * i + p for i, k in enumerate(gorder) for p in (0, 1)}
    R1, R2, R3 = ({k: r[n + k] for k in gorder} for n in ("R1", "R2", "R3"))
    outs = {k: r["o" + k] for k in gorder}

    def gslice(k, p):
        if k == "s":
            return slice(None), pl.ds(p * (D // 2), D // 2)
        if k == "x":
            return pl.ds(p * rows["x"], rows["x"]), slice(None)
        if k == "m":
            return slice(None), span(c * HW + p * (HW // 2), HW // 2)
        return slice(None), pl.ds(p * (3 * HW // 2), 3 * HW // 2)

    def add_into(ref, idx, other):
        ref[idx] = (ref[idx].astype(F32) + other[...].astype(F32)).astype(BF16)

    def rs_first(k, p):
        n = gnum[k, p]
        rs, cs = gslice(k, p)
        if p == 0:
            return remote(grad[k].at[:, :, 1 - x, rs, cs], R1[k].at[p], r["rs1"].at[n], r["rr1"].at[n], to_x)
        return remote(grad[k].at[:, 1 - y, :, rs, cs], R1[k].at[p], r["rs1"].at[n], r["rr1"].at[n], to_y)

    def rs_second(k, p):
        n = gnum[k, p]
        rs, cs = gslice(k, p)
        if p == 0:
            return remote(grad[k].at[:, 1 - y, x, rs, cs], R2[k].at[p], r["rs2"].at[n], r["rr2"].at[n], to_y)
        return remote(grad[k].at[:, y, 1 - x, rs, cs], R2[k].at[p], r["rs2"].at[n], r["rr2"].at[n], to_x)

    def rs_third(k, p, d):
        n = gnum[k, p]
        rs, cs = gslice(k, p)
        return remote(grad[k].at[zplus(d), y, x, rs, cs], R3[k].at[p, d - 1], r["rs3"].at[n, d - 1], r["rr3"].at[n, d - 1], to_z[d])

    def add_first(k, p):
        rs_first(k, p).wait_recv()
        rs, cs = gslice(k, p)
        for q in (1, 0):
            def one(i, _):
                if p == 0:
                    yy = y if q == 0 else 1 - y
                    add_into(grad[k], (i, yy, x, rs, cs), R1[k].at[p, i, yy])
                else:
                    xx = x if q == 0 else 1 - x
                    add_into(grad[k], (i, y, xx, rs, cs), R1[k].at[p, i, xx])
                return 0

            lax.fori_loop(0, Z, one, 0)
            if q == 1:
                rs_second(k, p).start()

    def add_second(k, p):
        rs_second(k, p).wait_recv()
        rs, cs = gslice(k, p)

        def one(i, _):
            add_into(grad[k], (i, y, x, rs, cs), R2[k].at[p, i])
            return 0

        lax.fori_loop(0, Z, one, 0)
        for d in range(1, Z):
            rs_third(k, p, d).start()

    def add_third(k, p):
        for d in range(1, Z):
            rs_third(k, p, d).wait_recv()
        rs, cs = gslice(k, p)
        tot = grad[k][z, y, x, rs, cs].astype(F32)
        for d in range(1, Z):
            tot = tot + R3[k][p, d - 1].astype(F32)
        grad[k][z, y, x, rs, cs] = tot.astype(BF16)

    fin_copies = []

    def finish(k):
        i = gorder.index(k)
        cs = {"m": span(c * HW, HW), "j": pl.ds(0, 3 * HW)}.get(k, slice(None))
        total = grad[k].at[z, y, x, :, cs]
        a = pltpu.make_async_copy(total, outs[k].at[c], r["fl"].at[i])
        b = remote(total, outs[k].at[c], r["fs"].at[i], r["fr"].at[i], to_o)
        a.start()
        b.start()
        fin_copies.extend([a, b])

    def first_pair(k):
        for p in (0, 1):
            rs_first(k, p).start()

    def rs_events(k):
        ev = [functools.partial(add_first, k, p) for p in (0, 1)]
        ev += [functools.partial(add_second, k, p) for p in (0, 1)]
        ev += [functools.partial(add_third, k, p) for p in (0, 1)]
        return ev + [functools.partial(finish, k)]

    FT = Y * X * rows["s"] // 2
    nft = FC // FT
    for t in range(nft):
        g = contract(G[:, t * FT : (t + 1) * FT], EB[...], FIRST)
        GS[t // 2, t % 2] = g.astype(BF16).reshape(X, rows["s"], D)
        pump(1)
    pump(len(events))
    gather_wait("s")
    first_pair("s")

    for t in range(nft):
        cc = slice(t * FT, (t + 1) * FT)
        w = W["s"][t // 2, t % 2].reshape(FT, D)
        vr = (8 + t * FT // D, t * FT % D)
        for h in range(2):
            rr = slice(h * R, (h + 1) * R)
            du = (contract(EB[rr, :], w, LAST) * DU[rr, cc].astype(F32)).astype(BF16)
            DU[rr, cc] = du
            VG[vr[0] : vr[0] + 1, vr[1] : vr[1] + FT] += jnp.sum(du.astype(F32), axis=0, keepdims=True)

    nt = D // TQ
    for t in range(nt):
        cc = slice(t * TQ, (t + 1) * TQ)
        XS[:, cc] = matmul(G[sib, :], W["s"][:, :, :, :, cc].reshape(FC, TQ)).astype(BF16)
    h2cp = to_pair(XS, OUTB)
    events.extend(rs_events("s")[::-1])
    h2cp.wait_recv()
    for t in range(nt):
        cc = slice(t * TQ, (t + 1) * TQ)
        own_part = matmul(G[own, :], W["s"][:, :, :, :, cc].reshape(FC, TQ))
        OUTB[:, cc] = ((H1[:, cc] + own_part + OUTB[:, cc].astype(F32) + V[5:6, cc]) * live[...]).astype(BF16)
    outcp = pltpu.make_async_copy(OUTB, r["out"], r["fl"].at[len(gorder)])
    outcp.start()
    h2cp.wait_send()
    gather_done("s")

    def back_part(left, wk, n, rr_):
        for t in range(Z):
            w = wk[t][:, :, :, 0:n].reshape(Y * X * rows["j"], n)
            cw = Y * X * rows["j"]
            XS[:, t * cw : (t + 1) * cw] = contract(left[rr_, 0:n], w, LAST).astype(BF16)

    back_part(DU, W["x"], FC, sib)
    dn2cp = to_pair(XS, XR)

    DT = Y * X * rows["x"]
    for t in range(Z):
        for p in (0, 1):
            g = contract(N2[:, t * DT : (t + 1) * DT], DU[:, p * (FC // 2) : (p + 1) * (FC // 2)], FIRST)
            GX[t, :, :, p * rows["x"] : (p + 1) * rows["x"], :] = g.astype(BF16).reshape(Y, X, rows["x"], FC // 2)
    first_pair("x")
    pump(2)
    dn2cp.wait()

    def norm_back(dy, scaled, inverse, gain, vg):
        ds_ = dy * gain
        VG[vg : vg + 1, :] += jnp.sum(dy * scaled, axis=0, keepdims=True)
        VG[vg + 1 : vg + 2, :] += jnp.sum(dy, axis=0, keepdims=True)
        cen = ds_ - jnp.mean(ds_, axis=-1, keepdims=True)
        cen = cen - scaled * jnp.mean(ds_ * scaled, axis=-1, keepdims=True)
        return cen * inverse

    for t in range(R // TR):
        rr = pl.ds(t * TR, TR)
        dy = contract(DU[span(c * R + t * TR, TR), :], W["x"][...].reshape(D, FC), LAST) + XR[rr, :].astype(F32)
        scaled, inverse = normed(H1[rr, :])
        dh = EB[span(c * R + t * TR, TR), :].astype(F32) + norm_back(dy, scaled, inverse, V[3:4, :], 3)
        H1[rr, :] = dh
        DA[rr, :] = dh.astype(BF16)
        VG[2:3, :] += jnp.sum(DA[rr, :].astype(F32), axis=0, keepdims=True)
    gather_done("x")
    pump(1)

    for t in range(2):
        base = o if t == 0 else c
        for u in range(HW // (X * rows["m"])):
            cw = X * rows["m"]
            zz, yy = (base * (Z // 2) + u // Y), u % Y
            w = W["m"][zz, yy].reshape(cw, D)
            res = contract(DA[...], w, LAST).astype(BF16)
            if t == 0:
                OS[:, u * cw : (u + 1) * cw] = res
            else:
                G[own, 3 * HW + u * cw : 3 * HW + (u + 1) * cw] = res
        if t == 0:
            docp = to_pair(OS, G.at[own, pl.ds(3 * HW, HW)])
    gather_done("m")
    pump(1)

    for t in range(Z):
        g = contract(OA[:, t * DT : (t + 1) * DT], DA[...], FIRST)
        GM[t] = g.astype(BF16).reshape(Y, X, rows["m"], D)
    gmcp = to_pair(GM.at[:, :, :, :, span(o * HW, HW)], r["GMR"])

    def attend_back(g, hp):
        rr = span(g * R, R)
        qc, kc, vc = (pl.ds(i * HW + hp * 2 * HD, 2 * HD) for i in range(3))
        q, k, v = QKV[rr, qc], QKV[rr, kc], QKV[rr, vc]
        do = G[rr, 3 * HW + hp * 2 * HD : 3 * HW + (hp + 1) * 2 * HD]
        same = same_image(g)
        dq, dk, dv = [], [], []
        for i in (0, 1):
            qi = jnp.where(lane == i, q.astype(F32) * HD**-0.5, 0.0).astype(BF16)
            di = jnp.where(lane == i, do.astype(F32), 0.0).astype(BF16)
            s = jnp.where(same, contract(k, qi, LAST), NEVER)
            pr = jnp.exp(s - L[g * half_heads + 2 * hp + i])
            dp = contract(v, di, LAST)
            delta = jnp.sum(pr * dp, axis=0, keepdims=True)
            dsb = (pr * (dp - delta) * HD**-0.5).astype(BF16)
            dq.append(contract(k, dsb, FIRST)[i * HD : (i + 1) * HD])
            dk.append(matmul(dsb, q))
            dv.append(matmul(pr.astype(BF16), do))
        G[rr, qc] = jnp.transpose(jnp.concatenate(dq, axis=0)).astype(BF16)
        G[rr, kc] = jnp.where(lane == 0, dk[0], dk[1]).astype(BF16)
        G[rr, vc] = jnp.where(lane == 0, dv[0], dv[1]).astype(BF16)

    for hp in range(half_heads // 2):
        attend_back(c, hp)
        if hp == 0:
            gmcp.wait()

            def add_pair(i, _):
                for j in range(Y * X):
                    add_into(GM, (i, j // X, j % X, slice(None), span(c * HW, HW)), r["GMR"].at[i, j // X, j % X])
                return 0

            lax.fori_loop(0, Z, add_pair, 0)
            first_pair("m")
            events[:0] = (rs_events("x") + rs_events("m"))[::-1]
        pump(1)
    docp.wait()
    for hp in range(half_heads // 2):
        attend_back(o, hp)
        pump(1)

    for t in range(Z):
        g = contract(N1[:, t * DT : (t + 1) * DT], G[:, 0 : 3 * HW], FIRST)
        GJ[t, :, :, :, 0 : 3 * HW] = g.astype(BF16).reshape(Y, X, rows["j"], 3 * HW)
    first_pair("j")
    events[:0] = rs_events("j")[::-1]
    gather_done("j")
    for t in range(3):
        VG[6 + t * HW // D : 7 + t * HW // D, t * HW % D : t * HW % D + HW] += jnp.sum(
            G[:, t * HW : (t + 1) * HW].astype(F32), axis=0, keepdims=True
        )

    back_part(G, W["j"], 3 * HW, sib)
    dn1cp = to_pair(XS, XR)
    pump(2)
    dn1cp.wait()
    for t in range(R // TR):
        rr = pl.ds(t * TR, TR)
        dy = contract(G[span(c * R + t * TR, TR), 0 : 3 * HW], W["j"][...].reshape(D, 3 * HW), LAST) + XR[rr, :].astype(F32)
        scaled, inverse = normed(h0[rr, :])
        H1[rr, :] = H1[rr, :] + norm_back(dy, scaled, inverse, V[0:1, :], 0)
    gtcp = pltpu.make_async_copy(H1, r["gt"], r["fl"].at[len(gorder) + 1])
    gtcp.start()

    VGR = r["VGR"]
    for slot, to in ((0, to_x), (1, to_y)):
        cp = remote(VG, VGR.at[slot], r["gs"].at[slot], r["gr"].at[slot], to)
        cp.start()
        cp.wait()
        VG[...] = VG[...] + VGR[slot]
        pump(1)
    cps = []
    for d in range(1, Z):
        cp = remote(VG, VGR.at[1 + d], r["gs"].at[1 + d], r["gr"].at[1 + d], to_z[d])
        cp.start()
        cps.append(cp)
    for cp in cps:
        cp.wait()
    acc = VG[...]
    for d in range(1, Z):
        acc = acc + VGR[1 + d]
    ov = r["ov"]
    ov[c] = acc
    cp = to_pair(ov.at[c], ov.at[c])

    pump(len(events))
    cp.wait()
    for k in gorder:
        for p in (0, 1):
            rs_first(k, p).wait_send()
            rs_second(k, p).wait_send()
            for d in range(1, Z):
                rs_third(k, p, d).wait_send()
    for f in fin_copies:
        f.wait()
    outcp.wait()
    gtcp.wait()


def spread_vector(piece, me, count):
    n = piece.shape[0]
    place = jnp.arange(n * count, dtype=jnp.int32) // n
    return jnp.where(place == me, jnp.tile(piece, count), 0).astype(BF16)


def fused_layer(dims, *args):
    (
        tokens,
        kept_patch,
        image_lengths,
        ground_distance,
        cotangent,
        norm_one_gain,
        norm_one_bias,
        joint_weight,
        joint_bias,
        merge_weight,
        merge_bias,
        norm_two_gain,
        norm_two_bias,
        expand_weight,
        expand_bias,
        shrink_weight,
        shrink_bias,
    ) = args
    Z, Y, X = dims
    N = Z * Y * X
    R, D = tokens.shape
    FF = expand_weight.shape[1]
    HW, FC, blk = D // 2, FF // 2, shrink_weight.shape[0] // 2
    rj = joint_weight.shape[0]
    me, c = lax.axis_index("dp"), lax.axis_index("rep")
    segment, live = packing(image_lengths[0], R)
    ground_rows = row_distance(segment, ground_distance[0])
    h0 = tokens.astype(F32) + positions(kept_patch, ground_rows, D)
    seg = jnp.broadcast_to(segment.astype(F32)[None, :], (8, R))
    jb = spread_vector(joint_bias, me, N).reshape(3, 2, HW)
    jb = jnp.where(c == 0, jb[:, 0], jb[:, 1]).reshape(-1)
    xb = spread_vector(expand_bias, me, N).reshape(FF // (2 * blk), 2, blk)
    xb = jnp.where(c == 0, xb[:, 0], xb[:, 1]).reshape(-1)
    flat = [
        spread_vector(v, me, N)
        for v in (norm_one_gain, norm_one_bias, merge_bias, norm_two_gain, norm_two_bias, shrink_bias)
    ]
    flat += [jb, jnp.zeros((2 * D - 3 * HW,), BF16), xb]
    vec = jnp.concatenate(flat).reshape(-1, D)
    vec = jnp.pad(vec, ((0, 16 - vec.shape[0]), (0, 0)))

    vm, hbm = pl.BlockSpec(memory_space=pltpu.VMEM), pl.BlockSpec(memory_space=pl.ANY)
    ins = [("h0", h0, vm), ("live", live[:, None], vm), ("seg", seg, vm), ("vec", vec, vm), ("cot", cotangent, hbm)]
    ins += [("wj", joint_weight, hbm), ("wm", merge_weight, hbm), ("wx", expand_weight, hbm), ("ws", shrink_weight, hbm)]
    S = jax.ShapeDtypeStruct
    outs = [
        ("out", S((R, D), BF16), hbm),
        ("gt", S((R, D), F32), hbm),
        ("oj", S((2, rj, 3 * HW), BF16), hbm),
        ("om", S((2, rj, HW), BF16), hbm),
        ("ox", S((2, 2 * rj, FC // 2), BF16), hbm),
        ("os", S((2, blk, D), BF16), hbm),
        ("ov", S((2, 16, D), F32), vm),
    ]
    V = pltpu.VMEM
    dma = pltpu.SemaphoreType.DMA
    cut = {"j": (rj, 3 * HW // 2), "m": (rj, HW // 2), "x": (rj, FC // 2), "s": (blk, D // 2)}
    scratch = [
        ("Wj", V((Z, Y, X, rj, 3 * HW), BF16)),
        ("Wm", V((Z, Y, X, rj, D), BF16)),
        ("Wx", V((Z, Y, X, rj, FC), BF16)),
        ("Ws", V((Z, Y, X, blk, D), BF16)),
        ("GS", V((Z, Y, X, blk, D), BF16)),
        ("GM", V((Z, Y, X, rj, D), BF16)),
        ("GMR", V((Z, Y, X, rj, HW), BF16)),
        ("N1", V((2 * R, D), BF16)),
        ("QKV", V((2 * R, 3 * HW), BF16)),
        ("OA", V((R, D), BF16)),
        ("H1", V((R, D), F32)),
        ("N2", V((2 * R, D), BF16)),
        ("G", V((2 * R, FC), BF16)),
        ("DU", V((2 * R, FC), BF16)),
        ("EB", V((2 * R, D), BF16)),
        ("SEG", V((2, 8, R), F32)),
        ("L", V((D // HD, 1, R), F32)),
        ("V", V((16, D), F32)),
        ("VR", V((Z + 1, 16, D), BF16)),
        ("VT", V((2, 16, D), BF16)),
        ("VG", V((16, D), F32)),
        ("VGR", V((Z + 1, 16, D), F32)),
        ("XS", V((R, D), BF16)),
        ("XR", V((R, D), BF16)),
        ("OUTB", V((R, D), BF16)),
        ("DA", V((R, D), BF16)),
    ]
    for k, (a, b) in cut.items():
        scratch += [("R1" + k, V((2, Z, 2, a, b), BF16)), ("R2" + k, V((2, Z, a, b), BF16))]
        scratch += [("R3" + k, V((2, Z - 1, a, b), BF16))]
    scratch += [
        ("ps", dma((12,))),
        ("pr", dma((12,))),
        ("vs", dma((Z + 1,))),
        ("vr", dma((Z + 1,))),
        ("gs", dma((Z + 1,))),
        ("gr", dma((Z + 1,))),
        ("ls", dma((5,))),
        ("as1", dma((8,))),
        ("ar1", dma((8, Z - 1))),
        ("as2", dma((8,))),
        ("ar2", dma((8, Z))),
        ("as3", dma((8,))),
        ("ar3", dma((8,))),
        ("rs1", dma((8,))),
        ("rr1", dma((8,))),
        ("rs2", dma((8,))),
        ("rr2", dma((8,))),
        ("rs3", dma((8, Z - 1))),
        ("rr3", dma((8, Z - 1))),
        ("fl", dma((6,))),
        ("fs", dma((4,))),
        ("fr", dma((4,))),
    ]
    names = [n for n, *_ in ins + outs + scratch]
    res = pl.pallas_call(
        functools.partial(layer_kernel, dims, names),
        out_shape=[s for _, s, _ in outs],
        in_specs=[s for _, _, s in ins],
        out_specs=[s for _, _, s in outs],
        scratch_shapes=[s for _, s in scratch],
        compiler_params=pltpu.CompilerParams(
            collective_id=0, has_side_effects=True, vmem_limit_bytes=VMEM_BYTES
        ),
    )(*[a for _, a, _ in ins])
    out, gt, oj, om, ox, os_, ov = res
    g_joint = oj.reshape(2, rj, 3, HW).transpose(1, 2, 0, 3).reshape(rj, 3 * D).astype(F32)
    g_merge = om.transpose(1, 0, 2).reshape(rj, D).astype(F32)
    g_expand = (
        ox.reshape(2, 2, rj, FC // (2 * blk), blk).transpose(2, 1, 3, 0, 4).reshape(rj, FF).astype(F32)
    )
    g_shrink = os_.reshape(2 * blk, D).astype(F32)
    both = ov[0, 0:6] + ov[1, 0:6]

    def mine(v):
        return lax.dynamic_slice_in_dim(v, me * (v.shape[0] // N), v.shape[0] // N)

    g_jb = mine(ov[:, 6:8].reshape(2, 2 * D)[:, : 3 * HW].reshape(2, 3, HW).transpose(1, 0, 2).reshape(-1))
    g_xb = mine(ov[:, 8:10].reshape(2, FC // blk, blk).transpose(1, 0, 2).reshape(-1))
    g1, b1, mb, g2, b2, sb = (mine(both[i]) for i in range(6))
    return out, gt, g1, b1, g_joint, g_jb, g_merge, mb, g2, b2, g_expand, g_xb, g_shrink, sb


def layout(mesh, joint_rows, shrink_rows):
    n = mesh.shape["dp"]
    if mesh.shape["rep"] != 2 or n % 8 or joint_rows % 16 or shrink_rows % 256:
        return None
    return (n // 4, 2, 2)


def on_device(mesh, *args):
    dims = layout(mesh, args[7].shape[0], args[15].shape[0])
    if dims is None:
        return general_layer(*args)
    return fused_layer(dims, *args)


def solution(mesh):
    rows, rows2 = P(("dp", "rep")), P(("dp", "rep"), None)
    vector, matrix = P("dp"), P("dp", None)
    return jax.shard_map(
        functools.partial(on_device, mesh),
        mesh=mesh,
        in_specs=(
            rows2,
            rows,
            rows2,
            rows2,
            rows2,
            vector,
            vector,
            matrix,
            vector,
            matrix,
            vector,
            vector,
            vector,
            matrix,
            vector,
            matrix,
            vector,
        ),
        out_specs=(
            rows2,
            rows2,
            vector,
            vector,
            matrix,
            vector,
            matrix,
            vector,
            vector,
            vector,
            matrix,
            vector,
            matrix,
            vector,
        ),
        check_vma=False,
    )
```

```python
import functools

import jax
import jax.numpy as jnp
from jax import lax
from jax.experimental import pallas as pl
from jax.experimental.pallas import tpu as pltpu
from jax.sharding import PartitionSpec as P

HD = 64
MESH = pl.DeviceIdType.MESH
F32 = jnp.float32
BF16 = jnp.bfloat16
NEVER = -1000000000.0
VMEM_BYTES = 127 * 2**19
SIDE = {"s": 0, "t": 0, "x": 1, "u": 0, "j": 0, "k": 0}
SCHEDULE = [
    "p0j30", "p0x20", "z0j10", "fzx10", "z0m10", "p0x30", "z0m00", "p0j20", "fzm10", "p1x20", "_rows", "_v1", "_h0",
    "fzj11", "fzs00", "z0j00", "fzm01", "p1j20", "p1j30", "z0x00", "fzj12", "fzm02", "p0s20", "fzj00", "fzm11",
    "fzj13", "_v2", "fzj01", "p2j30", "fzj02", "p2x20", "p1x30", "pzj31", "p0s30", "fzm03", "f2m11", "fzj10",
    "p2j20", "f2j11", "z0x10", "f2j12", "_v3", "_ln1", "p1s20", "fzm12", "pzj21", "p1s30", "f2j01", "pzx21", "fzm00",
    "pzj32", "f2j02", "f2j00", "fzj03", "fzm13", "f2j13", "p2x30", "f2j03", "f2j10", "fzx01", "fzx11", "f2m01",
    "f2m12", "pzj22", "pzx31", "fzx00", "pzj33", "fzx12", "f2m03", "pzj23", "z0s10", "p2s20", "fzx02", "_qkv0",
    "_qkv1", "p2s30", "_qkv2", "_qkv3", "_qkv4", "f2m00", "pzx22", "f2m13", "pzx32", "z0s00", "_qkv5", "f2m02",
    "_at0", "f2x01", "f2m10", "_at1", "_at2", "f2x10", "pzs21", "fzx13", "fzx03", "_at3", "_at4", "_at5", "f2x11",
    "_at6", "f2x00", "_at7", "_wm", "pzx23", "f2x12", "f2x02", "pzx33", "f2x03", "f2x13", "pzs31", "fzs01", "fzs11",
    "_mrg", "fzs02", "_ge0", "_ge1", "_ge2", "_ge3", "_ge4", "_ge5", "fzs10", "fzs12", "pzs32", "_ge6", "_ge7",
    "_gs0", "fzs03", "pzs22", "_gs1", "_gs2", "fzs13", "f2s00", "_gs3", "f2s11", "f2s03", "f2s01", "f2s02", "f2s10",
    "pzs33", "pzs23", "f2s12", "f2s13", "S1s00", "S1t10", "_du0", "S1t00", "_du1", "_du2", "_du3", "S1s10", "_h2s",
    "_dn2s", "_h2o", "_gx0", "A1s00", "S1x10", "S1x00", "_gx1", "A1t10", "S1u00", "S1x20", "S1x30", "A1t00", "_dn2o",
    "_dO", "A1s10", "_gm", "_ab0", "A1x00", "A2s00", "_gma", "_ab1", "A2t10", "A1x10", "_ab2", "_ab3", "_gj0",
    "S1m00", "S1j10", "A2t00", "_ab4", "S1j00", "A2x00", "_ab5", "A1u00", "A2s10", "_ab6", "S1u10", "A2x10", "_ab7",
    "_gj1", "_dn1s", "A1x20", "S1k10", "A2u00", "A3s00", "A1j10", "_dn1o", "_vz", "A1u10", "A2j10", "A1j00", "A3x00",
    "S1k00", "A1m00", "A3x10", "A3s10", "S1m10", "A2u10", "A3u00", "A1k10", "A3t00", "A2j00", "A3u10", "A2m00",
    "A2x20", "_vx", "A1x30", "A1k00", "A2k10", "A3x20", "F_s00", "A3j00", "F_u00", "A1m10", "A3t10", "A2k00",
    "A3j10", "_vy", "A3m00", "A2x30", "F_j00", "A2m10", "A3x30", "A3k00", "F_t00", "F_x00", "_vp", "A3k10", "F_k00",
    "A3m10", "F_m00", "_end",
]

LAST = (((1,), (1,)), ((), ()))
FIRST = (((0,), (0,)), ((), ()))

def packing(lengths, row_count):
    image_ends = jnp.cumsum(lengths)
    row_ids = jnp.arange(row_count, dtype=jnp.int32)
    segment = jnp.sum((image_ends[None, :] <= row_ids[:, None]).astype(jnp.int32), axis=1)
    live_rows = (row_ids < image_ends[-1]).astype(jnp.float32)
    return (segment, live_rows)


def row_distance(segment, distances):
    slots = jnp.arange(distances.shape[-1], dtype=jnp.int32)
    onehot = (segment[:, None] == slots[None, :]).astype(jnp.float32)
    return jnp.sum(onehot * distances[None, :].astype(jnp.float32), axis=1)


def positions(patch_index, ground_rows, model_width):
    quarter = model_width // 4
    frequency = 1.0 / 10000.0 ** (jnp.arange(quarter, dtype=jnp.float32) / quarter)
    factor = ground_rows / 10.0
    across_rows = ((patch_index // 14).astype(jnp.float32) * factor)[..., None] * frequency
    along_rows = ((patch_index % 14).astype(jnp.float32) * factor)[..., None] * frequency
    return jnp.concatenate(
        [jnp.sin(across_rows), jnp.cos(across_rows), jnp.sin(along_rows), jnp.cos(along_rows)],
        axis=-1,
    )


def norm_forward(hidden, scaling, offset):
    center = hidden - jnp.mean(hidden, axis=-1, keepdims=True)
    inverse = lax.rsqrt(jnp.mean(center * center, axis=-1, keepdims=True) + 1e-06)
    scaled = center * inverse
    return (scaled * scaling.astype(jnp.float32) + offset.astype(jnp.float32), scaled, inverse)


def norm_backward(incoming, scaled, inverse, scaling):
    grad_scaled = incoming * scaling.astype(jnp.float32)
    centered_grad = grad_scaled - jnp.mean(grad_scaled, axis=-1, keepdims=True)
    centered_grad = centered_grad - scaled * jnp.mean(grad_scaled * scaled, axis=-1, keepdims=True)
    return (centered_grad * inverse, jnp.sum(incoming * scaled, axis=0), jnp.sum(incoming, axis=0))


def gelu_slope(hidden_pre):
    normal_cdf = 0.5 * (1.0 + jax.scipy.special.erf(hidden_pre * 0.7071067811865476))
    density = jnp.exp(-0.5 * hidden_pre * hidden_pre) * 0.3989422804014327
    return normal_cdf + hidden_pre * density


def general_layer(
    tokens,
    kept_patch,
    image_lengths,
    ground_distance,
    cotangent,
    norm_one_gain,
    norm_one_bias,
    joint_weight,
    joint_bias,
    merge_weight,
    merge_bias,
    norm_two_gain,
    norm_two_bias,
    expand_weight,
    expand_bias,
    shrink_weight,
    shrink_bias,
):
    full = (
        lax.all_gather(norm_one_gain, "dp", axis=0, tiled=True),
        lax.all_gather(norm_one_bias, "dp", axis=0, tiled=True),
        lax.all_gather(joint_weight, "dp", axis=0, tiled=True),
        lax.all_gather(joint_bias, "dp", axis=0, tiled=True),
        lax.all_gather(merge_weight, "dp", axis=0, tiled=True),
        lax.all_gather(merge_bias, "dp", axis=0, tiled=True),
        lax.all_gather(norm_two_gain, "dp", axis=0, tiled=True),
        lax.all_gather(norm_two_bias, "dp", axis=0, tiled=True),
        lax.all_gather(expand_weight, "dp", axis=0, tiled=True),
        lax.all_gather(expand_bias, "dp", axis=0, tiled=True),
        lax.all_gather(shrink_weight, "dp", axis=0, tiled=True),
        lax.all_gather(shrink_bias, "dp", axis=0, tiled=True),
    )
    row_count = tokens.shape[0]
    model_width = tokens.shape[1]
    head_count = model_width // HD
    segment, live_rows = packing(image_lengths[0], row_count)
    ground_rows = row_distance(segment, ground_distance[0])
    residual_in = tokens.astype(jnp.float32) + positions(kept_patch, ground_rows, model_width)
    first, scaled_one, inverse_one = norm_forward(residual_in, full[0], full[1])
    first_low = first.astype(jnp.bfloat16)
    projected = (
        jnp.dot(first_low, full[2], preferred_element_type=jnp.float32)
        + full[3].astype(jnp.float32)
    ).astype(jnp.bfloat16)
    queries = projected[:, :model_width].reshape(row_count, head_count, HD)
    key_rows = projected[:, model_width : 2 * model_width].reshape(row_count, head_count, HD)
    value_rows = projected[:, 2 * model_width :].reshape(row_count, head_count, HD)
    score_scale = HD ** (-0.5)

    def block_scores():
        raw_scores = (
            jnp.einsum("qhd,khd->hqk", queries, key_rows, preferred_element_type=jnp.float32)
            * score_scale
        )
        same_image = segment[:, None] == segment[None, :]
        return jnp.where(same_image[None], raw_scores, -1000000000.0)

    scores = block_scores()
    highest_score = jnp.max(scores, axis=-1, keepdims=True)
    exponent = jnp.exp(scores - highest_score)
    row_total = jnp.sum(exponent, axis=-1, keepdims=True)
    softmax_rows = exponent / row_total
    log_totals = highest_score + jnp.log(row_total)
    attended_parts = jnp.einsum(
        "hqk,khd->qhd",
        softmax_rows.astype(jnp.bfloat16),
        value_rows,
        preferred_element_type=jnp.float32,
    )
    attended = attended_parts.reshape(row_count, model_width).astype(jnp.bfloat16)
    branch = jnp.dot(attended, full[4], preferred_element_type=jnp.float32) + full[5].astype(
        jnp.float32
    )
    middle = residual_in + branch
    second, scaled_two, inverse_two = norm_forward(middle, full[6], full[7])
    second_low = second.astype(jnp.bfloat16)
    hidden_pre = jnp.dot(second_low, full[8], preferred_element_type=jnp.float32) + full[9].astype(
        jnp.float32
    )
    active_low = jax.nn.gelu(hidden_pre, approximate=False).astype(jnp.bfloat16)
    branch_mlp = jnp.dot(active_low, full[10], preferred_element_type=jnp.float32) + full[
        11
    ].astype(jnp.float32)
    output = ((middle + branch_mlp) * live_rows[:, None]).astype(jnp.bfloat16)
    again = (
        lax.all_gather(norm_one_gain, "dp", axis=0, tiled=True),
        lax.all_gather(norm_one_bias, "dp", axis=0, tiled=True),
        lax.all_gather(joint_weight, "dp", axis=0, tiled=True),
        lax.all_gather(joint_bias, "dp", axis=0, tiled=True),
        lax.all_gather(merge_weight, "dp", axis=0, tiled=True),
        lax.all_gather(merge_bias, "dp", axis=0, tiled=True),
        lax.all_gather(norm_two_gain, "dp", axis=0, tiled=True),
        lax.all_gather(norm_two_bias, "dp", axis=0, tiled=True),
        lax.all_gather(expand_weight, "dp", axis=0, tiled=True),
        lax.all_gather(expand_bias, "dp", axis=0, tiled=True),
        lax.all_gather(shrink_weight, "dp", axis=0, tiled=True),
        lax.all_gather(shrink_bias, "dp", axis=0, tiled=True),
    )
    incoming = cotangent.astype(jnp.float32) * live_rows[:, None]
    incoming_low = incoming.astype(jnp.bfloat16)
    grad_shrink = jnp.einsum(
        "tf,to->fo", active_low, incoming_low, preferred_element_type=jnp.float32
    )
    grad_shrink_offset = jnp.sum(incoming_low.astype(jnp.float32), axis=0)
    grad_active = jnp.einsum(
        "to,fo->tf", incoming_low, again[10], preferred_element_type=jnp.float32
    )
    grad_hidden = (grad_active * gelu_slope(hidden_pre)).astype(jnp.bfloat16)
    grad_expand = jnp.einsum(
        "td,tf->df", second_low, grad_hidden, preferred_element_type=jnp.float32
    )
    grad_expand_offset = jnp.sum(grad_hidden.astype(jnp.float32), axis=0)
    grad_second = jnp.einsum("tf,df->td", grad_hidden, again[8], preferred_element_type=jnp.float32)
    back_two, grad_gain_two, grad_bias_two = norm_backward(
        grad_second, scaled_two, inverse_two, again[6]
    )
    grad_middle = incoming + back_two
    middle_low = grad_middle.astype(jnp.bfloat16)
    grad_merge = jnp.einsum("ti,to->io", attended, middle_low, preferred_element_type=jnp.float32)
    grad_merge_offset = jnp.sum(middle_low.astype(jnp.float32), axis=0)
    grad_attended = jnp.einsum(
        "to,io->ti", middle_low, again[4], preferred_element_type=jnp.float32
    )
    grad_attended = grad_attended.astype(jnp.bfloat16).reshape(row_count, head_count, HD)
    softmax_rows = jnp.exp(block_scores() - log_totals)
    grad_softmax = jnp.einsum(
        "qhd,khd->hqk", grad_attended, value_rows, preferred_element_type=jnp.float32
    )
    row_delta = jnp.sum(softmax_rows * grad_softmax, axis=-1, keepdims=True)
    grad_scores = (softmax_rows * (grad_softmax - row_delta) * score_scale).astype(jnp.bfloat16)
    grad_query_parts = jnp.einsum(
        "hqk,khd->qhd", grad_scores, key_rows, preferred_element_type=jnp.float32
    )
    grad_keys = jnp.einsum("hqk,qhd->khd", grad_scores, queries, preferred_element_type=jnp.float32)
    grad_values = jnp.einsum(
        "hqk,qhd->khd",
        softmax_rows.astype(jnp.bfloat16),
        grad_attended,
        preferred_element_type=jnp.float32,
    )
    grad_joint = jnp.concatenate(
        [
            grad_query_parts.reshape(row_count, model_width),
            grad_keys.reshape(row_count, model_width),
            grad_values.reshape(row_count, model_width),
        ],
        axis=1,
    ).astype(jnp.bfloat16)
    grad_joint_matrix = jnp.einsum(
        "td,tj->dj", first_low, grad_joint, preferred_element_type=jnp.float32
    )
    grad_joint_offset = jnp.sum(grad_joint.astype(jnp.float32), axis=0)
    grad_first = jnp.einsum("tj,dj->td", grad_joint, again[2], preferred_element_type=jnp.float32)
    back_one, grad_gain_one, grad_bias_one = norm_backward(
        grad_first, scaled_one, inverse_one, again[0]
    )
    grad_tokens = grad_middle + back_one
    grads_full = (
        grad_gain_one,
        grad_bias_one,
        grad_joint_matrix,
        grad_joint_offset,
        grad_merge,
        grad_merge_offset,
        grad_gain_two,
        grad_bias_two,
        grad_expand,
        grad_expand_offset,
        grad_shrink,
        grad_shrink_offset,
    )
    shares = (
        lax.psum_scatter(grads_full[0], "dp", scatter_dimension=0, tiled=True),
        lax.psum_scatter(grads_full[1], "dp", scatter_dimension=0, tiled=True),
        lax.psum_scatter(grads_full[2], "dp", scatter_dimension=0, tiled=True),
        lax.psum_scatter(grads_full[3], "dp", scatter_dimension=0, tiled=True),
        lax.psum_scatter(grads_full[4], "dp", scatter_dimension=0, tiled=True),
        lax.psum_scatter(grads_full[5], "dp", scatter_dimension=0, tiled=True),
        lax.psum_scatter(grads_full[6], "dp", scatter_dimension=0, tiled=True),
        lax.psum_scatter(grads_full[7], "dp", scatter_dimension=0, tiled=True),
        lax.psum_scatter(grads_full[8], "dp", scatter_dimension=0, tiled=True),
        lax.psum_scatter(grads_full[9], "dp", scatter_dimension=0, tiled=True),
        lax.psum_scatter(grads_full[10], "dp", scatter_dimension=0, tiled=True),
        lax.psum_scatter(grads_full[11], "dp", scatter_dimension=0, tiled=True),
    )
    totals = (
        lax.psum(shares[0].astype(jnp.bfloat16), "rep").astype(jnp.float32),
        lax.psum(shares[1].astype(jnp.bfloat16), "rep").astype(jnp.float32),
        lax.psum(shares[2].astype(jnp.bfloat16), "rep").astype(jnp.float32),
        lax.psum(shares[3].astype(jnp.bfloat16), "rep").astype(jnp.float32),
        lax.psum(shares[4].astype(jnp.bfloat16), "rep").astype(jnp.float32),
        lax.psum(shares[5].astype(jnp.bfloat16), "rep").astype(jnp.float32),
        lax.psum(shares[6].astype(jnp.bfloat16), "rep").astype(jnp.float32),
        lax.psum(shares[7].astype(jnp.bfloat16), "rep").astype(jnp.float32),
        lax.psum(shares[8].astype(jnp.bfloat16), "rep").astype(jnp.float32),
        lax.psum(shares[9].astype(jnp.bfloat16), "rep").astype(jnp.float32),
        lax.psum(shares[10].astype(jnp.bfloat16), "rep").astype(jnp.float32),
        lax.psum(shares[11].astype(jnp.bfloat16), "rep").astype(jnp.float32),
    )
    return (
        output,
        grad_tokens,
        totals[0],
        totals[1],
        totals[2],
        totals[3],
        totals[4],
        totals[5],
        totals[6],
        totals[7],
        totals[8],
        totals[9],
        totals[10],
        totals[11],
    )


def contract(a, b, dims):
    return lax.dot_general(a, b, dims, preferred_element_type=F32)


def matmul(a, b):
    return jnp.dot(a, b, preferred_element_type=F32)


def span(start, size):
    return pl.ds(start if isinstance(start, int) else pl.multiple_of(start, size), size)


def layer_kernel(dims, cuts, schedule, names, *args):
    r = dict(zip(names, args, strict=True))
    Z, Y, X = dims
    vec, cot = r["vec"], r["cot"]
    H0, N1, QKV, OA, H1, N2, G, DU, EB = (r[k] for k in ("H0", "N1", "QKV", "OA", "H1", "N2", "G", "DU", "EB"))
    SEG, L, V, XS, XR, OUTB, DA, VG, COL = (r[k] for k in ("SEG", "L", "V", "XS", "XR", "OUTB", "DA", "VG", "COL"))
    VR, VT, VGR, GM = (r[k] for k in ("VR", "VT", "VGR", "GM"))
    OS = XS.at[:, 0 : XS.shape[1] // 2]
    R, D = H0.shape
    half_heads = D // HD // 2
    HW = half_heads * HD
    FC = DU.shape[1]
    me = lax.axis_index("dp")
    c = lax.axis_index("rep")
    o = 1 - c
    x = lax.rem(me, X)
    y = lax.rem(me // X, Y)
    z = me // (X * Y)
    own = span(c * R, R)
    sib = span(o * R, R)

    def at(zz, yy, xx):
        return (zz * (Y * X) + yy * X + xx, c)

    def zplus(d):
        return lax.rem(z + d, Z)

    to_x, to_y, to_o = at(z, y, 1 - x), at(z, 1 - y, x), (me, o)
    to_z = [None] + [at(zplus(d), y, x) for d in range(1, Z)]
    up, down = to_z[1], to_z[Z - 1]

    def remote(src, dst, ssem, rsem, to):
        return pltpu.make_async_remote_copy(
            src_ref=src, dst_ref=dst, send_sem=ssem, recv_sem=rsem, device_id=to, device_id_type=MESH
        )

    barrier = pltpu.get_barrier_semaphore()
    for to in to_z[1:] + [to_x, to_y, to_o]:
        pl.semaphore_signal(barrier, inc=1, device_id=to, device_id_type=MESH)
    pl.semaphore_wait(barrier, Z - 1 + 3)

    pair_sems = iter(range(r["ps"].shape[0]))

    def to_pair(src, dst):
        k = next(pair_sems)
        cp = remote(src, dst, r["ps"].at[k], r["pr"].at[k], to_o)
        cp.start()
        return cp

    def vec_send(src, slot, to):
        cp = remote(src, VR.at[slot], r["vs"].at[slot], r["vr"].at[slot], to)
        cp.start()
        return cp

    vcps = [vec_send(vec, d - 1, to_z[d]) for d in range(1, Z)]

    W = {k: r["W" + k] for k in "jmxs"}
    blk = W["s"].shape[3]
    lnum = {k: i for i, k in enumerate("jmxset")}

    def qcols(hp, i):
        return pl.ds((3 * hp + i) * 2 * HD, 2 * HD)

    def local_copy(k, src, dst):
        pltpu.make_async_copy(src, dst, r["ls"].at[lnum[k]]).start()

    def local_wait(k, ref):
        pltpu.make_async_copy(ref, ref, r["ls"].at[lnum[k]]).wait()

    for i in range(3):
        for hp in range(half_heads // 2):
            src = r["wj"].at[:, span(i * D + c * HW + hp * 2 * HD, 2 * HD)]
            local_copy("j", src, W["j"].at[z, y, x, :, qcols(hp, i)])
    local_copy("m", r["wm"].at[:, span(c * HW, HW)], W["m"].at[z, y, x, :, span(c * HW, HW)])
    for i in range(FC // blk):
        local_copy("x", r["wx"].at[:, span(2 * blk * i + blk * c, blk)], W["x"].at[z, y, x, :, pl.ds(i * blk, blk)])
    local_copy("s", r["ws"].at[span(c * blk, blk), :], W["s"].at[z, y, x])
    local_copy("t", r["tok"], OUTB)
    local_copy("e", cot, EB.at[own, :])
    own_ref = {
        "j": W["j"].at[z, y, x],
        "m": W["m"].at[z, y, x, :, span(c * HW, HW)],
        "x": W["x"].at[z, y, x],
        "s": W["s"].at[z, y, x],
    }

    order = "jmxs"
    num = {(k, p): 4 * i + p for i, k in enumerate(order) for p in range(4)}

    def gcols(k, p):
        start, size = cuts["gather"][k][p]
        return span(c * HW + start, size) if k == "m" else pl.ds(start, size)

    def block(k, p, zz, yy=slice(None), xx=slice(None)):
        return W[k].at[zz, yy, xx, :, gcols(k, p)]

    def send(ref, ssem, rsem, to):
        remote(ref, ref, ssem, rsem, to).start()

    def line_block(k, p, zz):
        return block(k, p, zz, y, x) if p < 2 else block(k, p, zz)

    def line_send(k, p, zz, way):
        n = num[k, p]
        send(line_block(k, p, zz), r["az"].at[n, way, zz], r["bz"].at[n, zz], (up, down)[way])

    def line_start(k, p):
        @pl.when(z < Z - 1)
        def _():
            line_send(k, p, z, 0)

        @pl.when(z > 0)
        def _():
            line_send(k, p, z, 1)

    def line_arrive(k, p, t, then):
        def take(zz, way, more):
            n = num[k, p]
            ref = line_block(k, p, zz)
            remote(ref, ref, r["az"].at[n, way, zz], r["bz"].at[n, zz], up).wait_recv()

            @pl.when(more)
            def _():
                line_send(k, p, zz, way)

            then(zz)

        @pl.when(z >= t)
        def _():
            take(z - t, 0, z < Z - 1)

        @pl.when(z + t < Z)
        def _():
            take(z + t, 1, z > 0)

    def spread(k, p, zz):
        n = num[k, p]
        a, b = (to_y, to_x) if p == 0 else (to_x, to_y)
        ref = block(k, p, zz, y, x)
        send(ref, r["a2"].at[n], r["b2"].at[n, zz], a)
        send(ref, r["a3"].at[n], r["b3"].at[n], b)

    def second(k, p, zz):
        n = num[k, p]
        a, b = (to_y, to_x) if p == 0 else (to_x, to_y)
        ref = block(k, p, zz, 1 - y, x) if p == 0 else block(k, p, zz, y, 1 - x)
        remote(ref, ref, r["a2"].at[n], r["b2"].at[n, zz], a).wait_recv()
        send(ref, r["a3"].at[n], r["b3"].at[n], b)

    def g_z0(k, p, t):
        line_start(k, p)

    def g_fz(k, p, t):
        if t == 0:
            spread(k, p, z)
        else:
            line_arrive(k, p, t, functools.partial(spread, k, p))

    def g_f2(k, p, t):
        if t == 0:
            second(k, p, z)
        else:

            @pl.when(z >= t)
            def _():
                second(k, p, z - t)

            @pl.when(z + t < Z)
            def _():
                second(k, p, z + t)

    def g_p0(k, p, t):
        n = num[k, p]
        a, b = (to_x, to_y) if p == 2 else (to_y, to_x)
        send(block(k, p, z, y, x), r["a2"].at[n], r["b2"].at[n, 0], a)
        send(block(k, p, z, y, x), r["a3"].at[n], r["b3"].at[n], b)

    def g_p1(k, p, t):
        n = num[k, p]
        a, b = (to_x, to_y) if p == 2 else (to_y, to_x)
        ref = block(k, p, z, y, 1 - x) if p == 2 else block(k, p, z, 1 - y, x)
        remote(ref, ref, r["a2"].at[n], r["b2"].at[n, 0], a).wait_recv()
        send(ref, r["a3"].at[n], r["b3"].at[n], b)

    def g_p2(k, p, t):
        n = num[k, p]
        ref = block(k, p, z, 1 - y) if p == 2 else block(k, p, z, slice(None), 1 - x)
        remote(ref, ref, r["a3"].at[n], r["b3"].at[n], to_y if p == 2 else to_x).wait_recv()
        line_start(k, p)

    def g_pz(k, p, t):
        line_arrive(k, p, t, lambda zz: None)

    def gather_wait(k):
        for p in (0, 1):
            n = num[k, p]
            ref = block(k, p, slice(None), slice(None), 0) if p == 0 else block(k, p, slice(None), 0)
            remote(ref, ref, r["a3"].at[n], r["b3"].at[n], to_x if p == 0 else to_y).wait_recv()

    def gather_done(k):
        for p in range(4):
            if not cuts["gather"][k][p][1]:
                continue
            n = num[k, p]
            every = slice(None)
            if p < 2:
                done = [(block(k, p, every, 0, 0), "a2"), (block(k, p, every, every, 0), "a3")]
            else:
                done = [(block(k, p, 0, 0, 0), "a2"), (block(k, p, 0, 0), "a3")]
            for ref, s in done:
                remote(ref, ref, r[s].at[n], r["b3"].at[n], to_x).wait_send()
            for t in range(Z):
                ref = line_block(k, p, t)

                @pl.when((z < Z - 1) & (t <= z))
                def _():
                    remote(ref, ref, r["az"].at[n, 0, t], r["bz"].at[n, t], up).wait_send()

                @pl.when((z > 0) & (t >= z))
                def _():
                    remote(ref, ref, r["az"].at[n, 1, t], r["bz"].at[n, t], down).wait_send()

    GS, GX, GJ = r["GS"], W["s"], W["x"]
    grad = {"s": GS, "t": GS, "x": GX, "u": GX, "m": GM, "j": GJ, "k": GJ}
    gorder = "stxumjk"
    gnum = {(k, p): 4 * i + p for i, k in enumerate(gorder) for p in range(4)}
    outs = {k: r["o" + v] for k, v in zip(gorder, "ssxxmjj", strict=True)}

    def gslice(k, p):
        row, rows, begin, size = cuts["reduce"][k][p]
        return pl.ds(row, rows), span(c * HW + begin, size) if k == "m" else pl.ds(begin, size)

    def add_into(ref, idx, other):
        ref[idx] = (ref[idx].astype(F32) + other[...].astype(F32)).astype(BF16)

    def part(k, p, zz, yy, xx):
        return grad[k].at[(zz, yy, xx, *gslice(k, p))]

    def s1(k, p):
        n = gnum[k, p]
        every = slice(None)
        if p < 2:
            src = part(k, p, every, every, 1 - x) if p == 0 else part(k, p, every, 1 - y, every)
            return [remote(src, r["R1%s%d" % (k, p)], r["c1"].at[n, 0], r["d1"].at[n, 0], to_x if p == 0 else to_y)]
        return [
            remote(
                part(k, p, zplus(d), every, every),
                r["R1%s%d" % (k, p)].at[d - 1],
                r["c1"].at[n, d - 1],
                r["d1"].at[n, d - 1],
                to_z[d],
            )
            for d in range(1, Z)
        ]

    def s2(k, p):
        n = gnum[k, p]
        every = slice(None)
        src, to = {
            0: lambda: (part(k, p, every, 1 - y, x), to_y),
            1: lambda: (part(k, p, every, y, 1 - x), to_x),
            2: lambda: (part(k, p, z, 1 - y, every), to_y),
            3: lambda: (part(k, p, z, every, 1 - x), to_x),
        }[p]()
        return [remote(src, r["R2%s%d" % (k, p)], r["c2"].at[n], r["d2"].at[n], to)]

    def s3(k, p):
        n = gnum[k, p]
        if p < 2:
            return [
                remote(
                    part(k, p, zplus(d), y, x),
                    r["R3%s%d" % (k, p)].at[d - 1],
                    r["c3"].at[n, d - 1],
                    r["d3"].at[n, d - 1],
                    to_z[d],
                )
                for d in range(1, Z)
            ]
        src, to = (part(k, p, z, y, 1 - x), to_x) if p == 2 else (part(k, p, z, 1 - y, x), to_y)
        return [remote(src, r["R3%s%d" % (k, p)].at[0], r["c3"].at[n, 0], r["d3"].at[n, 0], to)]

    def start(copies):
        for cp in copies:
            cp.start()

    def arrived(copies):
        for cp in copies:
            cp.wait_recv()

    def r_S1(k, p, t):
        start(s1(k, p))

    def r_A1(k, p, t):
        arrived(s1(k, p))
        R1 = r["R1%s%d" % (k, p)]
        sl = gslice(k, p)
        for q in (1, 0):
            if p < 2:
                yy = y if q == 0 else 1 - y
                xx = x if q == 0 else 1 - x

                def one(i, _):
                    if p == 0:
                        add_into(grad[k], (i, yy, x, *sl), R1.at[i, yy])
                    else:
                        add_into(grad[k], (i, y, xx, *sl), R1.at[i, xx])
                    return 0

                lax.fori_loop(0, Z, one, 0)
            else:
                for i in range(2):
                    yy, xx = (1 - y if q else y, i) if p == 2 else (i, 1 - x if q else x)
                    idx = (z, yy, xx, *sl)
                    tot = grad[k][idx].astype(F32)
                    for d in range(1, Z):
                        tot = tot + R1[d - 1, yy, xx].astype(F32)
                    grad[k][idx] = tot.astype(BF16)
            if q == 1:
                start(s2(k, p))

    def r_A2(k, p, t):
        arrived(s2(k, p))
        R2 = r["R2%s%d" % (k, p)]
        sl = gslice(k, p)
        if p < 2:

            def one(i, _):
                add_into(grad[k], (i, y, x, *sl), R2.at[i])
                return 0

            lax.fori_loop(0, Z, one, 0)
            start(s3(k, p))
        else:
            for q in (1, 0):
                yy, xx = (y, 1 - x if q else x) if p == 2 else (1 - y if q else y, x)
                add_into(grad[k], (z, yy, xx, *sl), R2.at[xx if p == 2 else yy])
                if q == 1:
                    start(s3(k, p))

    def r_A3(k, p, t):
        arrived(s3(k, p))
        R3 = r["R3%s%d" % (k, p)]
        idx = (z, y, x, *gslice(k, p))
        tot = grad[k][idx].astype(F32)
        for i in range(R3.shape[0]):
            tot = tot + R3[i].astype(F32)
        grad[k][idx] = tot.astype(BF16)

    fin_copies = []

    def r_F(k, p, t):
        i = gorder.index(k)
        row, rows, begin, size = cuts["reduce"][k][0]
        size = sum(q[3] for q in cuts["reduce"][k])
        rs = pl.ds(row, rows)
        total = grad[k].at[z, y, x, rs, span(c * HW + begin, size) if k == "m" else pl.ds(begin, size)]
        dst = outs[k].at[c, rs, pl.ds(begin, size)]
        a = pltpu.make_async_copy(total, dst, r["fl"].at[i])
        b = remote(total, dst, r["fs"].at[i], r["fr"].at[i], to_o)
        a.start()
        b.start()
        fin_copies.extend([a, b])

    TQ, TR = 256, 256
    FT = Y * X * blk // 2
    DT = Y * X * W["j"].shape[3]
    copies = {}
    lane = lax.broadcasted_iota(jnp.int32, (1, 2 * HD), 1) // HD

    def normed(h):
        center = h - jnp.mean(h, axis=-1, keepdims=True)
        inverse = lax.rsqrt(jnp.mean(center * center, axis=-1, keepdims=True) + 1e-06)
        return center * inverse, inverse

    def c_rows():
        slots = r["len"].shape[1]
        sub = lax.broadcasted_iota(jnp.int32, (slots, slots), 0)
        lan = lax.broadcasted_iota(jnp.int32, (slots, slots), 1)
        lens, dist = r["len"][...].astype(F32), r["dist"][...].astype(F32)
        ends = jnp.sum(jnp.where(lan <= sub, lens, 0.0), axis=1, keepdims=True)
        dist = jnp.sum(jnp.where(lan == sub, dist, 0.0), axis=1, keepdims=True)
        places = lax.broadcasted_iota(jnp.int32, (slots, R), 1).astype(F32)
        segment = jnp.sum(jnp.where(ends <= places, 1.0, 0.0), axis=0, keepdims=True)
        slot = lax.broadcasted_iota(jnp.int32, (slots, R), 0).astype(F32)
        ground = jnp.sum(jnp.where(slot == segment, dist, 0.0), axis=0, keepdims=True)
        alive = jnp.where(segment < slots, 1.0, 0.0)
        factor = ground / 10.0
        patch = r["patch"][...].astype(F32)
        down_ = jnp.floor((patch + 0.5) * (1.0 / 14.0))
        along = patch - 14.0 * down_
        zero = jnp.zeros_like(factor)
        rows = jnp.concatenate([segment, alive, down_ * factor, along * factor, zero, zero, zero, zero], axis=0)
        SEG[c] = rows
        COL[...] = jnp.transpose(rows)
        copies["seg"] = to_pair(SEG.at[c], SEG.at[c])

    def c_v1():
        for cp in vcps:
            cp.wait()
        acc = vec[...].astype(F32)
        for d in range(1, Z):
            acc = acc + VR[d - 1].astype(F32)
        VT[0] = acc.astype(BF16)
        copies["vy"] = vec_send(VT.at[0], Z - 1, to_y)

    def c_v2():
        copies["vy"].wait()
        VT[1] = (VT[0].astype(F32) + VR[Z - 1].astype(F32)).astype(BF16)
        copies["vx"] = vec_send(VT.at[1], Z, to_x)

    def c_v3():
        copies["vx"].wait()
        V[...] = VT[1].astype(F32) + VR[Z].astype(F32)
        VG[...] = jnp.zeros_like(VG)

    def c_h0():
        local_wait("t", OUTB)
        local_wait("e", EB.at[own, :])

        def rows128(i, _):
            rr, gr = span(i * 128, 128), span(c * R + i * 128, 128)
            EB[gr, :] = (EB[gr, :].astype(F32) * COL[rr, 1:2]).astype(BF16)
            Q = D // 4
            for j in (0, 1):
                angle = COL[rr, 2 + j : 3 + j] * r["freq"][...]
                at_ = 2 * j * Q
                H0[rr, at_ : at_ + Q] = OUTB[rr, at_ : at_ + Q].astype(F32) + jnp.sin(angle)
                at_ += Q
                H0[rr, at_ : at_ + Q] = OUTB[rr, at_ : at_ + Q].astype(F32) + jnp.cos(angle)
            return 0

        lax.fori_loop(0, R // 128, rows128, 0)
        copies["eb"] = to_pair(EB.at[own, :], EB.at[own, :])

    def c_ln1():
        def norm_one(i, _):
            rr, gr = span(i * 128, 128), span(c * R + i * 128, 128)
            scaled, _i = normed(H0[rr, :])
            N1[gr, :] = (scaled * V[0:1, :] + V[1:2, :]).astype(BF16)
            VG[5:6, :] += jnp.sum(EB[gr, :].astype(F32), axis=0, keepdims=True)
            return 0

        lax.fori_loop(0, R // 128, norm_one, 0)
        copies["n1"] = to_pair(N1.at[own, :], N1.at[own, :])

    def c_qkv(t):
        if t == 0:
            copies["seg"].wait()
            copies["n1"].wait()
            copies["eb"].wait()
            gather_wait("j")
        w = W["j"][:, :, :, :, t * TQ : (t + 1) * TQ].reshape(D, TQ)
        f = t * TQ
        b = V[6 + f // D : 7 + f // D, f % D : f % D + TQ]
        QKV[:, f : f + TQ] = (matmul(N1[...], w) + b).astype(BF16)

    def same_image(g):
        return jnp.transpose(SEG[g])[:, 0:1] == SEG[g, 0:1, :]

    def attend(g, hp):
        rr = span(g * R, R)
        q, k, v = (QKV[rr, qcols(hp, i)] for i in range(3))
        same = same_image(g)
        res = []
        for i in (0, 1):
            qi = jnp.where(lane == i, q.astype(F32) * HD**-0.5, 0.0).astype(BF16)
            s = jnp.where(same, contract(k, qi, LAST), NEVER)
            top = jnp.max(s, axis=0, keepdims=True)
            e = jnp.exp(s - top)
            tot = jnp.sum(e, axis=0, keepdims=True)
            L[g * half_heads + 2 * hp + i] = top + jnp.log(tot)
            pb = (e * (1.0 / tot)).astype(BF16)
            res.append(contract(v, pb, FIRST)[i * HD : (i + 1) * HD])
        return jnp.transpose(jnp.concatenate(res, axis=0)).astype(BF16)

    pairs = half_heads // 2

    def c_at(i):
        if i < pairs:
            OS[:, 2 * HD * i : 2 * HD * (i + 1)] = attend(o, i)
            if i == pairs - 1:
                copies["o"] = to_pair(OS, OA.at[:, span(c * HW, HW)])
        else:
            OA[:, span(c * HW + 2 * HD * (i - pairs), 2 * HD)] = attend(c, i - pairs)

    def c_wm():
        gather_wait("m")
        half = W["m"].at[:, :, :, :, span(c * HW, HW)]
        copies["wm"] = to_pair(half, half)

    def c_mrg():
        copies["o"].wait()
        copies["wm"].wait()
        for t in range(R // TR):
            rr = pl.ds(t * TR, TR)
            h1 = H0[rr, :] + matmul(OA[rr, :], W["m"][...].reshape(D, D)) + V[2:3, :]
            H1[rr, :] = h1
            scaled, _i = normed(h1)
            N2[span(c * R + t * TR, TR), :] = (scaled * V[3:4, :] + V[4:5, :]).astype(BF16)
        copies["n2"] = to_pair(N2.at[own, :], N2.at[own, :])

    def c_ge(t):
        if t == 0:
            copies["n2"].wait()
            gather_wait("x")
        cc = slice(t * TQ, (t + 1) * TQ)
        f = t * TQ
        b = V[8 + f // D : 9 + f // D, f % D : f % D + TQ]
        for h in range(2):
            rr = slice(h * R, (h + 1) * R)
            u = matmul(N2[rr, :], W["x"][:, :, :, :, cc].reshape(D, TQ)) + b
            cdf = 0.5 * (1.0 + lax.erf(u * 0.7071067811865476))
            G[rr, cc] = (u * cdf).astype(BF16)
            DU[rr, cc] = (cdf + u * (jnp.exp(-0.5 * u * u) * 0.3989422804014327)).astype(BF16)

    def c_gs(i):
        for t in (2 * i, 2 * i + 1):
            g = contract(G[:, t * FT : (t + 1) * FT], EB[...], FIRST)
            GS[t // Y, t % Y] = g.astype(BF16).reshape(X, blk, D)

    def c_du(i):
        if i == 0:
            gather_wait("s")
        for t in (2 * i, 2 * i + 1):
            cc = slice(t * FT, (t + 1) * FT)
            w = W["s"][t // Y, t % Y].reshape(FT, D)
            row, col = 8 + t * FT // D, t * FT % D
            for h in range(2):
                rr = slice(h * R, (h + 1) * R)
                du = (contract(EB[rr, :], w, LAST) * DU[rr, cc].astype(F32)).astype(BF16)
                DU[rr, cc] = du
                VG[row : row + 1, col : col + FT] += jnp.sum(du.astype(F32), axis=0, keepdims=True)

    def c_h2s():
        for t in range(D // TQ):
            cc = slice(t * TQ, (t + 1) * TQ)
            XS[:, cc] = matmul(G[sib, :], W["s"][:, :, :, :, cc].reshape(FC, TQ)).astype(BF16)
        copies["h2"] = to_pair(XS, OUTB)

    def c_h2o():
        copies["h2"].wait_recv()
        for t in range(D // TQ):
            cc = slice(t * TQ, (t + 1) * TQ)
            own_part = matmul(G[own, :], W["s"][:, :, :, :, cc].reshape(FC, TQ))
            OUTB[:, cc] = (
                (H1[:, cc] + own_part + OUTB[:, cc].astype(F32) + V[5:6, cc]) * COL[:, 1:2]
            ).astype(BF16)
        copies["out"] = pltpu.make_async_copy(OUTB, r["out"], r["fl"].at[len(gorder)])
        copies["out"].start()
        gather_done("s")

    def back_part(left, wk, n, name, dst):
        for t in range(Z):
            w = wk[t][:, :, :, 0:n].reshape(DT, n)
            dst[:, t * DT : (t + 1) * DT] = contract(left[sib, 0:n], w, LAST).astype(BF16)
        copies[name] = to_pair(dst, XR)

    def c_dn2s():
        back_part(DU, W["x"], FC, "dn2", DA)

    def c_gx(i):
        h, half = W["j"].shape[3], FC // 2
        for t in range(Z):
            g = contract(N2[:, t * DT : (t + 1) * DT], DU[:, i * half : (i + 1) * half], FIRST)
            GX[t, :, :, i * h : (i + 1) * h, :] = g.astype(BF16).reshape(Y, X, h, half)

    def norm_back(dy, scaled, inverse, gain, vg):
        ds_ = dy * gain
        VG[vg : vg + 1, :] += jnp.sum(dy * scaled, axis=0, keepdims=True)
        VG[vg + 1 : vg + 2, :] += jnp.sum(dy, axis=0, keepdims=True)
        cen = ds_ - jnp.mean(ds_, axis=-1, keepdims=True)
        cen = cen - scaled * jnp.mean(ds_ * scaled, axis=-1, keepdims=True)
        return cen * inverse

    def c_dn2o():
        copies["dn2"].wait()
        for t in range(R // TR):
            rr, gr = pl.ds(t * TR, TR), span(c * R + t * TR, TR)
            dy = contract(DU[gr, :], W["x"][...].reshape(D, FC), LAST) + XR[rr, :].astype(F32)
            scaled, inverse = normed(H1[rr, :])
            dh = EB[gr, :].astype(F32) + norm_back(dy, scaled, inverse, V[3:4, :], 3)
            H1[rr, :] = dh
            DA[rr, :] = dh.astype(BF16)
            VG[2:3, :] += jnp.sum(DA[rr, :].astype(F32), axis=0, keepdims=True)
        gather_done("x")

    def c_dO():
        copies["h2"].wait_send()
        cw = X * W["m"].shape[3]
        for t, base in enumerate((o, c)):
            for u in range(HW // cw):
                w = W["m"][base * (Z // 2) + u // Y, u % Y].reshape(cw, D)
                res = contract(DA[...], w, LAST).astype(BF16)
                if t == 0:
                    OS[:, u * cw : (u + 1) * cw] = res
                else:
                    G[own, 3 * HW + u * cw : 3 * HW + (u + 1) * cw] = res
            if t == 0:
                copies["do"] = to_pair(OS, G.at[own, pl.ds(3 * HW, HW)])
        gather_done("m")

    def c_gm():
        for t in range(Z):
            g = contract(OA[:, t * DT : (t + 1) * DT], DA[...], FIRST)
            GM[t] = g.astype(BF16).reshape(Y, X, W["m"].shape[3], D)
        copies["gm"] = to_pair(GM.at[:, :, :, :, span(o * HW, HW)], r["GMR"])

    def c_gma():
        copies["gm"].wait()

        def add_pair(i, _):
            for j in range(Y * X):
                idx = (i, j // X, j % X, slice(None), span(c * HW, HW))
                add_into(GM, idx, r["GMR"].at[i, j // X, j % X])
            return 0

        lax.fori_loop(0, Z, add_pair, 0)

    def attend_back(g, hp):
        rr = span(g * R, R)
        qc, kc, vc = (qcols(hp, i) for i in range(3))
        q, k, v = QKV[rr, qc], QKV[rr, kc], QKV[rr, vc]
        do = G[rr, 3 * HW + hp * 2 * HD : 3 * HW + (hp + 1) * 2 * HD]
        same = same_image(g)
        dq, dk, dv = [], [], []
        for i in (0, 1):
            qi = jnp.where(lane == i, q.astype(F32) * HD**-0.5, 0.0).astype(BF16)
            di = jnp.where(lane == i, do.astype(F32), 0.0).astype(BF16)
            s = jnp.where(same, contract(k, qi, LAST), NEVER)
            pr = jnp.exp(s - L[g * half_heads + 2 * hp + i])
            dp = contract(v, di, LAST)
            delta = jnp.sum(pr * dp, axis=0, keepdims=True)
            dsb = (pr * (dp - delta) * HD**-0.5).astype(BF16)
            dq.append(contract(k, dsb, FIRST)[i * HD : (i + 1) * HD])
            dk.append(matmul(dsb, q))
            dv.append(matmul(pr.astype(BF16), do))
        G[rr, qc] = jnp.transpose(jnp.concatenate(dq, axis=0)).astype(BF16)
        G[rr, kc] = jnp.where(lane == 0, dk[0], dk[1]).astype(BF16)
        G[rr, vc] = jnp.where(lane == 0, dv[0], dv[1]).astype(BF16)

    def c_ab(i):
        few = pairs // 2
        if i == few:
            copies["do"].wait()
        attend_back(c if i % pairs < few else o, i // pairs * few + i % few)

    def c_gj(i):
        half = 3 * HW // 2
        for t in range(Z):
            g = contract(N1[:, t * DT : (t + 1) * DT], G[:, i * half : (i + 1) * half], FIRST)
            GJ[t, :, :, :, i * half : (i + 1) * half] = g.astype(BF16).reshape(Y, X, W["j"].shape[3], half)

    def c_dn1s():
        back_part(G, W["j"], 3 * HW, "dn1", XS)
        for t in range(3):
            row, col = 6 + t * HW // D, t * HW % D
            VG[row : row + 1, col : col + HW] += jnp.sum(
                G[:, t * HW : (t + 1) * HW].astype(F32), axis=0, keepdims=True
            )

    def c_dn1o():
        copies["dn1"].wait()
        for t in range(R // TR):
            rr, gr = pl.ds(t * TR, TR), span(c * R + t * TR, TR)
            dy = contract(G[gr, 0 : 3 * HW], W["j"][...].reshape(D, 3 * HW), LAST) + XR[rr, :].astype(F32)
            scaled, inverse = normed(H0[rr, :])
            H1[rr, :] = H1[rr, :] + norm_back(dy, scaled, inverse, V[0:1, :], 0)
        copies["gt"] = pltpu.make_async_copy(H1, r["gt"], r["fl"].at[len(gorder) + 1])
        copies["gt"].start()
        gather_done("j")

    def vg_send(slot, to):
        cp = remote(VG, VGR.at[slot], r["gs"].at[slot], r["gr"].at[slot], to)
        cp.start()
        return cp

    def vg_add(slots):
        acc = VG[...]
        for i in slots:
            acc = acc + VGR[i]
        VG[...] = acc

    def c_vz():
        copies["gz"] = [vg_send(d - 1, to_z[d]) for d in range(1, Z)]

    def c_vx():
        for cp in copies["gz"]:
            cp.wait()
        vg_add(range(Z - 1))
        copies["gx"] = vg_send(Z - 1, to_x)

    def c_vy():
        copies["gx"].wait()
        vg_add([Z - 1])
        copies["gy"] = vg_send(Z, to_y)

    def c_vp():
        copies["gy"].wait()
        vg_add([Z])
        copies["ov"] = pltpu.make_async_copy(VG, r["ov"].at[c], r["fl"].at[len(gorder) + 2])
        copies["ov"].start()
        copies["ovr"] = to_pair(VG, r["ov"].at[c])

    def c_end():
        for k in gorder:
            for p in range(4):
                if cuts["reduce"][k][p][3]:
                    for cp in s1(k, p) + s2(k, p) + s3(k, p):
                        cp.wait_send()
        for cp in fin_copies + [copies[n] for n in ("out", "gt", "ov", "ovr")]:
            cp.wait()

    steps = locals()
    landed = set()
    for word in schedule:
        if word[0] == "_":
            name = word[1:].rstrip("0123456789")
            if name in ("v", "h", "ln"):
                name = word[1:]
            arg = word[1 + len(name) :]
            steps["c_" + name](*([int(arg)] if arg else []))
            continue
        op, k, p, t = word[:2], word[2], int(word[3]), int(word[4])
        if op in ("z0", "p0", "fz") and t == 0 and k not in landed:
            landed.add(k)
            local_wait(k, own_ref[k])
        steps[("r_" if op[0] in "SAF" else "g_") + op.rstrip("_")](k, p, t)


def spread_vector(piece, me, count):
    n = piece.shape[0]
    place = jnp.arange(n * count, dtype=jnp.int32) // n
    return jnp.where(place == me, jnp.tile(piece, count), 0).astype(BF16)


def finish_kernel(dims, names, *args):
    r = dict(zip(names, args, strict=True))
    N = dims[0] * dims[1] * dims[2]
    big = [
        pltpu.make_async_copy(r["out"], r["f_out"], r["sem"].at[0]),
        pltpu.make_async_copy(r["gt"], r["f_gt"], r["sem"].at[1]),
    ]
    for cp in big:
        cp.start()
    rj, D = r["f_m"].shape
    HW, P2 = D // 2, 2 * HD
    blk = r["os"].shape[1]
    half = r["ox"].shape[2]
    for core in (0, 1):
        for hp in range(HW // P2):
            for i in range(3):
                to, of = i * D + core * HW + hp * P2, (3 * hp + i) * P2
                r["f_j"][:, to : to + P2] = r["oj"][core, :, of : of + P2].astype(F32)
        r["f_m"][:, core * HW : (core + 1) * HW] = r["om"][core].astype(F32)
        for i in range(2 * half // blk):
            row, col = i * blk // half * rj, i * blk % half
            to = (2 * i + core) * blk
            r["f_x"][:, to : to + blk] = r["ox"][core, row : row + rj, col : col + blk].astype(F32)
        r["f_s"][core * blk : (core + 1) * blk, :] = r["os"][core].astype(F32)
    me = lax.axis_index("dp")
    ov = r["ov"]
    both = ov[0, 0:8, :] + ov[1, 0:8, :]

    def mine(row, n):
        return pltpu.roll(row, (N - me) * n, 1)[:, :n]

    for i, name in enumerate(("g1", "b1", "mb", "g2", "b2", "sb")):
        r["f_" + name][...] = mine(jnp.broadcast_to(both[i : i + 1], (8, D)), D // N)[0:1]
    at_ = [((3 * hp + i) * P2, core) for i in range(3) for core in (0, 1) for hp in range(HW // P2)]
    row = jnp.concatenate([ov[core, 6 + a // D : 7 + a // D, a % D : a % D + P2] for a, core in at_], axis=1)
    r["f_jb"][...] = mine(jnp.broadcast_to(row, (8, 3 * D)), 3 * D // N)[0:1]
    for core in (0, 1):
        row = jnp.concatenate([ov[core, 8 + i : 9 + i, :] for i in range(2 * half // D)], axis=1)
        r["f_xb"][:, core * blk : (core + 1) * blk] = mine(jnp.broadcast_to(row, (8, 2 * half)), blk)[0:1]
    for cp in big:
        cp.wait()


def tiled_cuts(width, side):
    main = width // 2 - side * 128
    sizes = (main, main, side * 128, side * 128)
    starts = (0, main, 2 * main, 2 * main + side * 128)
    return list(zip(starts, sizes, strict=True))


def paths(rows, row, begin, width, side):
    return [(row, rows, begin + q, size) for q, size in tiled_cuts(width, side)]


def fused_layer(dims, *args):
    (
        tokens,
        kept_patch,
        image_lengths,
        ground_distance,
        cotangent,
        norm_one_gain,
        norm_one_bias,
        joint_weight,
        joint_bias,
        merge_weight,
        merge_bias,
        norm_two_gain,
        norm_two_bias,
        expand_weight,
        expand_bias,
        shrink_weight,
        shrink_bias,
    ) = args
    Z, Y, X = dims
    N = Z * Y * X
    R, D = tokens.shape
    FF = expand_weight.shape[1]
    HW, FC, blk = D // 2, FF // 2, shrink_weight.shape[0] // 2
    rj = joint_weight.shape[0]
    me, c = lax.axis_index("dp"), lax.axis_index("rep")
    jb = spread_vector(joint_bias, me, N).reshape(3, 2, HW // (2 * HD), 2 * HD)
    jb = jnp.where(c == 0, jb[:, 0], jb[:, 1]).transpose(1, 0, 2).reshape(-1)
    xb = spread_vector(expand_bias, me, N).reshape(FF // (2 * blk), 2, blk)
    xb = jnp.where(c == 0, xb[:, 0], xb[:, 1]).reshape(-1)
    flat = [
        spread_vector(v, me, N)
        for v in (norm_one_gain, norm_one_bias, merge_bias, norm_two_gain, norm_two_bias, shrink_bias)
    ]
    flat += [jb, jnp.zeros((2 * D - 3 * HW,), BF16), xb]
    flat.append(jnp.zeros((16 * D - sum(v.shape[0] for v in flat),), BF16))
    vec = jnp.concatenate(flat).reshape(16, D)
    quarter = D // 4
    freq = 1.0 / 10000.0 ** (jnp.arange(quarter, dtype=F32) / quarter)

    cuts = {
        "gather": {
            "j": tiled_cuts(3 * HW, 1),
            "m": tiled_cuts(HW, 0),
            "x": tiled_cuts(FC, 1),
            "s": tiled_cuts(D, 1),
        },
        "reduce": {
            "s": paths(blk, 0, 0, D // 2, SIDE["s"]),
            "t": paths(blk, 0, D // 2, D // 2, SIDE["t"]),
            "x": paths(rj, 0, 0, FC // 2, SIDE["x"]),
            "u": paths(rj, rj, 0, FC // 2, SIDE["u"]),
            "m": paths(rj, 0, 0, HW, 0),
            "j": paths(rj, 0, 0, 3 * HW // 2, SIDE["j"]),
            "k": paths(rj, 0, 3 * HW // 2, 3 * HW // 2, SIDE["k"]),
        },
    }

    vm, hbm = pl.BlockSpec(memory_space=pltpu.VMEM), pl.BlockSpec(memory_space=pl.ANY)
    ins = [("patch", kept_patch.reshape(1, R), vm), ("len", image_lengths, vm), ("dist", ground_distance, vm)]
    ins += [("freq", freq[None, :], vm), ("vec", vec, vm), ("tok", tokens, hbm), ("cot", cotangent, hbm)]
    ins += [("wj", joint_weight, hbm), ("wm", merge_weight, hbm), ("wx", expand_weight, hbm), ("ws", shrink_weight, hbm)]
    S = jax.ShapeDtypeStruct
    outs = [
        ("out", S((R, D), BF16), hbm),
        ("gt", S((R, D), F32), hbm),
        ("oj", S((2, rj, 3 * HW), BF16), hbm),
        ("om", S((2, rj, HW), BF16), hbm),
        ("ox", S((2, 2 * rj, FC // 2), BF16), hbm),
        ("os", S((2, blk, D), BF16), hbm),
        ("ov", S((2, 16, D), F32), hbm),
    ]
    V = pltpu.VMEM
    dma = pltpu.SemaphoreType.DMA
    scratch = [
        ("Wj", V((Z, Y, X, rj, 3 * HW), BF16)),
        ("Wm", V((Z, Y, X, rj, D), BF16)),
        ("Wx", V((Z, Y, X, rj, FC), BF16)),
        ("Ws", V((Z, Y, X, blk, D), BF16)),
        ("GS", V((Z, Y, X, blk, D), BF16)),
        ("GM", V((Z, Y, X, rj, D), BF16)),
        ("GMR", V((Z, Y, X, rj, HW), BF16)),
        ("H0", V((R, D), F32)),
        ("N1", V((2 * R, D), BF16)),
        ("QKV", V((2 * R, 3 * HW), BF16)),
        ("OA", V((R, D), BF16)),
        ("H1", V((R, D), F32)),
        ("N2", V((2 * R, D), BF16)),
        ("G", V((2 * R, FC), BF16)),
        ("DU", V((2 * R, FC), BF16)),
        ("EB", V((2 * R, D), BF16)),
        ("SEG", V((2, 8, R), F32)),
        ("COL", V((R, 8), F32)),
        ("L", V((D // HD, 1, R), F32)),
        ("V", V((16, D), F32)),
        ("VR", V((Z + 1, 16, D), BF16)),
        ("VT", V((2, 16, D), BF16)),
        ("VG", V((16, D), F32)),
        ("VGR", V((Z + 1, 16, D), F32)),
        ("XS", V((R, D), BF16)),
        ("XR", V((R, D), BF16)),
        ("OUTB", V((R, D), BF16)),
        ("DA", V((R, D), BF16)),
    ]
    for k, four in cuts["reduce"].items():
        for p, (_, n, _, w) in enumerate(four):
            if w:
                first = (Z, 2) if p < 2 else (Z - 1, Y, X)
                second, third = ((Z,), (Z - 1,)) if p < 2 else ((2,), (1,))
                for name, lead in (("R1", first), ("R2", second), ("R3", third)):
                    scratch.append(("%s%s%d" % (name, k, p), V((*lead, n, w), BF16)))
    for name, shape in (
        ("ps", (12,)),
        ("pr", (12,)),
        ("vs", (Z + 1,)),
        ("vr", (Z + 1,)),
        ("gs", (Z + 1,)),
        ("gr", (Z + 1,)),
        ("ls", (6,)),
        ("az", (16, 2, Z)),
        ("bz", (16, Z)),
        ("a2", (16,)),
        ("b2", (16, Z)),
        ("a3", (16,)),
        ("b3", (16,)),
        ("c1", (28, Z - 1)),
        ("d1", (28, Z - 1)),
        ("c2", (28,)),
        ("d2", (28,)),
        ("c3", (28, Z - 1)),
        ("d3", (28, Z - 1)),
        ("fl", (10,)),
        ("fs", (7,)),
        ("fr", (7,)),
    ):
        scratch.append((name, dma(shape)))
    names = [n for n, *_ in ins + outs + scratch]
    res = pl.pallas_call(
        functools.partial(layer_kernel, dims, cuts, SCHEDULE, names),
        out_shape=[s for _, s, _ in outs],
        in_specs=[s for _, _, s in ins],
        out_specs=[s for _, _, s in outs],
        scratch_shapes=[s for _, s in scratch],
        compiler_params=pltpu.CompilerParams(
            collective_id=0, has_side_effects=True, vmem_limit_bytes=VMEM_BYTES
        ),
    )(*[a for _, a, _ in ins])

    given = [(n, a, hbm if n in ("out", "gt") else vm) for (n, _, _), a in zip(outs, res, strict=True)]
    made = [("f_out", S((R, D), BF16), hbm), ("f_gt", S((R, D), F32), hbm)]
    made += [("f_" + n, S((1, D // N), F32), vm) for n in ("g1", "b1", "mb", "g2", "b2", "sb")]
    made += [("f_jb", S((1, 3 * D // N), F32), vm), ("f_xb", S((1, FF // N), F32), vm)]
    made += [("f_j", S((rj, 3 * D), F32), vm), ("f_m", S((rj, D), F32), vm)]
    made += [("f_x", S((rj, FF), F32), vm), ("f_s", S((2 * blk, D), F32), vm)]
    last = pl.pallas_call(
        functools.partial(finish_kernel, dims, [n for n, *_ in given + made] + ["sem"]),
        out_shape=[s for _, s, _ in made],
        in_specs=[s for _, _, s in given],
        out_specs=[s for _, _, s in made],
        scratch_shapes=[dma((2,))],
        compiler_params=pltpu.CompilerParams(vmem_limit_bytes=32 * 2**20),
    )(*[a for _, a, _ in given])
    f = {n[2:]: a for (n, *_), a in zip(made, last, strict=True)}
    g1, b1, mb, g2, b2, sb, g_jb, g_xb = (f[n].reshape(-1) for n in ("g1", "b1", "mb", "g2", "b2", "sb", "jb", "xb"))
    return f["out"], f["gt"], g1, b1, f["j"], g_jb, f["m"], mb, g2, b2, f["x"], g_xb, f["s"], sb


def layout(mesh, joint_rows, shrink_rows):
    n = mesh.shape["dp"]
    if mesh.shape["rep"] != 2 or n != 16 or joint_rows % 16 or shrink_rows % 256:
        return None
    return (n // 4, 2, 2)


def on_device(mesh, *args):
    dims = layout(mesh, args[7].shape[0], args[15].shape[0])
    if dims is None:
        return general_layer(*args)
    return fused_layer(dims, *args)


def solution(mesh):
    rows, rows2 = P(("dp", "rep")), P(("dp", "rep"), None)
    vector, matrix = P("dp"), P("dp", None)
    return jax.shard_map(
        functools.partial(on_device, mesh),
        mesh=mesh,
        in_specs=(
            rows2,
            rows,
            rows2,
            rows2,
            rows2,
            vector,
            vector,
            matrix,
            vector,
            matrix,
            vector,
            vector,
            vector,
            matrix,
            vector,
            matrix,
            vector,
        ),
        out_specs=(
            rows2,
            rows2,
            vector,
            vector,
            matrix,
            vector,
            matrix,
            vector,
            vector,
            vector,
            matrix,
            vector,
            matrix,
            vector,
        ),
        check_vma=False,
    )
```

```python
import functools

import jax
import jax.numpy as jnp
import numpy as np
from jax import lax
from jax.experimental import pallas as pl
from jax.experimental.pallas import tpu as pltpu
from jax.sharding import PartitionSpec as P

HD = 64
MESH = pl.DeviceIdType.MESH
F32 = jnp.float32
BF16 = jnp.bfloat16
NEVER = -1000000000.0
VMEM_BYTES = 127 * 2**19
SIDE = {"s": 1, "t": 0, "x": 1, "u": 0, "j": 1, "k": 0}
SCHEDULE = [
    "fzj00", "z0m10", "z0j00", "z0j10", "p0j20", "z0x00", "fzm10", "z0m00", "p0j30", "p0x20", "p0s20", "_rows",
    "_v1", "p1j20", "fzx10", "fzj10", "p0s30", "p1j30", "fzj11", "p0x30", "z0s10", "p1x20", "f2j10", "p2j20",
    "fzj12", "fzx00", "fzj01", "p1x30", "fzm11", "pzj21", "_v2", "f2j00", "p2j30", "fzj02", "pzj22", "z0x10",
    "f2j11", "p1s30", "fzj03", "fzj13", "pzj31", "f2j12", "_h0", "fzm12", "f2j01", "_v3", "pzj32", "f2x10", "f2j13",
    "fzm01", "p2x20", "fzm13", "pzj33", "pzj23", "f2j02", "_ln1", "fzm00", "f2j03", "fzx01", "f2m11", "fzm03",
    "p1s20", "fzm02", "fzx11", "p2s30", "_qkv0", "fzx12", "z0s00", "_qkv1", "f2m01", "f2m13", "_qkv2", "_qkv3",
    "fzx02", "_qkv4", "_qkv5", "f2m00", "_at0", "f2m12", "_at1", "pzx21", "_at2", "p2x30", "fzx13", "f2m10", "_at3",
    "f2m02", "pzs31", "_at4", "_at5", "p2s20", "fzx03", "f2m03", "pzx22", "_at6", "f2x11", "f2x13", "f2x00", "pzx31",
    "f2x12", "_at7", "_wm", "f2x02", "f2x03", "pzs32", "f2x01", "fzs11", "pzx32", "_mrg", "pzs21", "fzs00", "fzs10",
    "pzx23", "pzx33", "fzs12", "fzs01", "_ge0", "_ge1", "_ge2", "_ge3", "_ge4", "fzs13", "_ge5", "_ge6", "_ge7",
    "fzs02", "_gs0", "_gs1", "fzs03", "pzs22", "_gs2", "f2s10", "f2s00", "_gs3", "f2s11", "f2s01", "f2s12", "f2s02",
    "pzs33", "pzs23", "f2s13", "f2s03", "S1s30", "S1t10", "S1t00", "_du0", "S1s00", "_du1", "_du2", "S1s20", "_du3",
    "S1s10", "_h2s", "_dn2s", "A1t10", "A1t00", "_h2o", "_gx0", "A1s10", "S1x30", "A1s30", "A1s00", "_gx1", "S1x10",
    "S1u00", "S1u10", "_dn2o", "A2s00", "A1s20", "_dO", "A2t10", "_gm", "A2t00", "S1x20", "A1x10", "_ab0", "_gma",
    "_ab1", "S1m00", "A1x30", "A2s10", "A3t10", "A1u00", "_ab2", "A2x10", "A1u10", "S1m10", "A1x20", "_ab3", "_gj0",
    "A3t00", "S1x00", "A3s00", "A1m00", "S1j20", "S1j00", "S1j10", "A2u00", "_ab4", "_ab5", "A2u10", "_ab6", "A3x10",
    "A3u00", "A2s30", "A1x00", "S1j30", "A1m10", "A2m00", "A1j20", "A3s10", "_ab7", "A1j00", "_gj1", "S1k00",
    "A2x00", "S1k10", "A1j30", "_dn1s", "A2m10", "A3u10", "A2j20", "A4s10", "A3x00", "A2j00", "A1j10", "_dn1o",
    "_vz", "A2j30", "A1k00", "A2s20", "A1k10", "A4t00", "A2x30", "A3m00", "A4u00", "A4x10", "A2x20", "A4t10",
    "A2j10", "A4u10", "A4s00", "A4x00", "F_t00", "A3m10", "A3s30", "A2k00", "_vx", "A3j30", "A3j10", "A2k10",
    "A3x20", "A3j20", "A3s20", "A3j00", "A3k00", "A4m00", "A3x30", "A4m10", "A4s30", "_vy", "A4x20", "A4j20",
    "F_u00", "A4x30", "F_m00", "A3k10", "A4s20", "A4j00", "F_x00", "F_s00", "A4j30", "A4j10", "F_j00", "A4k00",
    "_vp", "A4k10", "F_k00", "_end",
]

LAST = (((1,), (1,)), ((), ()))
FIRST = (((0,), (0,)), ((), ()))

def packing(lengths, row_count):
    image_ends = jnp.cumsum(lengths)
    row_ids = jnp.arange(row_count, dtype=jnp.int32)
    segment = jnp.sum((image_ends[None, :] <= row_ids[:, None]).astype(jnp.int32), axis=1)
    live_rows = (row_ids < image_ends[-1]).astype(jnp.float32)
    return (segment, live_rows)


def row_distance(segment, distances):
    slots = jnp.arange(distances.shape[-1], dtype=jnp.int32)
    onehot = (segment[:, None] == slots[None, :]).astype(jnp.float32)
    return jnp.sum(onehot * distances[None, :].astype(jnp.float32), axis=1)


def positions(patch_index, ground_rows, model_width):
    quarter = model_width // 4
    frequency = 1.0 / 10000.0 ** (jnp.arange(quarter, dtype=jnp.float32) / quarter)
    factor = ground_rows / 10.0
    across_rows = ((patch_index // 14).astype(jnp.float32) * factor)[..., None] * frequency
    along_rows = ((patch_index % 14).astype(jnp.float32) * factor)[..., None] * frequency
    return jnp.concatenate(
        [jnp.sin(across_rows), jnp.cos(across_rows), jnp.sin(along_rows), jnp.cos(along_rows)],
        axis=-1,
    )


def norm_forward(hidden, scaling, offset):
    center = hidden - jnp.mean(hidden, axis=-1, keepdims=True)
    inverse = lax.rsqrt(jnp.mean(center * center, axis=-1, keepdims=True) + 1e-06)
    scaled = center * inverse
    return (scaled * scaling.astype(jnp.float32) + offset.astype(jnp.float32), scaled, inverse)


def norm_backward(incoming, scaled, inverse, scaling):
    grad_scaled = incoming * scaling.astype(jnp.float32)
    centered_grad = grad_scaled - jnp.mean(grad_scaled, axis=-1, keepdims=True)
    centered_grad = centered_grad - scaled * jnp.mean(grad_scaled * scaled, axis=-1, keepdims=True)
    return (centered_grad * inverse, jnp.sum(incoming * scaled, axis=0), jnp.sum(incoming, axis=0))


def gelu_slope(hidden_pre):
    normal_cdf = 0.5 * (1.0 + jax.scipy.special.erf(hidden_pre * 0.7071067811865476))
    density = jnp.exp(-0.5 * hidden_pre * hidden_pre) * 0.3989422804014327
    return normal_cdf + hidden_pre * density


def general_layer(
    tokens,
    kept_patch,
    image_lengths,
    ground_distance,
    cotangent,
    norm_one_gain,
    norm_one_bias,
    joint_weight,
    joint_bias,
    merge_weight,
    merge_bias,
    norm_two_gain,
    norm_two_bias,
    expand_weight,
    expand_bias,
    shrink_weight,
    shrink_bias,
):
    full = (
        lax.all_gather(norm_one_gain, "dp", axis=0, tiled=True),
        lax.all_gather(norm_one_bias, "dp", axis=0, tiled=True),
        lax.all_gather(joint_weight, "dp", axis=0, tiled=True),
        lax.all_gather(joint_bias, "dp", axis=0, tiled=True),
        lax.all_gather(merge_weight, "dp", axis=0, tiled=True),
        lax.all_gather(merge_bias, "dp", axis=0, tiled=True),
        lax.all_gather(norm_two_gain, "dp", axis=0, tiled=True),
        lax.all_gather(norm_two_bias, "dp", axis=0, tiled=True),
        lax.all_gather(expand_weight, "dp", axis=0, tiled=True),
        lax.all_gather(expand_bias, "dp", axis=0, tiled=True),
        lax.all_gather(shrink_weight, "dp", axis=0, tiled=True),
        lax.all_gather(shrink_bias, "dp", axis=0, tiled=True),
    )
    row_count = tokens.shape[0]
    model_width = tokens.shape[1]
    head_count = model_width // HD
    segment, live_rows = packing(image_lengths[0], row_count)
    ground_rows = row_distance(segment, ground_distance[0])
    residual_in = tokens.astype(jnp.float32) + positions(kept_patch, ground_rows, model_width)
    first, scaled_one, inverse_one = norm_forward(residual_in, full[0], full[1])
    first_low = first.astype(jnp.bfloat16)
    projected = (
        jnp.dot(first_low, full[2], preferred_element_type=jnp.float32)
        + full[3].astype(jnp.float32)
    ).astype(jnp.bfloat16)
    queries = projected[:, :model_width].reshape(row_count, head_count, HD)
    key_rows = projected[:, model_width : 2 * model_width].reshape(row_count, head_count, HD)
    value_rows = projected[:, 2 * model_width :].reshape(row_count, head_count, HD)
    score_scale = HD ** (-0.5)

    def block_scores():
        raw_scores = (
            jnp.einsum("qhd,khd->hqk", queries, key_rows, preferred_element_type=jnp.float32)
            * score_scale
        )
        same_image = segment[:, None] == segment[None, :]
        return jnp.where(same_image[None], raw_scores, -1000000000.0)

    scores = block_scores()
    highest_score = jnp.max(scores, axis=-1, keepdims=True)
    exponent = jnp.exp(scores - highest_score)
    row_total = jnp.sum(exponent, axis=-1, keepdims=True)
    softmax_rows = exponent / row_total
    log_totals = highest_score + jnp.log(row_total)
    attended_parts = jnp.einsum(
        "hqk,khd->qhd",
        softmax_rows.astype(jnp.bfloat16),
        value_rows,
        preferred_element_type=jnp.float32,
    )
    attended = attended_parts.reshape(row_count, model_width).astype(jnp.bfloat16)
    branch = jnp.dot(attended, full[4], preferred_element_type=jnp.float32) + full[5].astype(
        jnp.float32
    )
    middle = residual_in + branch
    second, scaled_two, inverse_two = norm_forward(middle, full[6], full[7])
    second_low = second.astype(jnp.bfloat16)
    hidden_pre = jnp.dot(second_low, full[8], preferred_element_type=jnp.float32) + full[9].astype(
        jnp.float32
    )
    active_low = jax.nn.gelu(hidden_pre, approximate=False).astype(jnp.bfloat16)
    branch_mlp = jnp.dot(active_low, full[10], preferred_element_type=jnp.float32) + full[
        11
    ].astype(jnp.float32)
    output = ((middle + branch_mlp) * live_rows[:, None]).astype(jnp.bfloat16)
    again = (
        lax.all_gather(norm_one_gain, "dp", axis=0, tiled=True),
        lax.all_gather(norm_one_bias, "dp", axis=0, tiled=True),
        lax.all_gather(joint_weight, "dp", axis=0, tiled=True),
        lax.all_gather(joint_bias, "dp", axis=0, tiled=True),
        lax.all_gather(merge_weight, "dp", axis=0, tiled=True),
        lax.all_gather(merge_bias, "dp", axis=0, tiled=True),
        lax.all_gather(norm_two_gain, "dp", axis=0, tiled=True),
        lax.all_gather(norm_two_bias, "dp", axis=0, tiled=True),
        lax.all_gather(expand_weight, "dp", axis=0, tiled=True),
        lax.all_gather(expand_bias, "dp", axis=0, tiled=True),
        lax.all_gather(shrink_weight, "dp", axis=0, tiled=True),
        lax.all_gather(shrink_bias, "dp", axis=0, tiled=True),
    )
    incoming = cotangent.astype(jnp.float32) * live_rows[:, None]
    incoming_low = incoming.astype(jnp.bfloat16)
    grad_shrink = jnp.einsum(
        "tf,to->fo", active_low, incoming_low, preferred_element_type=jnp.float32
    )
    grad_shrink_offset = jnp.sum(incoming_low.astype(jnp.float32), axis=0)
    grad_active = jnp.einsum(
        "to,fo->tf", incoming_low, again[10], preferred_element_type=jnp.float32
    )
    grad_hidden = (grad_active * gelu_slope(hidden_pre)).astype(jnp.bfloat16)
    grad_expand = jnp.einsum(
        "td,tf->df", second_low, grad_hidden, preferred_element_type=jnp.float32
    )
    grad_expand_offset = jnp.sum(grad_hidden.astype(jnp.float32), axis=0)
    grad_second = jnp.einsum("tf,df->td", grad_hidden, again[8], preferred_element_type=jnp.float32)
    back_two, grad_gain_two, grad_bias_two = norm_backward(
        grad_second, scaled_two, inverse_two, again[6]
    )
    grad_middle = incoming + back_two
    middle_low = grad_middle.astype(jnp.bfloat16)
    grad_merge = jnp.einsum("ti,to->io", attended, middle_low, preferred_element_type=jnp.float32)
    grad_merge_offset = jnp.sum(middle_low.astype(jnp.float32), axis=0)
    grad_attended = jnp.einsum(
        "to,io->ti", middle_low, again[4], preferred_element_type=jnp.float32
    )
    grad_attended = grad_attended.astype(jnp.bfloat16).reshape(row_count, head_count, HD)
    softmax_rows = jnp.exp(block_scores() - log_totals)
    grad_softmax = jnp.einsum(
        "qhd,khd->hqk", grad_attended, value_rows, preferred_element_type=jnp.float32
    )
    row_delta = jnp.sum(softmax_rows * grad_softmax, axis=-1, keepdims=True)
    grad_scores = (softmax_rows * (grad_softmax - row_delta) * score_scale).astype(jnp.bfloat16)
    grad_query_parts = jnp.einsum(
        "hqk,khd->qhd", grad_scores, key_rows, preferred_element_type=jnp.float32
    )
    grad_keys = jnp.einsum("hqk,qhd->khd", grad_scores, queries, preferred_element_type=jnp.float32)
    grad_values = jnp.einsum(
        "hqk,qhd->khd",
        softmax_rows.astype(jnp.bfloat16),
        grad_attended,
        preferred_element_type=jnp.float32,
    )
    grad_joint = jnp.concatenate(
        [
            grad_query_parts.reshape(row_count, model_width),
            grad_keys.reshape(row_count, model_width),
            grad_values.reshape(row_count, model_width),
        ],
        axis=1,
    ).astype(jnp.bfloat16)
    grad_joint_matrix = jnp.einsum(
        "td,tj->dj", first_low, grad_joint, preferred_element_type=jnp.float32
    )
    grad_joint_offset = jnp.sum(grad_joint.astype(jnp.float32), axis=0)
    grad_first = jnp.einsum("tj,dj->td", grad_joint, again[2], preferred_element_type=jnp.float32)
    back_one, grad_gain_one, grad_bias_one = norm_backward(
        grad_first, scaled_one, inverse_one, again[0]
    )
    grad_tokens = grad_middle + back_one
    grads_full = (
        grad_gain_one,
        grad_bias_one,
        grad_joint_matrix,
        grad_joint_offset,
        grad_merge,
        grad_merge_offset,
        grad_gain_two,
        grad_bias_two,
        grad_expand,
        grad_expand_offset,
        grad_shrink,
        grad_shrink_offset,
    )
    shares = (
        lax.psum_scatter(grads_full[0], "dp", scatter_dimension=0, tiled=True),
        lax.psum_scatter(grads_full[1], "dp", scatter_dimension=0, tiled=True),
        lax.psum_scatter(grads_full[2], "dp", scatter_dimension=0, tiled=True),
        lax.psum_scatter(grads_full[3], "dp", scatter_dimension=0, tiled=True),
        lax.psum_scatter(grads_full[4], "dp", scatter_dimension=0, tiled=True),
        lax.psum_scatter(grads_full[5], "dp", scatter_dimension=0, tiled=True),
        lax.psum_scatter(grads_full[6], "dp", scatter_dimension=0, tiled=True),
        lax.psum_scatter(grads_full[7], "dp", scatter_dimension=0, tiled=True),
        lax.psum_scatter(grads_full[8], "dp", scatter_dimension=0, tiled=True),
        lax.psum_scatter(grads_full[9], "dp", scatter_dimension=0, tiled=True),
        lax.psum_scatter(grads_full[10], "dp", scatter_dimension=0, tiled=True),
        lax.psum_scatter(grads_full[11], "dp", scatter_dimension=0, tiled=True),
    )
    totals = (
        lax.psum(shares[0].astype(jnp.bfloat16), "rep").astype(jnp.float32),
        lax.psum(shares[1].astype(jnp.bfloat16), "rep").astype(jnp.float32),
        lax.psum(shares[2].astype(jnp.bfloat16), "rep").astype(jnp.float32),
        lax.psum(shares[3].astype(jnp.bfloat16), "rep").astype(jnp.float32),
        lax.psum(shares[4].astype(jnp.bfloat16), "rep").astype(jnp.float32),
        lax.psum(shares[5].astype(jnp.bfloat16), "rep").astype(jnp.float32),
        lax.psum(shares[6].astype(jnp.bfloat16), "rep").astype(jnp.float32),
        lax.psum(shares[7].astype(jnp.bfloat16), "rep").astype(jnp.float32),
        lax.psum(shares[8].astype(jnp.bfloat16), "rep").astype(jnp.float32),
        lax.psum(shares[9].astype(jnp.bfloat16), "rep").astype(jnp.float32),
        lax.psum(shares[10].astype(jnp.bfloat16), "rep").astype(jnp.float32),
        lax.psum(shares[11].astype(jnp.bfloat16), "rep").astype(jnp.float32),
    )
    return (
        output,
        grad_tokens,
        totals[0],
        totals[1],
        totals[2],
        totals[3],
        totals[4],
        totals[5],
        totals[6],
        totals[7],
        totals[8],
        totals[9],
        totals[10],
        totals[11],
    )


def contract(a, b, dims):
    return lax.dot_general(a, b, dims, preferred_element_type=F32)


def matmul(a, b):
    return jnp.dot(a, b, preferred_element_type=F32)


def span(start, size):
    return pl.ds(start if isinstance(start, int) else pl.multiple_of(start, size), size)


def layer_kernel(dims, cuts, schedule, names, *args):
    r = dict(zip(names, args, strict=True))
    Z, Y, X = dims
    vec, cot = r["vec"], r["cot"]
    H0, N1, QKV, OA, H1, N2, G, DU, EB = (r[k] for k in ("H0", "N1", "QKV", "OA", "H1", "N2", "G", "DU", "EB"))
    SEG, L, V, XS, XR, OUTB, DA, VG, COL = (r[k] for k in ("SEG", "L", "V", "XS", "XR", "OUTB", "DA", "VG", "COL"))
    VGR, GM = r["VGR"], r["GM"]
    OS = XS.at[:, 0 : XS.shape[1] // 2]
    R, D = H0.shape
    half_heads = D // HD // 2
    HW = half_heads * HD
    FC = DU.shape[1]
    me = lax.axis_index("dp")
    c = lax.axis_index("rep")
    o = 1 - c
    x = lax.rem(me, X)
    y = lax.rem(me // X, Y)
    z = me // (X * Y)
    own = span(c * R, R)
    sib = span(o * R, R)

    def at(zz, yy, xx):
        return (zz * (Y * X) + yy * X + xx, c)

    def zplus(d):
        return lax.rem(z + d, Z)

    to_x, to_y, to_o = at(z, y, 1 - x), at(z, 1 - y, x), (me, o)
    to_z = [None] + [at(zplus(d), y, x) for d in range(1, Z)]
    up, down = to_z[1], to_z[Z - 1]
    z1, z2 = z + 1 - 2 * lax.rem(z, 2), lax.rem(z + 2, Z)
    to_z1, to_z2 = at(z1, y, x), at(z2, y, x)

    def remote(src, dst, ssem, rsem, to):
        return pltpu.make_async_remote_copy(
            src_ref=src, dst_ref=dst, send_sem=ssem, recv_sem=rsem, device_id=to, device_id_type=MESH
        )

    barrier = pltpu.get_barrier_semaphore()
    for to in to_z[1:] + [to_x, to_y, to_o]:
        pl.semaphore_signal(barrier, inc=1, device_id=to, device_id_type=MESH)
    pl.semaphore_wait(barrier, Z - 1 + 3)

    pair_sems = iter(range(r["ps"].shape[0]))

    def to_pair(src, dst):
        k = next(pair_sems)
        cp = remote(src, dst, r["ps"].at[k], r["pr"].at[k], to_o)
        cp.start()
        return cp

    TAB = r["TAB"]

    def tab_send(ref, slot, to, src=None):
        cp = remote(src if src is not None else ref, ref, r["vs"].at[slot], r["vr"].at[slot], to)
        cp.start()
        return cp

    vcps = [tab_send(TAB.at[z, y, x], d - 1, to_z[d], vec) for d in range(1, Z)]
    TAB[z, y, x] = vec[...]

    W = {k: r["W" + k] for k in "jmxs"}
    blk = W["s"].shape[3]
    lnum = {k: i for i, k in enumerate("jmxset")}

    def qcols(hp, i):
        return pl.ds((3 * hp + i) * 2 * HD, 2 * HD)

    def local_copy(k, src, dst):
        pltpu.make_async_copy(src, dst, r["ls"].at[lnum[k]]).start()

    def local_wait(k, ref):
        pltpu.make_async_copy(ref, ref, r["ls"].at[lnum[k]]).wait()

    for i in range(3):
        for hp in range(half_heads // 2):
            src = r["wj"].at[:, span(i * D + c * HW + hp * 2 * HD, 2 * HD)]
            local_copy("j", src, W["j"].at[z, y, x, :, qcols(hp, i)])
    local_copy("m", r["wm"].at[:, span(c * HW, HW)], W["m"].at[z, y, x, :, span(c * HW, HW)])
    for i in range(FC // blk):
        local_copy("x", r["wx"].at[:, span(2 * blk * i + blk * c, blk)], W["x"].at[z, y, x, :, pl.ds(i * blk, blk)])
    local_copy("s", r["ws"].at[span(c * blk, blk), :], W["s"].at[z, y, x])
    local_copy("t", r["tok"], OUTB)
    local_copy("e", cot, EB.at[own, :])
    own_ref = {
        "j": W["j"].at[z, y, x],
        "m": W["m"].at[z, y, x, :, span(c * HW, HW)],
        "x": W["x"].at[z, y, x],
        "s": W["s"].at[z, y, x],
    }

    order = "jmxs"
    num = {(k, p): 4 * i + p for i, k in enumerate(order) for p in range(4)}

    def gcols(k, p):
        start, size = cuts["gather"][k][p]
        return span(c * HW + start, size) if k == "m" else pl.ds(start, size)

    def block(k, p, zz, yy=slice(None), xx=slice(None)):
        return W[k].at[zz, yy, xx, :, gcols(k, p)]

    def send(ref, ssem, rsem, to):
        remote(ref, ref, ssem, rsem, to).start()

    def line_block(k, p, zz):
        return block(k, p, zz, y, x) if p < 2 else block(k, p, zz)

    def line_send(k, p, zz, way):
        n = num[k, p]
        send(line_block(k, p, zz), r["az"].at[n, way, zz], r["bz"].at[n, zz], (up, down)[way])

    def line_start(k, p):
        @pl.when(z < Z - 1)
        def _():
            line_send(k, p, z, 0)

        @pl.when(z > 0)
        def _():
            line_send(k, p, z, 1)

    def line_arrive(k, p, t, then):
        def take(zz, way, more):
            n = num[k, p]
            ref = line_block(k, p, zz)
            remote(ref, ref, r["az"].at[n, way, zz], r["bz"].at[n, zz], up).wait_recv()

            @pl.when(more)
            def _():
                line_send(k, p, zz, way)

            then(zz)

        @pl.when(z >= t)
        def _():
            take(z - t, 0, z < Z - 1)

        @pl.when(z + t < Z)
        def _():
            take(z + t, 1, z > 0)

    def spread(k, p, zz):
        n = num[k, p]
        a, b = (to_y, to_x) if p == 0 else (to_x, to_y)
        ref = block(k, p, zz, y, x)
        send(ref, r["a2"].at[n], r["b2"].at[n, zz], a)
        send(ref, r["a3"].at[n], r["b3"].at[n], b)

    def second(k, p, zz):
        n = num[k, p]
        a, b = (to_y, to_x) if p == 0 else (to_x, to_y)
        ref = block(k, p, zz, 1 - y, x) if p == 0 else block(k, p, zz, y, 1 - x)
        remote(ref, ref, r["a2"].at[n], r["b2"].at[n, zz], a).wait_recv()
        send(ref, r["a3"].at[n], r["b3"].at[n], b)

    def g_z0(k, p, t):
        line_start(k, p)

    def g_fz(k, p, t):
        if t == 0:
            spread(k, p, z)
        else:
            line_arrive(k, p, t, functools.partial(spread, k, p))

    def g_f2(k, p, t):
        if t == 0:
            second(k, p, z)
        else:

            @pl.when(z >= t)
            def _():
                second(k, p, z - t)

            @pl.when(z + t < Z)
            def _():
                second(k, p, z + t)

    def g_p0(k, p, t):
        n = num[k, p]
        a, b = (to_x, to_y) if p == 2 else (to_y, to_x)
        send(block(k, p, z, y, x), r["a2"].at[n], r["b2"].at[n, 0], a)
        send(block(k, p, z, y, x), r["a3"].at[n], r["b3"].at[n], b)

    def g_p1(k, p, t):
        n = num[k, p]
        a, b = (to_x, to_y) if p == 2 else (to_y, to_x)
        ref = block(k, p, z, y, 1 - x) if p == 2 else block(k, p, z, 1 - y, x)
        remote(ref, ref, r["a2"].at[n], r["b2"].at[n, 0], a).wait_recv()
        send(ref, r["a3"].at[n], r["b3"].at[n], b)

    def g_p2(k, p, t):
        n = num[k, p]
        ref = block(k, p, z, 1 - y) if p == 2 else block(k, p, z, slice(None), 1 - x)
        remote(ref, ref, r["a3"].at[n], r["b3"].at[n], to_y if p == 2 else to_x).wait_recv()
        line_start(k, p)

    def g_pz(k, p, t):
        line_arrive(k, p, t, lambda zz: None)

    def gather_wait(k):
        for p in (0, 1):
            n = num[k, p]
            ref = block(k, p, slice(None), slice(None), 0) if p == 0 else block(k, p, slice(None), 0)
            remote(ref, ref, r["a3"].at[n], r["b3"].at[n], to_x if p == 0 else to_y).wait_recv()

    def gather_done(k):
        for p in range(4):
            if not cuts["gather"][k][p][1]:
                continue
            n = num[k, p]
            every = slice(None)
            if p < 2:
                done = [(block(k, p, every, 0, 0), "a2"), (block(k, p, every, every, 0), "a3")]
            else:
                done = [(block(k, p, 0, 0, 0), "a2"), (block(k, p, 0, 0), "a3")]
            for ref, s in done:
                remote(ref, ref, r[s].at[n], r["b3"].at[n], to_x).wait_send()
            for t in range(Z):
                ref = line_block(k, p, t)

                @pl.when((z < Z - 1) & (t <= z))
                def _():
                    remote(ref, ref, r["az"].at[n, 0, t], r["bz"].at[n, t], up).wait_send()

                @pl.when((z > 0) & (t >= z))
                def _():
                    remote(ref, ref, r["az"].at[n, 1, t], r["bz"].at[n, t], down).wait_send()

    GS, GX, GJ = r["GS"], W["s"], W["x"]
    grad = {"s": GS, "t": GS, "x": GX, "u": GX, "m": GM, "j": GJ, "k": GJ}
    gorder = "stxumjk"
    gnum = {(k, p): 4 * i + p for i, k in enumerate(gorder) for p in range(4)}
    outs = {k: r["o" + v] for k, v in zip(gorder, "ssxxmjj", strict=True)}

    def gslice(k, p):
        row, rows, begin, size = cuts["reduce"][k][p]
        return pl.ds(row, rows), span(c * HW + begin, size) if k == "m" else pl.ds(begin, size)

    def add_into(ref, idx, other):
        ref[idx] = (ref[idx].astype(F32) + other[...].astype(F32)).astype(BF16)

    def part(k, p, zz, yy, xx):
        return grad[k].at[(zz, yy, xx, *gslice(k, p))]

    every = slice(None)

    def part(k, p, zz, yy=every, xx=every):
        return grad[k].at[(zz, yy, xx, *gslice(k, p))]

    def buf(name, k, p):
        return r["%s%s%d" % (name, k, p)]

    def line_first(k, p, name, at_):
        n = gnum[k, p]
        return [
            remote(
                part(k, p, zz, *at_), buf(name, k, p).at[i], r["c" + name[1]].at[n, i], r["d" + name[1]].at[n, i], to_z1
            )
            for i, zz in enumerate((z1, lax.rem(z1 + 2, Z)))
        ]

    def line_last(k, p, name, at_):
        n = gnum[k, p]
        return [
            remote(
                part(k, p, z2, *at_), buf(name, k, p).at[2], r["c" + name[1]].at[n, 2], r["d" + name[1]].at[n, 2], to_z2
            )
        ]

    def s1(k, p):
        n = gnum[k, p]
        if p > 1:
            return line_first(k, p, "R1", ())
        src = part(k, p, every, every, 1 - x) if p == 0 else part(k, p, every, 1 - y)
        return [remote(src, buf("R1", k, p), r["c1"].at[n, 0], r["d1"].at[n, 0], to_x if p == 0 else to_y)]

    def s1b(k, p):
        return line_last(k, p, "R1", ()) if p > 1 else []

    def s2(k, p):
        n = gnum[k, p]
        src, to = {
            0: lambda: (part(k, p, every, 1 - y, x), to_y),
            1: lambda: (part(k, p, every, y, 1 - x), to_x),
            2: lambda: (part(k, p, z, 1 - y), to_y),
            3: lambda: (part(k, p, z, every, 1 - x), to_x),
        }[p]()
        return [remote(src, buf("R2", k, p), r["c2"].at[n], r["d2"].at[n], to)]

    def s3(k, p):
        n = gnum[k, p]
        if p < 2:
            return line_first(k, p, "R3", (y, x))
        src, to = (part(k, p, z, y, 1 - x), to_x) if p == 2 else (part(k, p, z, 1 - y, x), to_y)
        return [remote(src, buf("R3", k, p).at[0], r["c3"].at[n, 0], r["d3"].at[n, 0], to)]

    def s3b(k, p):
        return line_last(k, p, "R3", (y, x)) if p < 2 else []

    def start(copies):
        for cp in copies:
            cp.start()

    def arrived(copies):
        for cp in copies:
            cp.wait_recv()

    def r_S1(k, p, t):
        start(s1(k, p))

    def goes_and_stays(k, p):
        for q in (1, 0):
            yield q, [(1 - y if q else y, i) if p == 2 else (i, 1 - x if q else x) for i in range(2)]

    def r_A1(k, p, t):
        arrived(s1(k, p))
        R1, sl = buf("R1", k, p), gslice(k, p)
        if p > 1:
            for i in range(Y * X):
                add_into(grad[k], (z2, i // X, i % X, *sl), R1.at[1, i // X, i % X])
            start(s1b(k, p))
            return
        for q in (1, 0):
            yy = y if q == 0 else 1 - y
            xx = x if q == 0 else 1 - x

            def one(i, _):
                if p == 0:
                    add_into(grad[k], (i, yy, x, *sl), R1.at[i, yy])
                else:
                    add_into(grad[k], (i, y, xx, *sl), R1.at[i, xx])
                return 0

            lax.fori_loop(0, Z, one, 0)
            if q == 1:
                start(s2(k, p))

    def r_A2(k, p, t):
        sl = gslice(k, p)
        if p < 2:
            arrived(s2(k, p))
            R2 = buf("R2", k, p)
            for zz in (z1, lax.rem(z1 + 2, Z)):
                add_into(grad[k], (zz, y, x, *sl), R2.at[zz])
            start(s3(k, p))
            for zz in (z, z2):
                add_into(grad[k], (zz, y, x, *sl), R2.at[zz])
            return
        arrived(s1b(k, p))
        R1 = buf("R1", k, p)
        for q, places in goes_and_stays(k, p):
            for yy, xx in places:
                idx = (z, yy, xx, *sl)
                tot = grad[k][idx].astype(F32) + R1[0, yy, xx].astype(F32) + R1[2, yy, xx].astype(F32)
                grad[k][idx] = tot.astype(BF16)
            if q == 1:
                start(s2(k, p))

    def r_A3(k, p, t):
        sl = gslice(k, p)
        if p < 2:
            arrived(s3(k, p))
            add_into(grad[k], (z2, y, x, *sl), buf("R3", k, p).at[1])
            start(s3b(k, p))
            return
        arrived(s2(k, p))
        R2 = buf("R2", k, p)
        for q in (1, 0):
            yy, xx = (y, 1 - x if q else x) if p == 2 else (1 - y if q else y, x)
            add_into(grad[k], (z, yy, xx, *sl), R2.at[xx if p == 2 else yy])
            if q == 1:
                start(s3(k, p))

    def r_A4(k, p, t):
        arrived(s3b(k, p) if p < 2 else s3(k, p))
        R3 = buf("R3", k, p)
        idx = (z, y, x, *gslice(k, p))
        tot = grad[k][idx].astype(F32) + R3[0].astype(F32)
        if p < 2:
            tot = tot + R3[2].astype(F32)
        grad[k][idx] = tot.astype(BF16)

    fin_copies = []

    def r_F(k, p, t):
        i = gorder.index(k)
        row, rows, begin, size = cuts["reduce"][k][0]
        size = sum(q[3] for q in cuts["reduce"][k])
        rs = pl.ds(row, rows)
        total = grad[k].at[z, y, x, rs, span(c * HW + begin, size) if k == "m" else pl.ds(begin, size)]
        dst = outs[k].at[c, rs, pl.ds(begin, size)]
        a = pltpu.make_async_copy(total, dst, r["fl"].at[i])
        b = remote(total, dst, r["fs"].at[i], r["fr"].at[i], to_o)
        a.start()
        b.start()
        fin_copies.extend([a, b])

    TQ, TR = 256, 256
    FT = Y * X * blk // 2
    DT = Y * X * W["j"].shape[3]
    copies = {}
    lane = lax.broadcasted_iota(jnp.int32, (1, 2 * HD), 1) // HD

    def normed(h):
        center = h - jnp.mean(h, axis=-1, keepdims=True)
        inverse = lax.rsqrt(jnp.mean(center * center, axis=-1, keepdims=True) + 1e-06)
        return center * inverse, inverse

    def c_rows():
        slots = r["len"].shape[1]
        sub = lax.broadcasted_iota(jnp.int32, (slots, slots), 0)
        lan = lax.broadcasted_iota(jnp.int32, (slots, slots), 1)
        lens, dist = r["len"][...].astype(F32), r["dist"][...].astype(F32)
        ends = jnp.sum(jnp.where(lan <= sub, lens, 0.0), axis=1, keepdims=True)
        dist = jnp.sum(jnp.where(lan == sub, dist, 0.0), axis=1, keepdims=True)
        places = lax.broadcasted_iota(jnp.int32, (slots, R), 1).astype(F32)
        segment = jnp.sum(jnp.where(ends <= places, 1.0, 0.0), axis=0, keepdims=True)
        slot = lax.broadcasted_iota(jnp.int32, (slots, R), 0).astype(F32)
        ground = jnp.sum(jnp.where(slot == segment, dist, 0.0), axis=0, keepdims=True)
        alive = jnp.where(segment < slots, 1.0, 0.0)
        factor = ground / 10.0
        patch = r["patch"][...].astype(F32)
        patch = jnp.concatenate([patch[i : i + 1] for i in range(R // 128)], axis=1)
        down_ = jnp.floor((patch + 0.5) * (1.0 / 14.0))
        along = patch - 14.0 * down_
        zero = jnp.zeros_like(factor)
        rows = jnp.concatenate([segment, alive, down_ * factor, along * factor, zero, zero, zero, zero], axis=0)
        SEG[c] = rows
        COL[...] = jnp.transpose(rows)
        copies["seg"] = to_pair(SEG.at[c], SEG.at[c])

    def c_v1():
        for cp in vcps:
            cp.wait()
        copies["vy"] = tab_send(TAB.at[:, y, x], Z - 1, to_y)

    def c_v2():
        copies["vy"].wait()
        copies["vx"] = tab_send(TAB.at[:, :, x], Z, to_x)

    def c_v3():
        copies["vx"].wait()
        VG[...] = jnp.zeros_like(VG)
        count = Z * Y * X
        n, nj = D // count, 3 * D // count
        flat = TAB[...].reshape(count * 8, 128)
        table = flat.astype(BF16)
        for s_ in range(count):
            f = s_ * blk
            piece = TAB[s_ // (Y * X), s_ // X % Y, s_ % X, pl.ds(c, 1), :]
            V[8 + f // D : 9 + f // D, f % D : f % D + blk] = piece
        wide = 4 * 128
        key = lax.broadcasted_iota(jnp.int32, (128, wide), 0).astype(F32)
        row = lax.broadcasted_iota(jnp.int32, (count * 8, wide), 0).astype(F32)
        column = lax.broadcasted_iota(jnp.int32, (1, wide), 1).astype(F32)

        def spread_out(shard, entry, first):
            spot = entry + first
            line = jnp.floor((spot + 0.5) * (1.0 / 128))
            pick = jnp.where(key == spot - 128.0 * line, 1.0, 0.0).astype(BF16)
            tiled = matmul(table, pick)
            return jnp.sum(jnp.where(row == 8.0 * shard + line, tiled, 0.0), axis=0, keepdims=True)

        for a in range(0, D, wide):
            shard = jnp.floor((column + (a + 0.5)) * (1.0 / n))
            for i in range(6):
                V[i : i + 1, a : a + wide] = spread_out(shard, column + a - n * shard, 2 * blk + nj + i * n)
        for a in range(0, 3 * HW, wide):
            tile = jnp.floor((column + (a + 0.5)) * (1.0 / 128))
            hp = jnp.floor((tile + 0.5) * (1.0 / 3))
            which = tile - 3.0 * hp
            of = which * D + c.astype(F32) * HW + hp * 128.0 + (column + a - 128.0 * tile)
            shard = jnp.floor((of + 0.5) * (1.0 / nj))
            V[6 + a // D : 7 + a // D, a % D : a % D + wide] = spread_out(shard, of - nj * shard, 2 * blk)

    def c_h0():
        local_wait("t", OUTB)
        local_wait("e", EB.at[own, :])

        def rows128(i, _):
            rr, gr = span(i * 128, 128), span(c * R + i * 128, 128)
            EB[gr, :] = (EB[gr, :].astype(F32) * COL[rr, 1:2]).astype(BF16)
            Q = D // 4
            for j in (0, 1):
                angle = COL[rr, 2 + j : 3 + j] * r["freq"][...]
                at_ = 2 * j * Q
                H0[rr, at_ : at_ + Q] = OUTB[rr, at_ : at_ + Q].astype(F32) + jnp.sin(angle)
                at_ += Q
                H0[rr, at_ : at_ + Q] = OUTB[rr, at_ : at_ + Q].astype(F32) + jnp.cos(angle)
            return 0

        lax.fori_loop(0, R // 128, rows128, 0)
        copies["eb"] = to_pair(EB.at[own, :], EB.at[own, :])

    def c_ln1():
        def norm_one(i, _):
            rr, gr = span(i * 128, 128), span(c * R + i * 128, 128)
            scaled, _i = normed(H0[rr, :])
            N1[gr, :] = (scaled * V[0:1, :] + V[1:2, :]).astype(BF16)
            VG[5:6, :] += jnp.sum(EB[gr, :].astype(F32), axis=0, keepdims=True)
            return 0

        lax.fori_loop(0, R // 128, norm_one, 0)
        copies["n1"] = to_pair(N1.at[own, :], N1.at[own, :])

    def c_qkv(t):
        if t == 0:
            copies["seg"].wait()
            copies["n1"].wait()
            copies["eb"].wait()
            gather_wait("j")
        w = W["j"][:, :, :, :, t * TQ : (t + 1) * TQ].reshape(D, TQ)
        f = t * TQ
        b = V[6 + f // D : 7 + f // D, f % D : f % D + TQ]
        QKV[:, f : f + TQ] = (matmul(N1[...], w) + b).astype(BF16)

    def same_image(g):
        return jnp.transpose(SEG[g])[:, 0:1] == SEG[g, 0:1, :]

    def attend(g, hp):
        rr = span(g * R, R)
        q, k, v = (QKV[rr, qcols(hp, i)] for i in range(3))
        same = same_image(g)
        res = []
        for i in (0, 1):
            qi = jnp.where(lane == i, q.astype(F32) * HD**-0.5, 0.0).astype(BF16)
            s = jnp.where(same, contract(k, qi, LAST), NEVER)
            top = jnp.max(s, axis=0, keepdims=True)
            e = jnp.exp(s - top)
            tot = jnp.sum(e, axis=0, keepdims=True)
            L[g * half_heads + 2 * hp + i] = top + jnp.log(tot)
            pb = (e * (1.0 / tot)).astype(BF16)
            res.append(contract(v, pb, FIRST)[i * HD : (i + 1) * HD])
        return jnp.transpose(jnp.concatenate(res, axis=0)).astype(BF16)

    pairs = half_heads // 2

    def c_at(i):
        if i < pairs:
            OS[:, 2 * HD * i : 2 * HD * (i + 1)] = attend(o, i)
            if i == pairs - 1:
                copies["o"] = to_pair(OS, OA.at[:, span(c * HW, HW)])
        else:
            OA[:, span(c * HW + 2 * HD * (i - pairs), 2 * HD)] = attend(c, i - pairs)

    def c_wm():
        gather_wait("m")
        half = W["m"].at[:, :, :, :, span(c * HW, HW)]
        copies["wm"] = to_pair(half, half)

    def c_mrg():
        copies["o"].wait()
        copies["wm"].wait()
        for t in range(R // TR):
            rr = pl.ds(t * TR, TR)
            h1 = H0[rr, :] + matmul(OA[rr, :], W["m"][...].reshape(D, D)) + V[2:3, :]
            H1[rr, :] = h1
            scaled, _i = normed(h1)
            N2[span(c * R + t * TR, TR), :] = (scaled * V[3:4, :] + V[4:5, :]).astype(BF16)
        copies["n2"] = to_pair(N2.at[own, :], N2.at[own, :])

    def c_ge(t):
        if t == 0:
            copies["n2"].wait()
            gather_wait("x")
        cc = slice(t * TQ, (t + 1) * TQ)
        f = t * TQ
        b = V[8 + f // D : 9 + f // D, f % D : f % D + TQ]
        for h in range(2):
            rr = slice(h * R, (h + 1) * R)
            u = matmul(N2[rr, :], W["x"][:, :, :, :, cc].reshape(D, TQ)) + b
            cdf = 0.5 * (1.0 + lax.erf(u * 0.7071067811865476))
            G[rr, cc] = (u * cdf).astype(BF16)
            DU[rr, cc] = (cdf + u * (jnp.exp(-0.5 * u * u) * 0.3989422804014327)).astype(BF16)

    def c_gs(i):
        for t in (2 * i, 2 * i + 1):
            g = contract(G[:, t * FT : (t + 1) * FT], EB[...], FIRST)
            GS[t // Y, t % Y] = g.astype(BF16).reshape(X, blk, D)

    def c_du(i):
        if i == 0:
            gather_wait("s")
        for t in (2 * i, 2 * i + 1):
            cc = slice(t * FT, (t + 1) * FT)
            w = W["s"][t // Y, t % Y].reshape(FT, D)
            row, col = 8 + t * FT // D, t * FT % D
            for h in range(2):
                rr = slice(h * R, (h + 1) * R)
                du = (contract(EB[rr, :], w, LAST) * DU[rr, cc].astype(F32)).astype(BF16)
                DU[rr, cc] = du
                VG[row : row + 1, col : col + FT] += jnp.sum(du.astype(F32), axis=0, keepdims=True)

    def c_h2s():
        for t in range(D // TQ):
            cc = slice(t * TQ, (t + 1) * TQ)
            XS[:, cc] = matmul(G[sib, :], W["s"][:, :, :, :, cc].reshape(FC, TQ)).astype(BF16)
        copies["h2"] = to_pair(XS, OUTB)

    def c_h2o():
        copies["h2"].wait_recv()
        for t in range(D // TQ):
            cc = slice(t * TQ, (t + 1) * TQ)
            own_part = matmul(G[own, :], W["s"][:, :, :, :, cc].reshape(FC, TQ))
            OUTB[:, cc] = (
                (H1[:, cc] + own_part + OUTB[:, cc].astype(F32) + V[5:6, cc]) * COL[:, 1:2]
            ).astype(BF16)
        copies["out"] = pltpu.make_async_copy(OUTB, r["out"], r["fl"].at[len(gorder)])
        copies["out"].start()
        gather_done("s")

    def back_part(left, wk, n, name, dst):
        for t in range(Z):
            w = wk[t][:, :, :, 0:n].reshape(DT, n)
            dst[:, t * DT : (t + 1) * DT] = contract(left[sib, 0:n], w, LAST).astype(BF16)
        copies[name] = to_pair(dst, XR)

    def c_dn2s():
        back_part(DU, W["x"], FC, "dn2", DA)

    def c_gx(i):
        h, half = W["j"].shape[3], FC // 2
        for t in range(Z):
            g = contract(N2[:, t * DT : (t + 1) * DT], DU[:, i * half : (i + 1) * half], FIRST)
            GX[t, :, :, i * h : (i + 1) * h, :] = g.astype(BF16).reshape(Y, X, h, half)

    def norm_back(dy, scaled, inverse, gain, vg):
        ds_ = dy * gain
        VG[vg : vg + 1, :] += jnp.sum(dy * scaled, axis=0, keepdims=True)
        VG[vg + 1 : vg + 2, :] += jnp.sum(dy, axis=0, keepdims=True)
        cen = ds_ - jnp.mean(ds_, axis=-1, keepdims=True)
        cen = cen - scaled * jnp.mean(ds_ * scaled, axis=-1, keepdims=True)
        return cen * inverse

    def c_dn2o():
        copies["dn2"].wait()
        for t in range(R // TR):
            rr, gr = pl.ds(t * TR, TR), span(c * R + t * TR, TR)
            dy = contract(DU[gr, :], W["x"][...].reshape(D, FC), LAST) + XR[rr, :].astype(F32)
            scaled, inverse = normed(H1[rr, :])
            dh = EB[gr, :].astype(F32) + norm_back(dy, scaled, inverse, V[3:4, :], 3)
            H1[rr, :] = dh
            DA[rr, :] = dh.astype(BF16)
            VG[2:3, :] += jnp.sum(DA[rr, :].astype(F32), axis=0, keepdims=True)
        gather_done("x")

    def c_dO():
        copies["h2"].wait_send()
        cw = X * W["m"].shape[3]
        for t, base in enumerate((o, c)):
            for u in range(HW // cw):
                w = W["m"][base * (Z // 2) + u // Y, u % Y].reshape(cw, D)
                res = contract(DA[...], w, LAST).astype(BF16)
                if t == 0:
                    OS[:, u * cw : (u + 1) * cw] = res
                else:
                    G[own, 3 * HW + u * cw : 3 * HW + (u + 1) * cw] = res
            if t == 0:
                copies["do"] = to_pair(OS, G.at[own, pl.ds(3 * HW, HW)])
        gather_done("m")

    def c_gm():
        for t in range(Z):
            g = contract(OA[:, t * DT : (t + 1) * DT], DA[...], FIRST)
            GM[t] = g.astype(BF16).reshape(Y, X, W["m"].shape[3], D)
        copies["gm"] = to_pair(GM.at[:, :, :, :, span(o * HW, HW)], r["GMR"])

    def c_gma():
        copies["gm"].wait()

        def add_pair(i, _):
            for j in range(Y * X):
                idx = (i, j // X, j % X, slice(None), span(c * HW, HW))
                add_into(GM, idx, r["GMR"].at[i, j // X, j % X])
            return 0

        lax.fori_loop(0, Z, add_pair, 0)

    def attend_back(g, hp):
        rr = span(g * R, R)
        qc, kc, vc = (qcols(hp, i) for i in range(3))
        q, k, v = QKV[rr, qc], QKV[rr, kc], QKV[rr, vc]
        do = G[rr, 3 * HW + hp * 2 * HD : 3 * HW + (hp + 1) * 2 * HD]
        same = same_image(g)
        dq, dk, dv = [], [], []
        for i in (0, 1):
            qi = jnp.where(lane == i, q.astype(F32) * HD**-0.5, 0.0).astype(BF16)
            di = jnp.where(lane == i, do.astype(F32), 0.0).astype(BF16)
            s = jnp.where(same, contract(k, qi, LAST), NEVER)
            pr = jnp.exp(s - L[g * half_heads + 2 * hp + i])
            dp = contract(v, di, LAST)
            delta = jnp.sum(pr * dp, axis=0, keepdims=True)
            dsb = (pr * (dp - delta) * HD**-0.5).astype(BF16)
            dq.append(contract(k, dsb, FIRST)[i * HD : (i + 1) * HD])
            dk.append(matmul(dsb, q))
            dv.append(matmul(pr.astype(BF16), do))
        G[rr, qc] = jnp.transpose(jnp.concatenate(dq, axis=0)).astype(BF16)
        G[rr, kc] = jnp.where(lane == 0, dk[0], dk[1]).astype(BF16)
        G[rr, vc] = jnp.where(lane == 0, dv[0], dv[1]).astype(BF16)

    def c_ab(i):
        few = pairs // 2
        if i == few:
            copies["do"].wait()
        attend_back(c if i % pairs < few else o, i // pairs * few + i % few)

    def c_gj(i):
        half = 3 * HW // 2
        for t in range(Z):
            g = contract(N1[:, t * DT : (t + 1) * DT], G[:, i * half : (i + 1) * half], FIRST)
            GJ[t, :, :, :, i * half : (i + 1) * half] = g.astype(BF16).reshape(Y, X, W["j"].shape[3], half)

    def c_dn1s():
        back_part(G, W["j"], 3 * HW, "dn1", XS)
        for t in range(3):
            row, col = 6 + t * HW // D, t * HW % D
            VG[row : row + 1, col : col + HW] += jnp.sum(
                G[:, t * HW : (t + 1) * HW].astype(F32), axis=0, keepdims=True
            )

    def c_dn1o():
        copies["dn1"].wait()
        for t in range(R // TR):
            rr, gr = pl.ds(t * TR, TR), span(c * R + t * TR, TR)
            dy = contract(G[gr, 0 : 3 * HW], W["j"][...].reshape(D, 3 * HW), LAST) + XR[rr, :].astype(F32)
            scaled, inverse = normed(H0[rr, :])
            H1[rr, :] = H1[rr, :] + norm_back(dy, scaled, inverse, V[0:1, :], 0)
        copies["gt"] = pltpu.make_async_copy(H1, r["gt"], r["fl"].at[len(gorder) + 1])
        copies["gt"].start()
        gather_done("j")

    def vg_send(slot, to):
        cp = remote(VG, VGR.at[slot], r["gs"].at[slot], r["gr"].at[slot], to)
        cp.start()
        return cp

    def vg_add(slots):
        acc = VG[...]
        for i in slots:
            acc = acc + VGR[i]
        VG[...] = acc

    def c_vz():
        copies["gz"] = [vg_send(d - 1, to_z[d]) for d in range(1, Z)]

    def c_vx():
        for cp in copies["gz"]:
            cp.wait()
        vg_add(range(Z - 1))
        copies["gx"] = vg_send(Z - 1, to_x)

    def c_vy():
        copies["gx"].wait()
        vg_add([Z - 1])
        copies["gy"] = vg_send(Z, to_y)

    def c_vp():
        copies["gy"].wait()
        vg_add([Z])
        copies["ov"] = pltpu.make_async_copy(VG, r["ov"].at[c], r["fl"].at[len(gorder) + 2])
        copies["ov"].start()
        copies["ovr"] = to_pair(VG, r["ov"].at[c])

    def c_end():
        for k in gorder:
            for p in range(4):
                if cuts["reduce"][k][p][3]:
                    for cp in s1(k, p) + s1b(k, p) + s2(k, p) + s3(k, p) + s3b(k, p):
                        cp.wait_send()
        for cp in fin_copies + [copies[n] for n in ("out", "gt", "ov", "ovr")]:
            cp.wait()

    steps = locals()
    landed = set()
    for word in schedule:
        if word[0] == "_":
            name = word[1:].rstrip("0123456789")
            if name in ("v", "h", "ln"):
                name = word[1:]
            arg = word[1 + len(name) :]
            steps["c_" + name](*([int(arg)] if arg else []))
            continue
        op, k, p, t = word[:2], word[2], int(word[3]), int(word[4])
        if op in ("z0", "p0", "fz") and t == 0 and k not in landed:
            landed.add(k)
            local_wait(k, own_ref[k])
        steps[("r_" if op[0] in "SAF" else "g_") + op.rstrip("_")](k, p, t)


def finish_kernel(dims, names, *args):
    r = dict(zip(names, args, strict=True))
    N = dims[0] * dims[1] * dims[2]
    taken = [
        pltpu.make_async_copy(r[n], r["v_" + n], r["sem"].at[i])
        for i, n in enumerate(("out", "gt", "oj", "om", "ox", "os", "ov"))
    ]
    for cp in taken:
        cp.start()
    big = [
        pltpu.make_async_copy(r["v_" + n], r["f_" + n], r["sem"].at[7 + i]) for i, n in enumerate(("out", "gt"))
    ]
    for i, cp in enumerate(taken):
        cp.wait()
        if i < 2:
            big[i].start()
    r.update({n: r["v_" + n] for n in ("oj", "om", "ox", "os", "ov")})
    rj, D = r["f_m"].shape
    HW, P2 = D // 2, 2 * HD
    blk = r["os"].shape[1]
    half = r["ox"].shape[2]
    for core in (0, 1):
        for hp in range(HW // P2):
            for i in range(3):
                to, of = i * D + core * HW + hp * P2, (3 * hp + i) * P2
                r["f_j"][:, to : to + P2] = r["oj"][core, :, of : of + P2].astype(F32)
        r["f_m"][:, core * HW : (core + 1) * HW] = r["om"][core].astype(F32)
        for i in range(2 * half // blk):
            row, col = i * blk // half * rj, i * blk % half
            to = (2 * i + core) * blk
            r["f_x"][:, to : to + blk] = r["ox"][core, row : row + rj, col : col + blk].astype(F32)
        r["f_s"][core * blk : (core + 1) * blk, :] = r["os"][core].astype(F32)
    me = lax.axis_index("dp")
    ov = r["ov"]
    both = ov[0, 0:8, :] + ov[1, 0:8, :]

    def mine(row, n):
        return pltpu.roll(row, (N - me) * n, 1)[:, :n]

    for i, name in enumerate(("g1", "b1", "mb", "g2", "b2", "sb")):
        r["f_" + name][...] = mine(jnp.broadcast_to(both[i : i + 1], (8, D)), D // N)[0:1]
    at_ = [((3 * hp + i) * P2, core) for i in range(3) for core in (0, 1) for hp in range(HW // P2)]
    row = jnp.concatenate([ov[core, 6 + a // D : 7 + a // D, a % D : a % D + P2] for a, core in at_], axis=1)
    r["f_jb"][...] = mine(jnp.broadcast_to(row, (8, 3 * D)), 3 * D // N)[0:1]
    for core in (0, 1):
        row = jnp.concatenate([ov[core, 8 + i : 9 + i, :] for i in range(2 * half // D)], axis=1)
        r["f_xb"][:, core * blk : (core + 1) * blk] = mine(jnp.broadcast_to(row, (8, 2 * half)), blk)[0:1]
    for cp in big:
        cp.wait()


def tiled_cuts(width, side):
    main = width // 2 - side * 128
    sizes = (main, main, side * 128, side * 128)
    starts = (0, main, 2 * main, 2 * main + side * 128)
    return list(zip(starts, sizes, strict=True))


def paths(rows, row, begin, width, side):
    return [(row, rows, begin + q, size) for q, size in tiled_cuts(width, side)]


def fused_layer(dims, *args):
    (
        tokens,
        kept_patch,
        image_lengths,
        ground_distance,
        cotangent,
        norm_one_gain,
        norm_one_bias,
        joint_weight,
        joint_bias,
        merge_weight,
        merge_bias,
        norm_two_gain,
        norm_two_bias,
        expand_weight,
        expand_bias,
        shrink_weight,
        shrink_bias,
    ) = args
    Z, Y, X = dims
    N = Z * Y * X
    R, D = tokens.shape
    FF = expand_weight.shape[1]
    HW, FC, blk = D // 2, FF // 2, shrink_weight.shape[0] // 2
    rj = joint_weight.shape[0]
    pieces = [expand_bias, joint_bias, norm_one_gain, norm_one_bias, merge_bias, norm_two_gain, norm_two_bias, shrink_bias]
    vec, begin = jnp.zeros((8 * 128,), F32), 0
    for v in pieces:
        vec = vec + jnp.pad(v.astype(F32), (begin, 8 * 128 - begin - v.shape[0]))
        begin += v.shape[0]
    vec = vec.reshape(8, 128)
    quarter = D // 4
    freq = 1.0 / np.float32(10000.0) ** (np.arange(quarter, dtype=np.float32) / np.float32(quarter))

    cuts = {
        "gather": {
            "j": tiled_cuts(3 * HW, 1),
            "m": tiled_cuts(HW, 0),
            "x": tiled_cuts(FC, 1),
            "s": tiled_cuts(D, 1),
        },
        "reduce": {
            "s": paths(blk, 0, 0, D // 2, SIDE["s"]),
            "t": paths(blk, 0, D // 2, D // 2, SIDE["t"]),
            "x": paths(rj, 0, 0, FC // 2, SIDE["x"]),
            "u": paths(rj, rj, 0, FC // 2, SIDE["u"]),
            "m": paths(rj, 0, 0, HW, 0),
            "j": paths(rj, 0, 0, 3 * HW // 2, SIDE["j"]),
            "k": paths(rj, 0, 3 * HW // 2, 3 * HW // 2, SIDE["k"]),
        },
    }

    vm, hbm = pl.BlockSpec(memory_space=pltpu.VMEM), pl.BlockSpec(memory_space=pl.ANY)
    ins = [("patch", kept_patch.reshape(R // 128, 128), vm), ("len", image_lengths, vm), ("dist", ground_distance, vm)]
    ins += [("freq", jnp.asarray(freq[None, :], F32), vm), ("vec", vec, vm), ("tok", tokens, hbm), ("cot", cotangent, hbm)]
    ins += [("wj", joint_weight, hbm), ("wm", merge_weight, hbm), ("wx", expand_weight, hbm), ("ws", shrink_weight, hbm)]
    S = jax.ShapeDtypeStruct
    outs = [
        ("out", S((R, D), BF16), hbm),
        ("gt", S((R, D), F32), hbm),
        ("oj", S((2, rj, 3 * HW), BF16), hbm),
        ("om", S((2, rj, HW), BF16), hbm),
        ("ox", S((2, 2 * rj, FC // 2), BF16), hbm),
        ("os", S((2, blk, D), BF16), hbm),
        ("ov", S((2, 16, D), F32), hbm),
    ]
    V = pltpu.VMEM
    dma = pltpu.SemaphoreType.DMA
    scratch = [
        ("Wj", V((Z, Y, X, rj, 3 * HW), BF16)),
        ("Wm", V((Z, Y, X, rj, D), BF16)),
        ("Wx", V((Z, Y, X, rj, FC), BF16)),
        ("Ws", V((Z, Y, X, blk, D), BF16)),
        ("GS", V((Z, Y, X, blk, D), BF16)),
        ("GM", V((Z, Y, X, rj, D), BF16)),
        ("GMR", V((Z, Y, X, rj, HW), BF16)),
        ("H0", V((R, D), F32)),
        ("N1", V((2 * R, D), BF16)),
        ("QKV", V((2 * R, 3 * HW), BF16)),
        ("OA", V((R, D), BF16)),
        ("H1", V((R, D), F32)),
        ("N2", V((2 * R, D), BF16)),
        ("G", V((2 * R, FC), BF16)),
        ("DU", V((2 * R, FC), BF16)),
        ("EB", V((2 * R, D), BF16)),
        ("SEG", V((2, 8, R), F32)),
        ("COL", V((R, 8), F32)),
        ("L", V((D // HD, 1, R), F32)),
        ("V", V((16, D), F32)),
        ("TAB", V((Z, Y, X, 8, 128), F32)),
        ("VG", V((16, D), F32)),
        ("VGR", V((Z + 1, 16, D), F32)),
        ("XS", V((R, D), BF16)),
        ("XR", V((R, D), BF16)),
        ("OUTB", V((R, D), BF16)),
        ("DA", V((R, D), BF16)),
    ]
    for k, four in cuts["reduce"].items():
        for p, (_, n, _, w) in enumerate(four):
            if w:
                first = (Z, 2) if p < 2 else (3, Y, X)
                second, third = ((Z,), (3,)) if p < 2 else ((2,), (1,))
                for name, lead in (("R1", first), ("R2", second), ("R3", third)):
                    scratch.append(("%s%s%d" % (name, k, p), V((*lead, n, w), BF16)))
    for name, shape in (
        ("ps", (12,)),
        ("pr", (12,)),
        ("vs", (Z + 1,)),
        ("vr", (Z + 1,)),
        ("gs", (Z + 1,)),
        ("gr", (Z + 1,)),
        ("ls", (6,)),
        ("az", (16, 2, Z)),
        ("bz", (16, Z)),
        ("a2", (16,)),
        ("b2", (16, Z)),
        ("a3", (16,)),
        ("b3", (16,)),
        ("c1", (28, 3)),
        ("d1", (28, 3)),
        ("c2", (28,)),
        ("d2", (28,)),
        ("c3", (28, 3)),
        ("d3", (28, 3)),
        ("fl", (10,)),
        ("fs", (7,)),
        ("fr", (7,)),
    ):
        scratch.append((name, dma(shape)))
    names = [n for n, *_ in ins + outs + scratch]
    res = pl.pallas_call(
        functools.partial(layer_kernel, dims, cuts, SCHEDULE, names),
        out_shape=[s for _, s, _ in outs],
        in_specs=[s for _, _, s in ins],
        out_specs=[s for _, _, s in outs],
        scratch_shapes=[s for _, s in scratch],
        compiler_params=pltpu.CompilerParams(
            collective_id=0, has_side_effects=True, vmem_limit_bytes=VMEM_BYTES
        ),
    )(*[a for _, a, _ in ins])

    far = pl.BlockSpec(memory_space=pltpu.HBM)
    given = [(n, a, far) for (n, _, _), a in zip(outs, res, strict=True)]
    made = [("f_out", S((R, D), BF16), far), ("f_gt", S((R, D), F32), far)]
    made += [("f_" + n, S((1, D // N), F32), vm) for n in ("g1", "b1", "mb", "g2", "b2", "sb")]
    made += [("f_jb", S((1, 3 * D // N), F32), vm), ("f_xb", S((1, FF // N), F32), vm)]
    made += [("f_j", S((rj, 3 * D), F32), vm), ("f_m", S((rj, D), F32), vm)]
    made += [("f_x", S((rj, FF), F32), vm), ("f_s", S((2 * blk, D), F32), vm)]
    last = pl.pallas_call(
        functools.partial(finish_kernel, dims, [n for n, *_ in given + made] + ["v_" + n for n, *_ in outs] + ["sem"]),
        out_shape=[s for _, s, _ in made],
        in_specs=[s for _, _, s in given],
        out_specs=[s for _, _, s in made],
        scratch_shapes=[V(s.shape, s.dtype) for _, s, _ in outs] + [dma((9,))],
        compiler_params=pltpu.CompilerParams(vmem_limit_bytes=VMEM_BYTES),
    )(*[a for _, a, _ in given])
    f = {n[2:]: a for (n, *_), a in zip(made, last, strict=True)}
    g1, b1, mb, g2, b2, sb, g_jb, g_xb = (f[n].reshape(-1) for n in ("g1", "b1", "mb", "g2", "b2", "sb", "jb", "xb"))
    return f["out"], f["gt"], g1, b1, f["j"], g_jb, f["m"], mb, g2, b2, f["x"], g_xb, f["s"], sb


def layout(mesh, joint_rows, shrink_rows):
    n = mesh.shape["dp"]
    if mesh.shape["rep"] != 2 or n != 16 or joint_rows % 16 or shrink_rows % 256:
        return None
    return (n // 4, 2, 2)


def on_device(mesh, *args):
    dims = layout(mesh, args[7].shape[0], args[15].shape[0])
    if dims is None:
        return general_layer(*args)
    return fused_layer(dims, *args)


def solution(mesh):
    rows, rows2 = P(("dp", "rep")), P(("dp", "rep"), None)
    vector, matrix = P("dp"), P("dp", None)
    return jax.shard_map(
        functools.partial(on_device, mesh),
        mesh=mesh,
        in_specs=(
            rows2,
            rows,
            rows2,
            rows2,
            rows2,
            vector,
            vector,
            matrix,
            vector,
            matrix,
            vector,
            vector,
            vector,
            matrix,
            vector,
            matrix,
            vector,
        ),
        out_specs=(
            rows2,
            rows2,
            vector,
            vector,
            matrix,
            vector,
            matrix,
            vector,
            vector,
            vector,
            matrix,
            vector,
            matrix,
            vector,
        ),
        check_vma=False,
    )
```

```python
import functools

import jax
import jax.numpy as jnp
import numpy as np
from jax import lax
from jax.experimental import pallas as pl
from jax.experimental.pallas import tpu as pltpu
from jax.sharding import PartitionSpec as P

HD = 64
MESH = pl.DeviceIdType.MESH
F32 = jnp.float32
BF16 = jnp.bfloat16
NEVER = -1000000000.0
VMEM_BYTES = 127 * 2**19
GATHER = {"j": (5, 5, 1, 1), "m": (2, 2, 0, 0), "x": (6, 6, 2, 2), "s": (3, 3, 1, 1)}
REDUCE = {
    "s": (1, 1, 1, 1),
    "t": (1, 1, 1, 1),
    "x": (3, 3, 1, 1),
    "u": (4, 4, 0, 0),
    "m": (2, 2, 0, 0),
    "j": (3, 3, 0, 0),
    "k": (2, 1, 0, 0),
    "l": (1, 2, 0, 0),
}
SCHEDULE = [
    "fzj10", "p0j30", "p0j20", "z0m10", "z0m00", "z0j00", "fzs10", "z0x10", "p0s30", "p1j30", "fzx10", "fzm11",
    "z0j10", "p2j30", "fzm01", "z0x00", "fzj01", "p0x20", "p1j20", "fzm10", "p1s30", "_rows", "fzm12", "_v1",
    "p0s20", "fzj00", "p0x30", "fzj11", "fzm13", "fzm02", "f2j10", "fzx01", "fzj12", "fzj13", "p1s20", "fzj02",
    "fzm00", "fzj03", "p2j20", "z0s10", "f2j13", "p1x20", "pzj31", "p1x30", "f2j01", "z0s00", "fzm03", "_v2",
    "fzx02", "f2m02", "_h0", "pzj21", "f2m10", "fzx03", "f2m13", "f2j11", "fzx11", "p2s20", "f2j02", "pzj22",
    "p2x30", "f2j12", "f2j03", "f2j00", "fzx12", "f2x03", "fzx00", "pzj32", "_v3", "f2m11", "fzs01", "_ln1", "pzx31",
    "f2m00", "p2x20", "f2m12", "pzj33", "pzj23", "fzx13", "f2x10", "fzs02", "f2x11", "_qkv0", "_qkv1", "p2s30",
    "_qkv2", "_qkv3", "_qkv4", "pzx32", "f2m01", "fzs11", "f2m03", "f2x01", "pzx21", "_qkv5", "_at0", "fzs03",
    "f2x12", "_at1", "_at2", "f2x00", "pzs31", "_at3", "_at4", "_at5", "_at6", "_at7", "f2x02", "f2x13", "pzx33",
    "fzs12", "_wm", "pzx22", "fzs00", "f2s03", "_mrg", "f2s11", "pzs32", "fzs13", "f2s01", "pzx23", "pzs21", "_ge0",
    "_ge1", "f2s12", "_ge2", "_ge3", "_ge4", "f2s00", "pzs33", "f2s10", "_ge5", "f2s02", "_ge6", "pzs22", "_ge7",
    "_gs0", "f2s13", "_gs1", "_gs2", "_gs3", "S1s00", "S1t20", "S1t00", "pzs23", "S1s20", "S1s30", "S1t30", "S1s10",
    "_du0", "S1t10", "_du1", "_du2", "_du3", "_h2s", "_dn2s", "A1s10", "A1s00", "A1t00", "A1t10", "_h2o", "_gx0",
    "S1x00", "S1x10", "A1s30", "A2s00", "_gx1", "S1x30", "S1x20", "_dn2o", "A1t20", "A2s10", "S1u10", "S1u00", "_dO",
    "_gm", "A1x10", "A2t10", "_ab0", "A1s20", "_gma", "A1x00", "A1x20", "S1m10", "_ab1", "A2t00", "_ab2", "_ab3",
    "A3s10", "A1u10", "_gj0", "A2x00", "A1x30", "S1j10", "S1j00", "A2x10", "_ab4", "_ab5", "A3t10", "A1t30", "A1m10",
    "_gj1", "_ab6", "A2u10", "A3x00", "A3t00", "A1u00", "A3x10", "_ab7", "A3s00", "S1k10", "A1j10", "_gj2", "_dn1s",
    "A2m10", "S1k00", "S1l10", "S1l00", "A3u10", "A2u00", "_dn1o", "A2j10", "A1k10", "_vz", "A4t00", "A4s00",
    "A1k00", "A1j00", "A3m10", "S1m00", "A2k10", "A3u00", "A4u10", "A2k00", "A1l10", "A3j10", "A1l00", "A2t20",
    "A2x30", "_vx", "A2j00", "A4x10", "A1m00", "A2s20", "A4s10", "A2t30", "A3k10", "A2l00", "A3k00", "A4j10",
    "A2s30", "A2l10", "A4m10", "A2x20", "A3j00", "A4t10", "A3t20", "A2m00", "A4u00", "_vy", "A3t30", "A3l00",
    "A4k00", "A3x30", "A3l10", "A3s20", "A4k10", "F_k00", "A3s30", "A4x00", "A3x20", "F_u00", "A3m00", "A4t30",
    "_vp", "A4t20", "A4j00", "A4s30", "A4x30", "A4s20", "A4x20", "F_x00", "F_j00", "A4l00", "F_s00", "A4l10",
    "F_l00", "F_t00", "A4m00", "F_m00", "_end",
]

LAST = (((1,), (1,)), ((), ()))
FIRST = (((0,), (0,)), ((), ()))

def packing(lengths, row_count):
    image_ends = jnp.cumsum(lengths)
    row_ids = jnp.arange(row_count, dtype=jnp.int32)
    segment = jnp.sum((image_ends[None, :] <= row_ids[:, None]).astype(jnp.int32), axis=1)
    live_rows = (row_ids < image_ends[-1]).astype(jnp.float32)
    return (segment, live_rows)


def row_distance(segment, distances):
    slots = jnp.arange(distances.shape[-1], dtype=jnp.int32)
    onehot = (segment[:, None] == slots[None, :]).astype(jnp.float32)
    return jnp.sum(onehot * distances[None, :].astype(jnp.float32), axis=1)


def positions(patch_index, ground_rows, model_width):
    quarter = model_width // 4
    frequency = 1.0 / 10000.0 ** (jnp.arange(quarter, dtype=jnp.float32) / quarter)
    factor = ground_rows / 10.0
    across_rows = ((patch_index // 14).astype(jnp.float32) * factor)[..., None] * frequency
    along_rows = ((patch_index % 14).astype(jnp.float32) * factor)[..., None] * frequency
    return jnp.concatenate(
        [jnp.sin(across_rows), jnp.cos(across_rows), jnp.sin(along_rows), jnp.cos(along_rows)],
        axis=-1,
    )


def norm_forward(hidden, scaling, offset):
    center = hidden - jnp.mean(hidden, axis=-1, keepdims=True)
    inverse = lax.rsqrt(jnp.mean(center * center, axis=-1, keepdims=True) + 1e-06)
    scaled = center * inverse
    return (scaled * scaling.astype(jnp.float32) + offset.astype(jnp.float32), scaled, inverse)


def norm_backward(incoming, scaled, inverse, scaling):
    grad_scaled = incoming * scaling.astype(jnp.float32)
    centered_grad = grad_scaled - jnp.mean(grad_scaled, axis=-1, keepdims=True)
    centered_grad = centered_grad - scaled * jnp.mean(grad_scaled * scaled, axis=-1, keepdims=True)
    return (centered_grad * inverse, jnp.sum(incoming * scaled, axis=0), jnp.sum(incoming, axis=0))


def gelu_slope(hidden_pre):
    normal_cdf = 0.5 * (1.0 + jax.scipy.special.erf(hidden_pre * 0.7071067811865476))
    density = jnp.exp(-0.5 * hidden_pre * hidden_pre) * 0.3989422804014327
    return normal_cdf + hidden_pre * density


def general_layer(
    tokens,
    kept_patch,
    image_lengths,
    ground_distance,
    cotangent,
    norm_one_gain,
    norm_one_bias,
    joint_weight,
    joint_bias,
    merge_weight,
    merge_bias,
    norm_two_gain,
    norm_two_bias,
    expand_weight,
    expand_bias,
    shrink_weight,
    shrink_bias,
):
    full = (
        lax.all_gather(norm_one_gain, "dp", axis=0, tiled=True),
        lax.all_gather(norm_one_bias, "dp", axis=0, tiled=True),
        lax.all_gather(joint_weight, "dp", axis=0, tiled=True),
        lax.all_gather(joint_bias, "dp", axis=0, tiled=True),
        lax.all_gather(merge_weight, "dp", axis=0, tiled=True),
        lax.all_gather(merge_bias, "dp", axis=0, tiled=True),
        lax.all_gather(norm_two_gain, "dp", axis=0, tiled=True),
        lax.all_gather(norm_two_bias, "dp", axis=0, tiled=True),
        lax.all_gather(expand_weight, "dp", axis=0, tiled=True),
        lax.all_gather(expand_bias, "dp", axis=0, tiled=True),
        lax.all_gather(shrink_weight, "dp", axis=0, tiled=True),
        lax.all_gather(shrink_bias, "dp", axis=0, tiled=True),
    )
    row_count = tokens.shape[0]
    model_width = tokens.shape[1]
    head_count = model_width // HD
    segment, live_rows = packing(image_lengths[0], row_count)
    ground_rows = row_distance(segment, ground_distance[0])
    residual_in = tokens.astype(jnp.float32) + positions(kept_patch, ground_rows, model_width)
    first, scaled_one, inverse_one = norm_forward(residual_in, full[0], full[1])
    first_low = first.astype(jnp.bfloat16)
    projected = (
        jnp.dot(first_low, full[2], preferred_element_type=jnp.float32)
        + full[3].astype(jnp.float32)
    ).astype(jnp.bfloat16)
    queries = projected[:, :model_width].reshape(row_count, head_count, HD)
    key_rows = projected[:, model_width : 2 * model_width].reshape(row_count, head_count, HD)
    value_rows = projected[:, 2 * model_width :].reshape(row_count, head_count, HD)
    score_scale = HD ** (-0.5)

    def block_scores():
        raw_scores = (
            jnp.einsum("qhd,khd->hqk", queries, key_rows, preferred_element_type=jnp.float32)
            * score_scale
        )
        same_image = segment[:, None] == segment[None, :]
        return jnp.where(same_image[None], raw_scores, -1000000000.0)

    scores = block_scores()
    highest_score = jnp.max(scores, axis=-1, keepdims=True)
    exponent = jnp.exp(scores - highest_score)
    row_total = jnp.sum(exponent, axis=-1, keepdims=True)
    softmax_rows = exponent / row_total
    log_totals = highest_score + jnp.log(row_total)
    attended_parts = jnp.einsum(
        "hqk,khd->qhd",
        softmax_rows.astype(jnp.bfloat16),
        value_rows,
        preferred_element_type=jnp.float32,
    )
    attended = attended_parts.reshape(row_count, model_width).astype(jnp.bfloat16)
    branch = jnp.dot(attended, full[4], preferred_element_type=jnp.float32) + full[5].astype(
        jnp.float32
    )
    middle = residual_in + branch
    second, scaled_two, inverse_two = norm_forward(middle, full[6], full[7])
    second_low = second.astype(jnp.bfloat16)
    hidden_pre = jnp.dot(second_low, full[8], preferred_element_type=jnp.float32) + full[9].astype(
        jnp.float32
    )
    active_low = jax.nn.gelu(hidden_pre, approximate=False).astype(jnp.bfloat16)
    branch_mlp = jnp.dot(active_low, full[10], preferred_element_type=jnp.float32) + full[
        11
    ].astype(jnp.float32)
    output = ((middle + branch_mlp) * live_rows[:, None]).astype(jnp.bfloat16)
    again = (
        lax.all_gather(norm_one_gain, "dp", axis=0, tiled=True),
        lax.all_gather(norm_one_bias, "dp", axis=0, tiled=True),
        lax.all_gather(joint_weight, "dp", axis=0, tiled=True),
        lax.all_gather(joint_bias, "dp", axis=0, tiled=True),
        lax.all_gather(merge_weight, "dp", axis=0, tiled=True),
        lax.all_gather(merge_bias, "dp", axis=0, tiled=True),
        lax.all_gather(norm_two_gain, "dp", axis=0, tiled=True),
        lax.all_gather(norm_two_bias, "dp", axis=0, tiled=True),
        lax.all_gather(expand_weight, "dp", axis=0, tiled=True),
        lax.all_gather(expand_bias, "dp", axis=0, tiled=True),
        lax.all_gather(shrink_weight, "dp", axis=0, tiled=True),
        lax.all_gather(shrink_bias, "dp", axis=0, tiled=True),
    )
    incoming = cotangent.astype(jnp.float32) * live_rows[:, None]
    incoming_low = incoming.astype(jnp.bfloat16)
    grad_shrink = jnp.einsum(
        "tf,to->fo", active_low, incoming_low, preferred_element_type=jnp.float32
    )
    grad_shrink_offset = jnp.sum(incoming_low.astype(jnp.float32), axis=0)
    grad_active = jnp.einsum(
        "to,fo->tf", incoming_low, again[10], preferred_element_type=jnp.float32
    )
    grad_hidden = (grad_active * gelu_slope(hidden_pre)).astype(jnp.bfloat16)
    grad_expand = jnp.einsum(
        "td,tf->df", second_low, grad_hidden, preferred_element_type=jnp.float32
    )
    grad_expand_offset = jnp.sum(grad_hidden.astype(jnp.float32), axis=0)
    grad_second = jnp.einsum("tf,df->td", grad_hidden, again[8], preferred_element_type=jnp.float32)
    back_two, grad_gain_two, grad_bias_two = norm_backward(
        grad_second, scaled_two, inverse_two, again[6]
    )
    grad_middle = incoming + back_two
    middle_low = grad_middle.astype(jnp.bfloat16)
    grad_merge = jnp.einsum("ti,to->io", attended, middle_low, preferred_element_type=jnp.float32)
    grad_merge_offset = jnp.sum(middle_low.astype(jnp.float32), axis=0)
    grad_attended = jnp.einsum(
        "to,io->ti", middle_low, again[4], preferred_element_type=jnp.float32
    )
    grad_attended = grad_attended.astype(jnp.bfloat16).reshape(row_count, head_count, HD)
    softmax_rows = jnp.exp(block_scores() - log_totals)
    grad_softmax = jnp.einsum(
        "qhd,khd->hqk", grad_attended, value_rows, preferred_element_type=jnp.float32
    )
    row_delta = jnp.sum(softmax_rows * grad_softmax, axis=-1, keepdims=True)
    grad_scores = (softmax_rows * (grad_softmax - row_delta) * score_scale).astype(jnp.bfloat16)
    grad_query_parts = jnp.einsum(
        "hqk,khd->qhd", grad_scores, key_rows, preferred_element_type=jnp.float32
    )
    grad_keys = jnp.einsum("hqk,qhd->khd", grad_scores, queries, preferred_element_type=jnp.float32)
    grad_values = jnp.einsum(
        "hqk,qhd->khd",
        softmax_rows.astype(jnp.bfloat16),
        grad_attended,
        preferred_element_type=jnp.float32,
    )
    grad_joint = jnp.concatenate(
        [
            grad_query_parts.reshape(row_count, model_width),
            grad_keys.reshape(row_count, model_width),
            grad_values.reshape(row_count, model_width),
        ],
        axis=1,
    ).astype(jnp.bfloat16)
    grad_joint_matrix = jnp.einsum(
        "td,tj->dj", first_low, grad_joint, preferred_element_type=jnp.float32
    )
    grad_joint_offset = jnp.sum(grad_joint.astype(jnp.float32), axis=0)
    grad_first = jnp.einsum("tj,dj->td", grad_joint, again[2], preferred_element_type=jnp.float32)
    back_one, grad_gain_one, grad_bias_one = norm_backward(
        grad_first, scaled_one, inverse_one, again[0]
    )
    grad_tokens = grad_middle + back_one
    grads_full = (
        grad_gain_one,
        grad_bias_one,
        grad_joint_matrix,
        grad_joint_offset,
        grad_merge,
        grad_merge_offset,
        grad_gain_two,
        grad_bias_two,
        grad_expand,
        grad_expand_offset,
        grad_shrink,
        grad_shrink_offset,
    )
    shares = (
        lax.psum_scatter(grads_full[0], "dp", scatter_dimension=0, tiled=True),
        lax.psum_scatter(grads_full[1], "dp", scatter_dimension=0, tiled=True),
        lax.psum_scatter(grads_full[2], "dp", scatter_dimension=0, tiled=True),
        lax.psum_scatter(grads_full[3], "dp", scatter_dimension=0, tiled=True),
        lax.psum_scatter(grads_full[4], "dp", scatter_dimension=0, tiled=True),
        lax.psum_scatter(grads_full[5], "dp", scatter_dimension=0, tiled=True),
        lax.psum_scatter(grads_full[6], "dp", scatter_dimension=0, tiled=True),
        lax.psum_scatter(grads_full[7], "dp", scatter_dimension=0, tiled=True),
        lax.psum_scatter(grads_full[8], "dp", scatter_dimension=0, tiled=True),
        lax.psum_scatter(grads_full[9], "dp", scatter_dimension=0, tiled=True),
        lax.psum_scatter(grads_full[10], "dp", scatter_dimension=0, tiled=True),
        lax.psum_scatter(grads_full[11], "dp", scatter_dimension=0, tiled=True),
    )
    totals = (
        lax.psum(shares[0].astype(jnp.bfloat16), "rep").astype(jnp.float32),
        lax.psum(shares[1].astype(jnp.bfloat16), "rep").astype(jnp.float32),
        lax.psum(shares[2].astype(jnp.bfloat16), "rep").astype(jnp.float32),
        lax.psum(shares[3].astype(jnp.bfloat16), "rep").astype(jnp.float32),
        lax.psum(shares[4].astype(jnp.bfloat16), "rep").astype(jnp.float32),
        lax.psum(shares[5].astype(jnp.bfloat16), "rep").astype(jnp.float32),
        lax.psum(shares[6].astype(jnp.bfloat16), "rep").astype(jnp.float32),
        lax.psum(shares[7].astype(jnp.bfloat16), "rep").astype(jnp.float32),
        lax.psum(shares[8].astype(jnp.bfloat16), "rep").astype(jnp.float32),
        lax.psum(shares[9].astype(jnp.bfloat16), "rep").astype(jnp.float32),
        lax.psum(shares[10].astype(jnp.bfloat16), "rep").astype(jnp.float32),
        lax.psum(shares[11].astype(jnp.bfloat16), "rep").astype(jnp.float32),
    )
    return (
        output,
        grad_tokens,
        totals[0],
        totals[1],
        totals[2],
        totals[3],
        totals[4],
        totals[5],
        totals[6],
        totals[7],
        totals[8],
        totals[9],
        totals[10],
        totals[11],
    )


def contract(a, b, dims):
    return lax.dot_general(a, b, dims, preferred_element_type=F32)


def matmul(a, b):
    return jnp.dot(a, b, preferred_element_type=F32)


def span(start, size):
    return pl.ds(start if isinstance(start, int) else pl.multiple_of(start, size), size)


def layer_kernel(dims, cuts, schedule, names, *args):
    r = dict(zip(names, args, strict=True))
    Z, Y, X = dims
    vec, cot = r["vec"], r["cot"]
    H0, N1, QKV, OA, H1, N2, G, DU, EB = (r[k] for k in ("H0", "N1", "QKV", "OA", "H1", "N2", "G", "DU", "EB"))
    SEG, L, V, XS, XR, OUTB, DA, VG, COL = (r[k] for k in ("SEG", "L", "V", "XS", "XR", "OUTB", "DA", "VG", "COL"))
    VGR, GM = r["VGR"], r["GM"]
    OS = XS.at[:, 0 : XS.shape[1] // 2]
    R, D = H0.shape
    half_heads = D // HD // 2
    HW = half_heads * HD
    FC = DU.shape[1]
    me = lax.axis_index("dp")
    c = lax.axis_index("rep")
    o = 1 - c
    x = lax.rem(me, X)
    y = lax.rem(me // X, Y)
    z = me // (X * Y)
    own = span(c * R, R)
    sib = span(o * R, R)

    def at(zz, yy, xx):
        return (zz * (Y * X) + yy * X + xx, c)

    def zplus(d):
        return lax.rem(z + d, Z)

    to_x, to_y, to_o = at(z, y, 1 - x), at(z, 1 - y, x), (me, o)
    to_z = [None] + [at(zplus(d), y, x) for d in range(1, Z)]
    up, down = to_z[1], to_z[Z - 1]
    z1, z2 = z + 1 - 2 * lax.rem(z, 2), lax.rem(z + 2, Z)
    to_z1, to_z2 = at(z1, y, x), at(z2, y, x)

    def remote(src, dst, ssem, rsem, to):
        return pltpu.make_async_remote_copy(
            src_ref=src, dst_ref=dst, send_sem=ssem, recv_sem=rsem, device_id=to, device_id_type=MESH
        )

    barrier = pltpu.get_barrier_semaphore()
    for to in to_z[1:] + [to_x, to_y, to_o]:
        pl.semaphore_signal(barrier, inc=1, device_id=to, device_id_type=MESH)
    W = {k: r["W" + k] for k in "jmxs"}
    blk = W["s"].shape[3]
    lnum = {k: i for i, k in enumerate("jmxset")}

    def qcols(hp, i):
        return pl.ds((3 * hp + i) * 2 * HD, 2 * HD)

    def local_copy(k, src, dst):
        pltpu.make_async_copy(src, dst, r["ls"].at[lnum[k]]).start()

    def local_wait(k, ref):
        pltpu.make_async_copy(ref, ref, r["ls"].at[lnum[k]]).wait()

    for i in range(3):
        for hp in range(half_heads // 2):
            src = r["wj"].at[:, span(i * D + c * HW + hp * 2 * HD, 2 * HD)]
            local_copy("j", src, W["j"].at[z, y, x, :, qcols(hp, i)])
    local_copy("m", r["wm"].at[:, span(c * HW, HW)], W["m"].at[z, y, x, :, span(c * HW, HW)])
    for i in range(FC // blk):
        local_copy("x", r["wx"].at[:, span(2 * blk * i + blk * c, blk)], W["x"].at[z, y, x, :, pl.ds(i * blk, blk)])
    local_copy("s", r["ws"].at[span(c * blk, blk), :], W["s"].at[z, y, x])
    local_copy("t", r["tok"], OUTB)
    local_copy("e", cot, EB.at[own, :])
    own_ref = {
        "j": W["j"].at[z, y, x],
        "m": W["m"].at[z, y, x, :, span(c * HW, HW)],
        "x": W["x"].at[z, y, x],
        "s": W["s"].at[z, y, x],
    }

    TAB = r["TAB"]
    TAB[z, y, x] = vec[...]
    pl.semaphore_wait(barrier, Z - 1 + 3)

    pair_sems = iter(range(r["ps"].shape[0]))

    def to_pair(src, dst):
        k = next(pair_sems)
        cp = remote(src, dst, r["ps"].at[k], r["pr"].at[k], to_o)
        cp.start()
        return cp

    def tab_send(ref, slot, to, src=None):
        cp = remote(src if src is not None else ref, ref, r["vs"].at[slot], r["vr"].at[slot], to)
        cp.start()
        return cp

    vcps = [tab_send(TAB.at[z, y, x], d - 1, to_z[d], vec) for d in range(1, Z)]
    order = "jmxs"
    num = {(k, p): 4 * i + p for i, k in enumerate(order) for p in range(4)}

    def gcols(k, p):
        start, size = cuts["gather"][k][p]
        return span(c * HW + start, size) if k == "m" else pl.ds(start, size)

    def block(k, p, zz, yy=slice(None), xx=slice(None)):
        return W[k].at[zz, yy, xx, :, gcols(k, p)]

    def send(ref, ssem, rsem, to):
        remote(ref, ref, ssem, rsem, to).start()

    def line_block(k, p, zz):
        return block(k, p, zz, y, x) if p < 2 else block(k, p, zz)

    def line_send(k, p, zz, way):
        n = num[k, p]
        send(line_block(k, p, zz), r["az"].at[n, way, zz], r["bz"].at[n, zz], (up, down)[way])

    def line_start(k, p):
        @pl.when(z < Z - 1)
        def _():
            line_send(k, p, z, 0)

        @pl.when(z > 0)
        def _():
            line_send(k, p, z, 1)

    def line_arrive(k, p, t, then):
        def take(zz, way, more):
            n = num[k, p]
            ref = line_block(k, p, zz)
            remote(ref, ref, r["az"].at[n, way, zz], r["bz"].at[n, zz], up).wait_recv()

            @pl.when(more)
            def _():
                line_send(k, p, zz, way)

            then(zz)

        @pl.when(z >= t)
        def _():
            take(z - t, 0, z < Z - 1)

        @pl.when(z + t < Z)
        def _():
            take(z + t, 1, z > 0)

    def spread(k, p, zz):
        n = num[k, p]
        a, b = (to_y, to_x) if p == 0 else (to_x, to_y)
        ref = block(k, p, zz, y, x)
        send(ref, r["a2"].at[n], r["b2"].at[n, zz], a)
        send(ref, r["a3"].at[n], r["b3"].at[n], b)

    def second(k, p, zz):
        n = num[k, p]
        a, b = (to_y, to_x) if p == 0 else (to_x, to_y)
        ref = block(k, p, zz, 1 - y, x) if p == 0 else block(k, p, zz, y, 1 - x)
        remote(ref, ref, r["a2"].at[n], r["b2"].at[n, zz], a).wait_recv()
        send(ref, r["a3"].at[n], r["b3"].at[n], b)

    def g_z0(k, p, t):
        line_start(k, p)

    def g_fz(k, p, t):
        if t == 0:
            spread(k, p, z)
        else:
            line_arrive(k, p, t, functools.partial(spread, k, p))

    def g_f2(k, p, t):
        if t == 0:
            second(k, p, z)
        else:

            @pl.when(z >= t)
            def _():
                second(k, p, z - t)

            @pl.when(z + t < Z)
            def _():
                second(k, p, z + t)

    def g_p0(k, p, t):
        n = num[k, p]
        a, b = (to_x, to_y) if p == 2 else (to_y, to_x)
        send(block(k, p, z, y, x), r["a2"].at[n], r["b2"].at[n, 0], a)
        send(block(k, p, z, y, x), r["a3"].at[n], r["b3"].at[n], b)

    def g_p1(k, p, t):
        n = num[k, p]
        a, b = (to_x, to_y) if p == 2 else (to_y, to_x)
        ref = block(k, p, z, y, 1 - x) if p == 2 else block(k, p, z, 1 - y, x)
        remote(ref, ref, r["a2"].at[n], r["b2"].at[n, 0], a).wait_recv()
        send(ref, r["a3"].at[n], r["b3"].at[n], b)

    def g_p2(k, p, t):
        n = num[k, p]
        ref = block(k, p, z, 1 - y) if p == 2 else block(k, p, z, slice(None), 1 - x)
        remote(ref, ref, r["a3"].at[n], r["b3"].at[n], to_y if p == 2 else to_x).wait_recv()
        line_start(k, p)

    def g_pz(k, p, t):
        line_arrive(k, p, t, lambda zz: None)

    def gather_wait(k):
        for p in (0, 1):
            n = num[k, p]
            ref = block(k, p, slice(None), slice(None), 0) if p == 0 else block(k, p, slice(None), 0)
            remote(ref, ref, r["a3"].at[n], r["b3"].at[n], to_x if p == 0 else to_y).wait_recv()

    def gather_done(k):
        for p in range(4):
            if not cuts["gather"][k][p][1]:
                continue
            n = num[k, p]
            every = slice(None)
            if p < 2:
                done = [(block(k, p, every, 0, 0), "a2"), (block(k, p, every, every, 0), "a3")]
            else:
                done = [(block(k, p, 0, 0, 0), "a2"), (block(k, p, 0, 0), "a3")]
            for ref, s in done:
                remote(ref, ref, r[s].at[n], r["b3"].at[n], to_x).wait_send()
            for t in range(Z):
                ref = line_block(k, p, t)

                @pl.when((z < Z - 1) & (t <= z))
                def _():
                    remote(ref, ref, r["az"].at[n, 0, t], r["bz"].at[n, t], up).wait_send()

                @pl.when((z > 0) & (t >= z))
                def _():
                    remote(ref, ref, r["az"].at[n, 1, t], r["bz"].at[n, t], down).wait_send()

    GS, GX, GJ = r["GS"], W["s"], W["x"]
    grad = {"s": GS, "t": GS, "x": GX, "u": GX, "m": GM, "j": GJ, "k": GJ, "l": GJ}
    gorder = "stxumjkl"
    gnum = {(k, p): 4 * i + p for i, k in enumerate(gorder) for p in range(4)}
    outs = {k: r["o" + v] for k, v in zip(gorder, "ssxxmjjj", strict=True)}

    def gslice(k, p):
        row, rows, begin, size = cuts["reduce"][k][p]
        return pl.ds(row, rows), span(c * HW + begin, size) if k == "m" else pl.ds(begin, size)

    def add_into(ref, idx, other):
        ref[idx] = (ref[idx].astype(F32) + other[...].astype(F32)).astype(BF16)

    def part(k, p, zz, yy, xx):
        return grad[k].at[(zz, yy, xx, *gslice(k, p))]

    every = slice(None)

    def part(k, p, zz, yy=every, xx=every):
        return grad[k].at[(zz, yy, xx, *gslice(k, p))]

    def buf(name, k, p):
        return r["%s%s%d" % (name, k, p)]

    def line_first(k, p, name, at_):
        n = gnum[k, p]
        return [
            remote(
                part(k, p, zz, *at_), buf(name, k, p).at[i], r["c" + name[1]].at[n, i], r["d" + name[1]].at[n, i], to_z1
            )
            for i, zz in enumerate((z1, lax.rem(z1 + 2, Z)))
        ]

    def line_last(k, p, name, at_):
        n = gnum[k, p]
        return [
            remote(
                part(k, p, z2, *at_), buf(name, k, p).at[2], r["c" + name[1]].at[n, 2], r["d" + name[1]].at[n, 2], to_z2
            )
        ]

    def s1(k, p):
        n = gnum[k, p]
        if p > 1:
            return line_first(k, p, "R1", ())
        src = part(k, p, every, every, 1 - x) if p == 0 else part(k, p, every, 1 - y)
        return [remote(src, buf("R1", k, p), r["c1"].at[n, 0], r["d1"].at[n, 0], to_x if p == 0 else to_y)]

    def s1b(k, p):
        return line_last(k, p, "R1", ()) if p > 1 else []

    def s2(k, p):
        n = gnum[k, p]
        src, to = {
            0: lambda: (part(k, p, every, 1 - y, x), to_y),
            1: lambda: (part(k, p, every, y, 1 - x), to_x),
            2: lambda: (part(k, p, z, 1 - y), to_y),
            3: lambda: (part(k, p, z, every, 1 - x), to_x),
        }[p]()
        return [remote(src, buf("R2", k, p), r["c2"].at[n], r["d2"].at[n], to)]

    def s3(k, p):
        n = gnum[k, p]
        if p < 2:
            return line_first(k, p, "R3", (y, x))
        src, to = (part(k, p, z, y, 1 - x), to_x) if p == 2 else (part(k, p, z, 1 - y, x), to_y)
        return [remote(src, buf("R3", k, p).at[0], r["c3"].at[n, 0], r["d3"].at[n, 0], to)]

    def s3b(k, p):
        return line_last(k, p, "R3", (y, x)) if p < 2 else []

    def start(copies):
        for cp in copies:
            cp.start()

    def arrived(copies):
        for cp in copies:
            cp.wait_recv()

    def r_S1(k, p, t):
        start(s1(k, p))

    def goes_and_stays(k, p):
        for q in (1, 0):
            yield q, [(1 - y if q else y, i) if p == 2 else (i, 1 - x if q else x) for i in range(2)]

    def r_A1(k, p, t):
        arrived(s1(k, p))
        R1, sl = buf("R1", k, p), gslice(k, p)
        if p > 1:
            for i in range(Y * X):
                add_into(grad[k], (z2, i // X, i % X, *sl), R1.at[1, i // X, i % X])
            start(s1b(k, p))
            return
        for q in (1, 0):
            yy = y if q == 0 else 1 - y
            xx = x if q == 0 else 1 - x

            def one(i, _):
                if p == 0:
                    add_into(grad[k], (i, yy, x, *sl), R1.at[i, yy])
                else:
                    add_into(grad[k], (i, y, xx, *sl), R1.at[i, xx])
                return 0

            lax.fori_loop(0, Z, one, 0)
            if q == 1:
                start(s2(k, p))

    def r_A2(k, p, t):
        sl = gslice(k, p)
        if p < 2:
            arrived(s2(k, p))
            R2 = buf("R2", k, p)
            for zz in (z1, lax.rem(z1 + 2, Z)):
                add_into(grad[k], (zz, y, x, *sl), R2.at[zz])
            start(s3(k, p))
            for zz in (z, z2):
                add_into(grad[k], (zz, y, x, *sl), R2.at[zz])
            return
        arrived(s1b(k, p))
        R1 = buf("R1", k, p)
        for q, places in goes_and_stays(k, p):
            for yy, xx in places:
                idx = (z, yy, xx, *sl)
                tot = grad[k][idx].astype(F32) + R1[0, yy, xx].astype(F32) + R1[2, yy, xx].astype(F32)
                grad[k][idx] = tot.astype(BF16)
            if q == 1:
                start(s2(k, p))

    def r_A3(k, p, t):
        sl = gslice(k, p)
        if p < 2:
            arrived(s3(k, p))
            add_into(grad[k], (z2, y, x, *sl), buf("R3", k, p).at[1])
            start(s3b(k, p))
            return
        arrived(s2(k, p))
        R2 = buf("R2", k, p)
        for q in (1, 0):
            yy, xx = (y, 1 - x if q else x) if p == 2 else (1 - y if q else y, x)
            add_into(grad[k], (z, yy, xx, *sl), R2.at[xx if p == 2 else yy])
            if q == 1:
                start(s3(k, p))

    def r_A4(k, p, t):
        arrived(s3b(k, p) if p < 2 else s3(k, p))
        R3 = buf("R3", k, p)
        idx = (z, y, x, *gslice(k, p))
        tot = grad[k][idx].astype(F32) + R3[0].astype(F32)
        if p < 2:
            tot = tot + R3[2].astype(F32)
        grad[k][idx] = tot.astype(BF16)

    fin_copies = []

    def r_F(k, p, t):
        i = gorder.index(k)
        row, rows, begin, size = cuts["reduce"][k][0]
        size = sum(q[3] for q in cuts["reduce"][k])
        rs = pl.ds(row, rows)
        total = grad[k].at[z, y, x, rs, span(c * HW + begin, size) if k == "m" else pl.ds(begin, size)]
        dst = outs[k].at[c, rs, pl.ds(begin, size)]
        a = pltpu.make_async_copy(total, dst, r["fl"].at[i])
        b = remote(total, dst, r["fs"].at[i], r["fr"].at[i], to_o)
        a.start()
        b.start()
        fin_copies.extend([a, b])

    TQ, TR = 256, 256
    FT = Y * X * blk // 2
    DT = Y * X * W["j"].shape[3]
    copies = {}
    lane = lax.broadcasted_iota(jnp.int32, (1, 2 * HD), 1) // HD

    def normed(h):
        center = h - jnp.mean(h, axis=-1, keepdims=True)
        inverse = lax.rsqrt(jnp.mean(center * center, axis=-1, keepdims=True) + 1e-06)
        return center * inverse, inverse

    def c_rows():
        slots = r["len"].shape[1]
        sub = lax.broadcasted_iota(jnp.int32, (slots, slots), 0)
        lan = lax.broadcasted_iota(jnp.int32, (slots, slots), 1)
        lens, dist = r["len"][...].astype(F32), r["dist"][...].astype(F32)
        ends = jnp.sum(jnp.where(lan <= sub, lens, 0.0), axis=1, keepdims=True)
        dist = jnp.sum(jnp.where(lan == sub, dist, 0.0), axis=1, keepdims=True)
        places = lax.broadcasted_iota(jnp.int32, (slots, R), 1).astype(F32)
        segment = jnp.sum(jnp.where(ends <= places, 1.0, 0.0), axis=0, keepdims=True)
        slot = lax.broadcasted_iota(jnp.int32, (slots, R), 0).astype(F32)
        ground = jnp.sum(jnp.where(slot == segment, dist, 0.0), axis=0, keepdims=True)
        alive = jnp.where(segment < slots, 1.0, 0.0)
        factor = ground / 10.0
        patch = r["patch"][...].astype(F32)
        patch = jnp.concatenate([patch[i : i + 1] for i in range(R // 128)], axis=1)
        down_ = jnp.floor((patch + 0.5) * (1.0 / 14.0))
        along = patch - 14.0 * down_
        zero = jnp.zeros_like(factor)
        rows = jnp.concatenate([segment, alive, down_ * factor, along * factor, zero, zero, zero, zero], axis=0)
        SEG[c] = rows
        COL[...] = jnp.transpose(rows)
        copies["seg"] = to_pair(SEG.at[c], SEG.at[c])

    def c_v1():
        for cp in vcps:
            cp.wait()
        copies["vy"] = tab_send(TAB.at[:, y, x], Z - 1, to_y)

    def c_v2():
        copies["vy"].wait()
        copies["vx"] = tab_send(TAB.at[:, :, x], Z, to_x)

    def c_v3():
        copies["vx"].wait()
        VG[...] = jnp.zeros_like(VG)
        count = Z * Y * X
        n, nj = D // count, 3 * D // count
        flat = TAB[...].reshape(count * 8, 128)
        table = flat.astype(BF16)
        for s_ in range(count):
            f = s_ * blk
            piece = TAB[s_ // (Y * X), s_ // X % Y, s_ % X, pl.ds(c, 1), :]
            V[8 + f // D : 9 + f // D, f % D : f % D + blk] = piece
        wide = 4 * 128
        key = lax.broadcasted_iota(jnp.int32, (128, wide), 0).astype(F32)
        row = lax.broadcasted_iota(jnp.int32, (count * 8, wide), 0).astype(F32)
        column = lax.broadcasted_iota(jnp.int32, (1, wide), 1).astype(F32)

        def spread_out(shard, entry, first):
            spot = entry + first
            line = jnp.floor((spot + 0.5) * (1.0 / 128))
            pick = jnp.where(key == spot - 128.0 * line, 1.0, 0.0).astype(BF16)
            tiled = matmul(table, pick)
            return jnp.sum(jnp.where(row == 8.0 * shard + line, tiled, 0.0), axis=0, keepdims=True)

        for a in range(0, D, wide):
            shard = jnp.floor((column + (a + 0.5)) * (1.0 / n))
            for i in range(6):
                V[i : i + 1, a : a + wide] = spread_out(shard, column + a - n * shard, 2 * blk + nj + i * n)
        for a in range(0, 3 * HW, wide):
            tile = jnp.floor((column + (a + 0.5)) * (1.0 / 128))
            hp = jnp.floor((tile + 0.5) * (1.0 / 3))
            which = tile - 3.0 * hp
            of = which * D + c.astype(F32) * HW + hp * 128.0 + (column + a - 128.0 * tile)
            shard = jnp.floor((of + 0.5) * (1.0 / nj))
            V[6 + a // D : 7 + a // D, a % D : a % D + wide] = spread_out(shard, of - nj * shard, 2 * blk)

    def c_h0():
        local_wait("t", OUTB)
        local_wait("e", EB.at[own, :])

        def rows128(i, _):
            rr, gr = span(i * 128, 128), span(c * R + i * 128, 128)
            EB[gr, :] = (EB[gr, :].astype(F32) * COL[rr, 1:2]).astype(BF16)
            Q = D // 4
            for j in (0, 1):
                angle = COL[rr, 2 + j : 3 + j] * r["freq"][...]
                at_ = 2 * j * Q
                H0[rr, at_ : at_ + Q] = OUTB[rr, at_ : at_ + Q].astype(F32) + jnp.sin(angle)
                at_ += Q
                H0[rr, at_ : at_ + Q] = OUTB[rr, at_ : at_ + Q].astype(F32) + jnp.cos(angle)
            return 0

        lax.fori_loop(0, R // 128, rows128, 0)
        copies["eb"] = to_pair(EB.at[own, :], EB.at[own, :])

    def c_ln1():
        def norm_one(i, _):
            rr, gr = span(i * 128, 128), span(c * R + i * 128, 128)
            scaled, _i = normed(H0[rr, :])
            N1[gr, :] = (scaled * V[0:1, :] + V[1:2, :]).astype(BF16)
            VG[5:6, :] += jnp.sum(EB[gr, :].astype(F32), axis=0, keepdims=True)
            return 0

        lax.fori_loop(0, R // 128, norm_one, 0)
        copies["n1"] = to_pair(N1.at[own, :], N1.at[own, :])

    def c_qkv(t):
        if t == 0:
            copies["seg"].wait()
            copies["n1"].wait()
            copies["eb"].wait()
            gather_wait("j")
        w = W["j"][:, :, :, :, t * TQ : (t + 1) * TQ].reshape(D, TQ)
        f = t * TQ
        b = V[6 + f // D : 7 + f // D, f % D : f % D + TQ]
        QKV[:, f : f + TQ] = (matmul(N1[...], w) + b).astype(BF16)

    def same_image(g):
        return jnp.transpose(SEG[g])[:, 0:1] == SEG[g, 0:1, :]

    def attend(g, hp):
        rr = span(g * R, R)
        q, k, v = (QKV[rr, qcols(hp, i)] for i in range(3))
        same = same_image(g)
        res = []
        for i in (0, 1):
            qi = jnp.where(lane == i, q.astype(F32) * HD**-0.5, 0.0).astype(BF16)
            s = jnp.where(same, contract(k, qi, LAST), NEVER)
            top = jnp.max(s, axis=0, keepdims=True)
            e = jnp.exp(s - top)
            tot = jnp.sum(e, axis=0, keepdims=True)
            L[g * half_heads + 2 * hp + i] = top + jnp.log(tot)
            pb = (e * (1.0 / tot)).astype(BF16)
            res.append(contract(v, pb, FIRST)[i * HD : (i + 1) * HD])
        return jnp.transpose(jnp.concatenate(res, axis=0)).astype(BF16)

    pairs = half_heads // 2

    def c_at(i):
        if i < pairs:
            OS[:, 2 * HD * i : 2 * HD * (i + 1)] = attend(o, i)
            if i == pairs - 1:
                copies["o"] = to_pair(OS, OA.at[:, span(c * HW, HW)])
        else:
            OA[:, span(c * HW + 2 * HD * (i - pairs), 2 * HD)] = attend(c, i - pairs)

    def c_wm():
        gather_wait("m")
        half = W["m"].at[:, :, :, :, span(c * HW, HW)]
        copies["wm"] = to_pair(half, half)

    def c_mrg():
        copies["o"].wait()
        copies["wm"].wait()
        for t in range(R // TR):
            rr = pl.ds(t * TR, TR)
            h1 = H0[rr, :] + matmul(OA[rr, :], W["m"][...].reshape(D, D)) + V[2:3, :]
            H1[rr, :] = h1
            scaled, _i = normed(h1)
            N2[span(c * R + t * TR, TR), :] = (scaled * V[3:4, :] + V[4:5, :]).astype(BF16)
        copies["n2"] = to_pair(N2.at[own, :], N2.at[own, :])

    def c_ge(t):
        if t == 0:
            copies["n2"].wait()
            gather_wait("x")
        cc = slice(t * TQ, (t + 1) * TQ)
        f = t * TQ
        b = V[8 + f // D : 9 + f // D, f % D : f % D + TQ]
        for h in range(2):
            rr = slice(h * R, (h + 1) * R)
            u = matmul(N2[rr, :], W["x"][:, :, :, :, cc].reshape(D, TQ)) + b
            cdf = 0.5 * (1.0 + lax.erf(u * 0.7071067811865476))
            G[rr, cc] = (u * cdf).astype(BF16)
            DU[rr, cc] = (cdf + u * (jnp.exp(-0.5 * u * u) * 0.3989422804014327)).astype(BF16)

    def c_gs(i):
        for t in (2 * i, 2 * i + 1):
            g = contract(G[:, t * FT : (t + 1) * FT], EB[...], FIRST)
            GS[t // Y, t % Y] = g.astype(BF16).reshape(X, blk, D)

    def c_du(i):
        if i == 0:
            gather_wait("s")
        for t in (2 * i, 2 * i + 1):
            cc = slice(t * FT, (t + 1) * FT)
            w = W["s"][t // Y, t % Y].reshape(FT, D)
            row, col = 8 + t * FT // D, t * FT % D
            for h in range(2):
                rr = slice(h * R, (h + 1) * R)
                du = (contract(EB[rr, :], w, LAST) * DU[rr, cc].astype(F32)).astype(BF16)
                DU[rr, cc] = du
                VG[row : row + 1, col : col + FT] += jnp.sum(du.astype(F32), axis=0, keepdims=True)

    def c_h2s():
        for t in range(D // TQ):
            cc = slice(t * TQ, (t + 1) * TQ)
            XS[:, cc] = matmul(G[sib, :], W["s"][:, :, :, :, cc].reshape(FC, TQ)).astype(BF16)
        copies["h2"] = to_pair(XS, OUTB)

    def c_h2o():
        copies["h2"].wait_recv()
        for t in range(D // TQ):
            cc = slice(t * TQ, (t + 1) * TQ)
            own_part = matmul(G[own, :], W["s"][:, :, :, :, cc].reshape(FC, TQ))
            OUTB[:, cc] = (
                (H1[:, cc] + own_part + OUTB[:, cc].astype(F32) + V[5:6, cc]) * COL[:, 1:2]
            ).astype(BF16)
        copies["out"] = pltpu.make_async_copy(OUTB, r["out"], r["fl"].at[len(gorder)])
        copies["out"].start()
        gather_done("s")

    def back_part(left, wk, n, name, dst):
        for t in range(Z):
            w = wk[t][:, :, :, 0:n].reshape(DT, n)
            dst[:, t * DT : (t + 1) * DT] = contract(left[sib, 0:n], w, LAST).astype(BF16)
        copies[name] = to_pair(dst, XR)

    def c_dn2s():
        back_part(DU, W["x"], FC, "dn2", DA)

    def c_gx(i):
        h, half = W["j"].shape[3], FC // 2
        for t in range(Z):
            g = contract(N2[:, t * DT : (t + 1) * DT], DU[:, i * half : (i + 1) * half], FIRST)
            GX[t, :, :, i * h : (i + 1) * h, :] = g.astype(BF16).reshape(Y, X, h, half)

    def norm_back(dy, scaled, inverse, gain, vg):
        ds_ = dy * gain
        VG[vg : vg + 1, :] += jnp.sum(dy * scaled, axis=0, keepdims=True)
        VG[vg + 1 : vg + 2, :] += jnp.sum(dy, axis=0, keepdims=True)
        cen = ds_ - jnp.mean(ds_, axis=-1, keepdims=True)
        cen = cen - scaled * jnp.mean(ds_ * scaled, axis=-1, keepdims=True)
        return cen * inverse

    def c_dn2o():
        copies["dn2"].wait()
        for t in range(R // TR):
            rr, gr = pl.ds(t * TR, TR), span(c * R + t * TR, TR)
            dy = contract(DU[gr, :], W["x"][...].reshape(D, FC), LAST) + XR[rr, :].astype(F32)
            scaled, inverse = normed(H1[rr, :])
            dh = EB[gr, :].astype(F32) + norm_back(dy, scaled, inverse, V[3:4, :], 3)
            H1[rr, :] = dh
            DA[rr, :] = dh.astype(BF16)
            VG[2:3, :] += jnp.sum(DA[rr, :].astype(F32), axis=0, keepdims=True)
        gather_done("x")

    def c_dO():
        copies["h2"].wait_send()
        cw = X * W["m"].shape[3]
        for t, base in enumerate((o, c)):
            for u in range(HW // cw):
                w = W["m"][base * (Z // 2) + u // Y, u % Y].reshape(cw, D)
                res = contract(DA[...], w, LAST).astype(BF16)
                if t == 0:
                    OS[:, u * cw : (u + 1) * cw] = res
                else:
                    G[own, 3 * HW + u * cw : 3 * HW + (u + 1) * cw] = res
            if t == 0:
                copies["do"] = to_pair(OS, G.at[own, pl.ds(3 * HW, HW)])
        gather_done("m")

    def c_gm():
        for t in range(Z):
            g = contract(OA[:, t * DT : (t + 1) * DT], DA[...], FIRST)
            GM[t] = g.astype(BF16).reshape(Y, X, W["m"].shape[3], D)
        copies["gm"] = to_pair(GM.at[:, :, :, :, span(o * HW, HW)], r["GMR"])

    def c_gma():
        copies["gm"].wait()

        def add_pair(i, _):
            for j in range(Y * X):
                idx = (i, j // X, j % X, slice(None), span(c * HW, HW))
                add_into(GM, idx, r["GMR"].at[i, j // X, j % X])
            return 0

        lax.fori_loop(0, Z, add_pair, 0)

    def attend_back(g, hp):
        rr = span(g * R, R)
        qc, kc, vc = (qcols(hp, i) for i in range(3))
        q, k, v = QKV[rr, qc], QKV[rr, kc], QKV[rr, vc]
        do = G[rr, 3 * HW + hp * 2 * HD : 3 * HW + (hp + 1) * 2 * HD]
        same = same_image(g)
        dq, dk, dv = [], [], []
        for i in (0, 1):
            qi = jnp.where(lane == i, q.astype(F32) * HD**-0.5, 0.0).astype(BF16)
            di = jnp.where(lane == i, do.astype(F32), 0.0).astype(BF16)
            s = jnp.where(same, contract(k, qi, LAST), NEVER)
            pr = jnp.exp(s - L[g * half_heads + 2 * hp + i])
            dp = contract(v, di, LAST)
            delta = jnp.sum(pr * dp, axis=0, keepdims=True)
            dsb = (pr * (dp - delta) * HD**-0.5).astype(BF16)
            dq.append(contract(k, dsb, FIRST)[i * HD : (i + 1) * HD])
            dk.append(matmul(dsb, q))
            dv.append(matmul(pr.astype(BF16), do))
        G[rr, qc] = jnp.transpose(jnp.concatenate(dq, axis=0)).astype(BF16)
        G[rr, kc] = jnp.where(lane == 0, dk[0], dk[1]).astype(BF16)
        G[rr, vc] = jnp.where(lane == 0, dv[0], dv[1]).astype(BF16)

    few = pairs // 2
    back_order = [(c, hp) for hp in range(few)] + [(o, hp) for hp in range(few)]
    back_order += [(g, hp) for hp in range(few, pairs) for g in (c, o)]

    def c_ab(i):
        if i == few:
            copies["do"].wait()
        attend_back(*back_order[i])

    def c_gj(i):
        row, rows, begin, size = cuts["reduce"]["jkl"[i]][0]
        size = sum(q[3] for q in cuts["reduce"]["jkl"[i]])
        for t in range(Z):
            g = contract(N1[:, t * DT : (t + 1) * DT], G[:, begin : begin + size], FIRST)
            GJ[t, :, :, :, begin : begin + size] = g.astype(BF16).reshape(Y, X, rows, size)

    def c_dn1s():
        back_part(G, W["j"], 3 * HW, "dn1", XS)
        for t in range(3):
            row, col = 6 + t * HW // D, t * HW % D
            VG[row : row + 1, col : col + HW] += jnp.sum(
                G[:, t * HW : (t + 1) * HW].astype(F32), axis=0, keepdims=True
            )

    def c_dn1o():
        copies["dn1"].wait()
        for t in range(R // TR):
            rr, gr = pl.ds(t * TR, TR), span(c * R + t * TR, TR)
            dy = contract(G[gr, 0 : 3 * HW], W["j"][...].reshape(D, 3 * HW), LAST) + XR[rr, :].astype(F32)
            scaled, inverse = normed(H0[rr, :])
            H1[rr, :] = H1[rr, :] + norm_back(dy, scaled, inverse, V[0:1, :], 0)
        copies["gt"] = pltpu.make_async_copy(H1, r["gt"], r["fl"].at[len(gorder) + 1])
        copies["gt"].start()
        gather_done("j")

    def vg_send(slot, to):
        cp = remote(VG, VGR.at[slot], r["gs"].at[slot], r["gr"].at[slot], to)
        cp.start()
        return cp

    def vg_add(slots):
        acc = VG[...]
        for i in slots:
            acc = acc + VGR[i]
        VG[...] = acc

    def c_vz():
        copies["gz"] = [vg_send(d - 1, to_z[d]) for d in range(1, Z)]

    def c_vx():
        for cp in copies["gz"]:
            cp.wait()
        vg_add(range(Z - 1))
        copies["gx"] = vg_send(Z - 1, to_x)

    def c_vy():
        copies["gx"].wait()
        vg_add([Z - 1])
        copies["gy"] = vg_send(Z, to_y)

    def c_vp():
        copies["gy"].wait()
        vg_add([Z])
        copies["ov"] = pltpu.make_async_copy(VG, r["ov"].at[c], r["fl"].at[len(gorder) + 2])
        copies["ov"].start()
        copies["ovr"] = to_pair(VG, r["ov"].at[c])

    def c_end():
        for k in gorder:
            for p in range(4):
                if cuts["reduce"][k][p][3]:
                    for cp in s1(k, p) + s1b(k, p) + s2(k, p) + s3(k, p) + s3b(k, p):
                        cp.wait_send()
        for cp in fin_copies + [copies[n] for n in ("out", "gt", "ov", "ovr")]:
            cp.wait()

    steps = locals()
    landed = set()
    for word in schedule:
        if word[0] == "_":
            name = word[1:].rstrip("0123456789")
            if name in ("v", "h", "ln"):
                name = word[1:]
            arg = word[1 + len(name) :]
            steps["c_" + name](*([int(arg)] if arg else []))
            continue
        op, k, p, t = word[:2], word[2], int(word[3]), int(word[4])
        if op in ("z0", "p0", "fz") and t == 0 and k not in landed:
            landed.add(k)
            local_wait(k, own_ref[k])
        steps[("r_" if op[0] in "SAF" else "g_") + op.rstrip("_")](k, p, t)


def finish_kernel(dims, names, *args):
    r = dict(zip(names, args, strict=True))
    N = dims[0] * dims[1] * dims[2]
    taken = [
        pltpu.make_async_copy(r[n], r["v_" + n], r["sem"].at[i])
        for i, n in enumerate(("out", "gt", "oj", "om", "ox", "os", "ov"))
    ]
    for cp in taken:
        cp.start()
    big = [
        pltpu.make_async_copy(r["v_" + n], r["f_" + n], r["sem"].at[7 + i]) for i, n in enumerate(("out", "gt"))
    ]
    for i, cp in enumerate(taken):
        cp.wait()
        if i < 2:
            big[i].start()
    r.update({n: r["v_" + n] for n in ("oj", "om", "ox", "os", "ov")})
    rj, D = r["f_m"].shape
    HW, P2 = D // 2, 2 * HD
    blk = r["os"].shape[1]
    half = r["ox"].shape[2]
    for core in (0, 1):
        for hp in range(HW // P2):
            for i in range(3):
                to, of = i * D + core * HW + hp * P2, (3 * hp + i) * P2
                r["f_j"][:, to : to + P2] = r["oj"][core, :, of : of + P2].astype(F32)
        r["f_m"][:, core * HW : (core + 1) * HW] = r["om"][core].astype(F32)
        for i in range(2 * half // blk):
            row, col = i * blk // half * rj, i * blk % half
            to = (2 * i + core) * blk
            r["f_x"][:, to : to + blk] = r["ox"][core, row : row + rj, col : col + blk].astype(F32)
        r["f_s"][core * blk : (core + 1) * blk, :] = r["os"][core].astype(F32)
    me = lax.axis_index("dp")
    ov = r["ov"]
    both = ov[0, 0:8, :] + ov[1, 0:8, :]

    def mine(row, n):
        return pltpu.roll(row, (N - me) * n, 1)[:, :n]

    for i, name in enumerate(("g1", "b1", "mb", "g2", "b2", "sb")):
        r["f_" + name][...] = mine(jnp.broadcast_to(both[i : i + 1], (8, D)), D // N)[0:1]
    at_ = [((3 * hp + i) * P2, core) for i in range(3) for core in (0, 1) for hp in range(HW // P2)]
    row = jnp.concatenate([ov[core, 6 + a // D : 7 + a // D, a % D : a % D + P2] for a, core in at_], axis=1)
    r["f_jb"][...] = mine(jnp.broadcast_to(row, (8, 3 * D)), 3 * D // N)[0:1]
    for core in (0, 1):
        row = jnp.concatenate([ov[core, 8 + i : 9 + i, :] for i in range(2 * half // D)], axis=1)
        r["f_xb"][:, core * blk : (core + 1) * blk] = mine(jnp.broadcast_to(row, (8, 2 * half)), blk)[0:1]
    for cp in big:
        cp.wait()


def tiled_cuts(tiles):
    starts = [sum(tiles[:p]) * 128 for p in range(4)]
    return [(start, n * 128) for start, n in zip(starts, tiles, strict=True)]


def paths(rows, row, begin, tiles):
    return [(row, rows, begin + start, size) for start, size in tiled_cuts(tiles)]


def fused_layer(dims, *args):
    (
        tokens,
        kept_patch,
        image_lengths,
        ground_distance,
        cotangent,
        norm_one_gain,
        norm_one_bias,
        joint_weight,
        joint_bias,
        merge_weight,
        merge_bias,
        norm_two_gain,
        norm_two_bias,
        expand_weight,
        expand_bias,
        shrink_weight,
        shrink_bias,
    ) = args
    Z, Y, X = dims
    N = Z * Y * X
    R, D = tokens.shape
    FF = expand_weight.shape[1]
    HW, FC, blk = D // 2, FF // 2, shrink_weight.shape[0] // 2
    rj = joint_weight.shape[0]
    pieces = [expand_bias, joint_bias, norm_one_gain, norm_one_bias, merge_bias, norm_two_gain, norm_two_bias, shrink_bias]
    vec, begin = jnp.zeros((8 * 128,), F32), 0
    for v in pieces:
        vec = vec + jnp.pad(v.astype(F32), (begin, 8 * 128 - begin - v.shape[0]))
        begin += v.shape[0]
    vec = vec.reshape(8, 128)
    quarter = D // 4
    freq = 1.0 / np.float32(10000.0) ** (np.arange(quarter, dtype=np.float32) / np.float32(quarter))

    cuts = {
        "gather": {k: tiled_cuts(tiles) for k, tiles in GATHER.items()},
        "reduce": {
            "s": paths(blk, 0, 0, REDUCE["s"]),
            "t": paths(blk, 0, D // 2, REDUCE["t"]),
            "x": paths(rj, 0, 0, REDUCE["x"]),
            "u": paths(rj, rj, 0, REDUCE["u"]),
            "m": paths(rj, 0, 0, REDUCE["m"]),
            "j": paths(rj, 0, 0, REDUCE["j"]),
            "k": paths(rj, 0, 3 * HW // 2, REDUCE["k"]),
            "l": paths(rj, 0, 9 * HW // 4, REDUCE["l"]),
        },
    }

    vm, hbm = pl.BlockSpec(memory_space=pltpu.VMEM), pl.BlockSpec(memory_space=pl.ANY)
    ins = [("patch", kept_patch.reshape(R // 128, 128), vm), ("len", image_lengths, vm), ("dist", ground_distance, vm)]
    ins += [("freq", jnp.asarray(freq[None, :], F32), vm), ("vec", vec, vm), ("tok", tokens, hbm), ("cot", cotangent, hbm)]
    ins += [("wj", joint_weight, hbm), ("wm", merge_weight, hbm), ("wx", expand_weight, hbm), ("ws", shrink_weight, hbm)]
    S = jax.ShapeDtypeStruct
    outs = [
        ("out", S((R, D), BF16), hbm),
        ("gt", S((R, D), F32), hbm),
        ("oj", S((2, rj, 3 * HW), BF16), hbm),
        ("om", S((2, rj, HW), BF16), hbm),
        ("ox", S((2, 2 * rj, FC // 2), BF16), hbm),
        ("os", S((2, blk, D), BF16), hbm),
        ("ov", S((2, 16, D), F32), hbm),
    ]
    V = pltpu.VMEM
    dma = pltpu.SemaphoreType.DMA
    scratch = [
        ("Wj", V((Z, Y, X, rj, 3 * HW), BF16)),
        ("Wm", V((Z, Y, X, rj, D), BF16)),
        ("Wx", V((Z, Y, X, rj, FC), BF16)),
        ("Ws", V((Z, Y, X, blk, D), BF16)),
        ("GS", V((Z, Y, X, blk, D), BF16)),
        ("GM", V((Z, Y, X, rj, D), BF16)),
        ("GMR", V((Z, Y, X, rj, HW), BF16)),
        ("H0", V((R, D), F32)),
        ("N1", V((2 * R, D), BF16)),
        ("QKV", V((2 * R, 3 * HW), BF16)),
        ("OA", V((R, D), BF16)),
        ("H1", V((R, D), F32)),
        ("N2", V((2 * R, D), BF16)),
        ("G", V((2 * R, FC), BF16)),
        ("DU", V((2 * R, FC), BF16)),
        ("EB", V((2 * R, D), BF16)),
        ("SEG", V((2, 8, R), F32)),
        ("COL", V((R, 8), F32)),
        ("L", V((D // HD, 1, R), F32)),
        ("V", V((16, D), F32)),
        ("TAB", V((Z, Y, X, 8, 128), F32)),
        ("VG", V((16, D), F32)),
        ("VGR", V((Z + 1, 16, D), F32)),
        ("XS", V((R, D), BF16)),
        ("XR", V((R, D), BF16)),
        ("OUTB", V((R, D), BF16)),
        ("DA", V((R, D), BF16)),
    ]
    for k, four in cuts["reduce"].items():
        for p, (_, n, _, w) in enumerate(four):
            if w:
                first = (Z, 2) if p < 2 else (3, Y, X)
                second, third = ((Z,), (3,)) if p < 2 else ((2,), (1,))
                for name, lead in (("R1", first), ("R2", second), ("R3", third)):
                    scratch.append(("%s%s%d" % (name, k, p), V((*lead, n, w), BF16)))
    for name, shape in (
        ("ps", (12,)),
        ("pr", (12,)),
        ("vs", (Z + 1,)),
        ("vr", (Z + 1,)),
        ("gs", (Z + 1,)),
        ("gr", (Z + 1,)),
        ("ls", (6,)),
        ("az", (16, 2, Z)),
        ("bz", (16, Z)),
        ("a2", (16,)),
        ("b2", (16, Z)),
        ("a3", (16,)),
        ("b3", (16,)),
        ("c1", (32, 3)),
        ("d1", (32, 3)),
        ("c2", (32,)),
        ("d2", (32,)),
        ("c3", (32, 3)),
        ("d3", (32, 3)),
        ("fl", (11,)),
        ("fs", (8,)),
        ("fr", (8,)),
    ):
        scratch.append((name, dma(shape)))
    names = [n for n, *_ in ins + outs + scratch]
    res = pl.pallas_call(
        functools.partial(layer_kernel, dims, cuts, SCHEDULE, names),
        out_shape=[s for _, s, _ in outs],
        in_specs=[s for _, _, s in ins],
        out_specs=[s for _, _, s in outs],
        scratch_shapes=[s for _, s in scratch],
        compiler_params=pltpu.CompilerParams(
            collective_id=0, has_side_effects=True, vmem_limit_bytes=VMEM_BYTES
        ),
    )(*[a for _, a, _ in ins])

    far = pl.BlockSpec(memory_space=pltpu.HBM)
    given = [(n, a, far) for (n, _, _), a in zip(outs, res, strict=True)]
    made = [("f_out", S((R, D), BF16), far), ("f_gt", S((R, D), F32), far)]
    made += [("f_" + n, S((1, D // N), F32), vm) for n in ("g1", "b1", "mb", "g2", "b2", "sb")]
    made += [("f_jb", S((1, 3 * D // N), F32), vm), ("f_xb", S((1, FF // N), F32), vm)]
    made += [("f_j", S((rj, 3 * D), F32), vm), ("f_m", S((rj, D), F32), vm)]
    made += [("f_x", S((rj, FF), F32), vm), ("f_s", S((2 * blk, D), F32), vm)]
    last = pl.pallas_call(
        functools.partial(finish_kernel, dims, [n for n, *_ in given + made] + ["v_" + n for n, *_ in outs] + ["sem"]),
        out_shape=[s for _, s, _ in made],
        in_specs=[s for _, _, s in given],
        out_specs=[s for _, _, s in made],
        scratch_shapes=[V(s.shape, s.dtype) for _, s, _ in outs] + [dma((9,))],
        compiler_params=pltpu.CompilerParams(vmem_limit_bytes=VMEM_BYTES),
    )(*[a for _, a, _ in given])
    f = {n[2:]: a for (n, *_), a in zip(made, last, strict=True)}
    g1, b1, mb, g2, b2, sb, g_jb, g_xb = (f[n].reshape(-1) for n in ("g1", "b1", "mb", "g2", "b2", "sb", "jb", "xb"))
    return f["out"], f["gt"], g1, b1, f["j"], g_jb, f["m"], mb, g2, b2, f["x"], g_xb, f["s"], sb


def layout(mesh, joint_rows, shrink_rows):
    n = mesh.shape["dp"]
    if mesh.shape["rep"] != 2 or n != 16 or joint_rows % 16 or shrink_rows % 256:
        return None
    return (n // 4, 2, 2)


def on_device(mesh, *args):
    dims = layout(mesh, args[7].shape[0], args[15].shape[0])
    if dims is None:
        return general_layer(*args)
    return fused_layer(dims, *args)


def solution(mesh):
    rows, rows2 = P(("dp", "rep")), P(("dp", "rep"), None)
    vector, matrix = P("dp"), P("dp", None)
    return jax.shard_map(
        functools.partial(on_device, mesh),
        mesh=mesh,
        in_specs=(
            rows2,
            rows,
            rows2,
            rows2,
            rows2,
            vector,
            vector,
            matrix,
            vector,
            matrix,
            vector,
            vector,
            vector,
            matrix,
            vector,
            matrix,
            vector,
        ),
        out_specs=(
            rows2,
            rows2,
            vector,
            vector,
            matrix,
            vector,
            matrix,
            vector,
            vector,
            vector,
            matrix,
            vector,
            matrix,
            vector,
        ),
        check_vma=False,
    )
```

```python
import functools

import jax
import jax.numpy as jnp
import numpy as np
from jax import lax
from jax.experimental import pallas as pl
from jax.experimental.pallas import tpu as pltpu
from jax.sharding import PartitionSpec as P

HD = 64
MESH = pl.DeviceIdType.MESH
F32 = jnp.float32
BF16 = jnp.bfloat16
NEVER = -1000000000.0
VMEM_BYTES = 127 * 2**19
GATHER = {"j": (5, 5, 1, 1), "m": (2, 2, 0, 0), "x": (6, 6, 2, 2), "s": (3, 3, 1, 1)}
REDUCE = {
    "s": (1, 1, 1, 1),
    "t": (1, 1, 1, 1),
    "x": (3, 3, 1, 1),
    "u": (4, 4, 0, 0),
    "m": (2, 2, 0, 0),
    "j": (3, 3, 0, 0),
    "k": (2, 1, 0, 0),
    "l": (1, 2, 0, 0),
}
SCHEDULE = [
    "p0s20", "z0m10", "p0x30", "fzx10", "z0j00", "z0j10", "z0m00", "p0j30", "fzj00", "fzm00", "fzm10", "z0x10",
    "p0j20", "p1j30", "fzj01", "_rows", "fzj11", "p2j30", "p1x30", "p1j20", "_v1", "p0x20", "fzj10", "fzs10",
    "fzm11", "fzj12", "fzm12", "p0s30", "p1s20", "fzj02", "fzm01", "fzj13", "p2j20", "_v2", "fzx11", "f2j01",
    "f2j11", "p1x20", "fzj03", "f2j00", "p2x30", "f2m00", "_h0", "pzj21", "pzj31", "z0x00", "z0s10", "f2m01",
    "f2j10", "pzj32", "fzm13", "f2j13", "pzj22", "f2x10", "f2j02", "f2j03", "fzm02", "f2j12", "fzx01", "fzx12",
    "pzj33", "_v3", "fzm03", "pzx31", "_ln1", "fzx00", "p2x20", "z0s00", "pzj23", "fzx13", "_qkv0", "_qkv1", "_qkv2",
    "fzx02", "p1s30", "pzx21", "f2m03", "_qkv3", "_qkv4", "p2s20", "f2m12", "fzs01", "f2x01", "_qkv5", "_at0",
    "f2x13", "fzx03", "_at1", "_at2", "_at3", "f2m02", "pzx32", "fzs11", "f2m10", "_at4", "f2x00", "f2m11", "p2s30",
    "f2x02", "f2x12", "f2m13", "pzx33", "_at5", "fzs02", "f2x11", "f2x03", "_at6", "_at7", "_wm", "fzs00", "fzs12",
    "pzx22", "fzs03", "f2s01", "pzs31", "f2s11", "pzs21", "_mrg", "fzs13", "f2s10", "pzx23", "_ge0", "f2s02", "_ge1",
    "_ge2", "_ge3", "f2s03", "pzs32", "pzs22", "_ge4", "_ge5", "f2s12", "_ge6", "_ge7", "f2s00", "_gs0", "f2s13",
    "_gs1", "_gs2", "_gs3", "S1s30", "pzs23", "S1t00", "S1t30", "S1s20", "S1t10", "S1s00", "S1s10", "S1t20", "pzs33",
    "_du0", "_du1", "_du2", "_du3", "_h2s", "A1t00", "A1t10", "_dn2s", "_h2o", "A1s10", "A1s00", "_gx0", "S1x10",
    "S1x00", "A1t30", "_gx1", "S1u10", "A1s20", "_dn2o", "S1x30", "S1x20", "S1u00", "_dO", "_gm", "_ab0", "A2t30",
    "A2t00", "A1t20", "_gma", "A1x30", "A1x10", "S1m10", "_ab1", "A2t10", "A2s10", "_ab2", "A2s00", "A1u10", "A1x00",
    "_ab3", "A3t00", "_gj0", "A1s30", "A1m10", "S1j10", "_ab4", "A1x20", "A2x10", "A3t30", "S1j00", "A3s10", "_ab5",
    "A3t10", "S1m00", "A2u10", "_gj1", "A1u00", "A2x00", "A2m10", "_ab6", "A3x10", "_ab7", "_gj2", "S1l10", "A3u10",
    "_dn1s", "A3x00", "S1l00", "A1j10", "S1k00", "A3s00", "A3m10", "A1j00", "A2u00", "_dn1o", "_vz", "S1k10",
    "A1l10", "A1m00", "A2x20", "A1l00", "A2j00", "A2j10", "A2s20", "A3u00", "A2m00", "A2s30", "A4s00", "A1k00",
    "A3j00", "A1k10", "A3j10", "A2l00", "A4s10", "_vx", "A2t20", "A4u00", "A3x20", "A4t30", "A2x30", "A3s20",
    "A2l10", "A3m00", "A3s30", "A4u10", "A2k10", "A2k00", "_vy", "A4x00", "A3l00", "A4m10", "A3l10", "A4s30",
    "A3t20", "A3x30", "A3k10", "A4m00", "F_u00", "A3k00", "F_m00", "A4s20", "F_s00", "A4x20", "A4j10", "_vp",
    "A4l00", "A4t20", "A4x30", "A4j00", "A4x10", "A4t00", "F_j00", "F_x00", "A4k10", "A4l10", "A4t10", "F_l00",
    "F_t00", "A4k00", "F_k00", "_end",
]

LAST = (((1,), (1,)), ((), ()))
FIRST = (((0,), (0,)), ((), ()))

def packing(lengths, row_count):
    image_ends = jnp.cumsum(lengths)
    row_ids = jnp.arange(row_count, dtype=jnp.int32)
    segment = jnp.sum((image_ends[None, :] <= row_ids[:, None]).astype(jnp.int32), axis=1)
    live_rows = (row_ids < image_ends[-1]).astype(jnp.float32)
    return (segment, live_rows)


def row_distance(segment, distances):
    slots = jnp.arange(distances.shape[-1], dtype=jnp.int32)
    onehot = (segment[:, None] == slots[None, :]).astype(jnp.float32)
    return jnp.sum(onehot * distances[None, :].astype(jnp.float32), axis=1)


def positions(patch_index, ground_rows, model_width):
    quarter = model_width // 4
    frequency = 1.0 / 10000.0 ** (jnp.arange(quarter, dtype=jnp.float32) / quarter)
    factor = ground_rows / 10.0
    across_rows = ((patch_index // 14).astype(jnp.float32) * factor)[..., None] * frequency
    along_rows = ((patch_index % 14).astype(jnp.float32) * factor)[..., None] * frequency
    return jnp.concatenate(
        [jnp.sin(across_rows), jnp.cos(across_rows), jnp.sin(along_rows), jnp.cos(along_rows)],
        axis=-1,
    )


def norm_forward(hidden, scaling, offset):
    center = hidden - jnp.mean(hidden, axis=-1, keepdims=True)
    inverse = lax.rsqrt(jnp.mean(center * center, axis=-1, keepdims=True) + 1e-06)
    scaled = center * inverse
    return (scaled * scaling.astype(jnp.float32) + offset.astype(jnp.float32), scaled, inverse)


def norm_backward(incoming, scaled, inverse, scaling):
    grad_scaled = incoming * scaling.astype(jnp.float32)
    centered_grad = grad_scaled - jnp.mean(grad_scaled, axis=-1, keepdims=True)
    centered_grad = centered_grad - scaled * jnp.mean(grad_scaled * scaled, axis=-1, keepdims=True)
    return (centered_grad * inverse, jnp.sum(incoming * scaled, axis=0), jnp.sum(incoming, axis=0))


def gelu_slope(hidden_pre):
    normal_cdf = 0.5 * (1.0 + jax.scipy.special.erf(hidden_pre * 0.7071067811865476))
    density = jnp.exp(-0.5 * hidden_pre * hidden_pre) * 0.3989422804014327
    return normal_cdf + hidden_pre * density


def general_layer(
    tokens,
    kept_patch,
    image_lengths,
    ground_distance,
    cotangent,
    norm_one_gain,
    norm_one_bias,
    joint_weight,
    joint_bias,
    merge_weight,
    merge_bias,
    norm_two_gain,
    norm_two_bias,
    expand_weight,
    expand_bias,
    shrink_weight,
    shrink_bias,
):
    full = (
        lax.all_gather(norm_one_gain, "dp", axis=0, tiled=True),
        lax.all_gather(norm_one_bias, "dp", axis=0, tiled=True),
        lax.all_gather(joint_weight, "dp", axis=0, tiled=True),
        lax.all_gather(joint_bias, "dp", axis=0, tiled=True),
        lax.all_gather(merge_weight, "dp", axis=0, tiled=True),
        lax.all_gather(merge_bias, "dp", axis=0, tiled=True),
        lax.all_gather(norm_two_gain, "dp", axis=0, tiled=True),
        lax.all_gather(norm_two_bias, "dp", axis=0, tiled=True),
        lax.all_gather(expand_weight, "dp", axis=0, tiled=True),
        lax.all_gather(expand_bias, "dp", axis=0, tiled=True),
        lax.all_gather(shrink_weight, "dp", axis=0, tiled=True),
        lax.all_gather(shrink_bias, "dp", axis=0, tiled=True),
    )
    row_count = tokens.shape[0]
    model_width = tokens.shape[1]
    head_count = model_width // HD
    segment, live_rows = packing(image_lengths[0], row_count)
    ground_rows = row_distance(segment, ground_distance[0])
    residual_in = tokens.astype(jnp.float32) + positions(kept_patch, ground_rows, model_width)
    first, scaled_one, inverse_one = norm_forward(residual_in, full[0], full[1])
    first_low = first.astype(jnp.bfloat16)
    projected = (
        jnp.dot(first_low, full[2], preferred_element_type=jnp.float32)
        + full[3].astype(jnp.float32)
    ).astype(jnp.bfloat16)
    queries = projected[:, :model_width].reshape(row_count, head_count, HD)
    key_rows = projected[:, model_width : 2 * model_width].reshape(row_count, head_count, HD)
    value_rows = projected[:, 2 * model_width :].reshape(row_count, head_count, HD)
    score_scale = HD ** (-0.5)

    def block_scores():
        raw_scores = (
            jnp.einsum("qhd,khd->hqk", queries, key_rows, preferred_element_type=jnp.float32)
            * score_scale
        )
        same_image = segment[:, None] == segment[None, :]
        return jnp.where(same_image[None], raw_scores, -1000000000.0)

    scores = block_scores()
    highest_score = jnp.max(scores, axis=-1, keepdims=True)
    exponent = jnp.exp(scores - highest_score)
    row_total = jnp.sum(exponent, axis=-1, keepdims=True)
    softmax_rows = exponent / row_total
    log_totals = highest_score + jnp.log(row_total)
    attended_parts = jnp.einsum(
        "hqk,khd->qhd",
        softmax_rows.astype(jnp.bfloat16),
        value_rows,
        preferred_element_type=jnp.float32,
    )
    attended = attended_parts.reshape(row_count, model_width).astype(jnp.bfloat16)
    branch = jnp.dot(attended, full[4], preferred_element_type=jnp.float32) + full[5].astype(
        jnp.float32
    )
    middle = residual_in + branch
    second, scaled_two, inverse_two = norm_forward(middle, full[6], full[7])
    second_low = second.astype(jnp.bfloat16)
    hidden_pre = jnp.dot(second_low, full[8], preferred_element_type=jnp.float32) + full[9].astype(
        jnp.float32
    )
    active_low = jax.nn.gelu(hidden_pre, approximate=False).astype(jnp.bfloat16)
    branch_mlp = jnp.dot(active_low, full[10], preferred_element_type=jnp.float32) + full[
        11
    ].astype(jnp.float32)
    output = ((middle + branch_mlp) * live_rows[:, None]).astype(jnp.bfloat16)
    again = (
        lax.all_gather(norm_one_gain, "dp", axis=0, tiled=True),
        lax.all_gather(norm_one_bias, "dp", axis=0, tiled=True),
        lax.all_gather(joint_weight, "dp", axis=0, tiled=True),
        lax.all_gather(joint_bias, "dp", axis=0, tiled=True),
        lax.all_gather(merge_weight, "dp", axis=0, tiled=True),
        lax.all_gather(merge_bias, "dp", axis=0, tiled=True),
        lax.all_gather(norm_two_gain, "dp", axis=0, tiled=True),
        lax.all_gather(norm_two_bias, "dp", axis=0, tiled=True),
        lax.all_gather(expand_weight, "dp", axis=0, tiled=True),
        lax.all_gather(expand_bias, "dp", axis=0, tiled=True),
        lax.all_gather(shrink_weight, "dp", axis=0, tiled=True),
        lax.all_gather(shrink_bias, "dp", axis=0, tiled=True),
    )
    incoming = cotangent.astype(jnp.float32) * live_rows[:, None]
    incoming_low = incoming.astype(jnp.bfloat16)
    grad_shrink = jnp.einsum(
        "tf,to->fo", active_low, incoming_low, preferred_element_type=jnp.float32
    )
    grad_shrink_offset = jnp.sum(incoming_low.astype(jnp.float32), axis=0)
    grad_active = jnp.einsum(
        "to,fo->tf", incoming_low, again[10], preferred_element_type=jnp.float32
    )
    grad_hidden = (grad_active * gelu_slope(hidden_pre)).astype(jnp.bfloat16)
    grad_expand = jnp.einsum(
        "td,tf->df", second_low, grad_hidden, preferred_element_type=jnp.float32
    )
    grad_expand_offset = jnp.sum(grad_hidden.astype(jnp.float32), axis=0)
    grad_second = jnp.einsum("tf,df->td", grad_hidden, again[8], preferred_element_type=jnp.float32)
    back_two, grad_gain_two, grad_bias_two = norm_backward(
        grad_second, scaled_two, inverse_two, again[6]
    )
    grad_middle = incoming + back_two
    middle_low = grad_middle.astype(jnp.bfloat16)
    grad_merge = jnp.einsum("ti,to->io", attended, middle_low, preferred_element_type=jnp.float32)
    grad_merge_offset = jnp.sum(middle_low.astype(jnp.float32), axis=0)
    grad_attended = jnp.einsum(
        "to,io->ti", middle_low, again[4], preferred_element_type=jnp.float32
    )
    grad_attended = grad_attended.astype(jnp.bfloat16).reshape(row_count, head_count, HD)
    softmax_rows = jnp.exp(block_scores() - log_totals)
    grad_softmax = jnp.einsum(
        "qhd,khd->hqk", grad_attended, value_rows, preferred_element_type=jnp.float32
    )
    row_delta = jnp.sum(softmax_rows * grad_softmax, axis=-1, keepdims=True)
    grad_scores = (softmax_rows * (grad_softmax - row_delta) * score_scale).astype(jnp.bfloat16)
    grad_query_parts = jnp.einsum(
        "hqk,khd->qhd", grad_scores, key_rows, preferred_element_type=jnp.float32
    )
    grad_keys = jnp.einsum("hqk,qhd->khd", grad_scores, queries, preferred_element_type=jnp.float32)
    grad_values = jnp.einsum(
        "hqk,qhd->khd",
        softmax_rows.astype(jnp.bfloat16),
        grad_attended,
        preferred_element_type=jnp.float32,
    )
    grad_joint = jnp.concatenate(
        [
            grad_query_parts.reshape(row_count, model_width),
            grad_keys.reshape(row_count, model_width),
            grad_values.reshape(row_count, model_width),
        ],
        axis=1,
    ).astype(jnp.bfloat16)
    grad_joint_matrix = jnp.einsum(
        "td,tj->dj", first_low, grad_joint, preferred_element_type=jnp.float32
    )
    grad_joint_offset = jnp.sum(grad_joint.astype(jnp.float32), axis=0)
    grad_first = jnp.einsum("tj,dj->td", grad_joint, again[2], preferred_element_type=jnp.float32)
    back_one, grad_gain_one, grad_bias_one = norm_backward(
        grad_first, scaled_one, inverse_one, again[0]
    )
    grad_tokens = grad_middle + back_one
    grads_full = (
        grad_gain_one,
        grad_bias_one,
        grad_joint_matrix,
        grad_joint_offset,
        grad_merge,
        grad_merge_offset,
        grad_gain_two,
        grad_bias_two,
        grad_expand,
        grad_expand_offset,
        grad_shrink,
        grad_shrink_offset,
    )
    shares = (
        lax.psum_scatter(grads_full[0], "dp", scatter_dimension=0, tiled=True),
        lax.psum_scatter(grads_full[1], "dp", scatter_dimension=0, tiled=True),
        lax.psum_scatter(grads_full[2], "dp", scatter_dimension=0, tiled=True),
        lax.psum_scatter(grads_full[3], "dp", scatter_dimension=0, tiled=True),
        lax.psum_scatter(grads_full[4], "dp", scatter_dimension=0, tiled=True),
        lax.psum_scatter(grads_full[5], "dp", scatter_dimension=0, tiled=True),
        lax.psum_scatter(grads_full[6], "dp", scatter_dimension=0, tiled=True),
        lax.psum_scatter(grads_full[7], "dp", scatter_dimension=0, tiled=True),
        lax.psum_scatter(grads_full[8], "dp", scatter_dimension=0, tiled=True),
        lax.psum_scatter(grads_full[9], "dp", scatter_dimension=0, tiled=True),
        lax.psum_scatter(grads_full[10], "dp", scatter_dimension=0, tiled=True),
        lax.psum_scatter(grads_full[11], "dp", scatter_dimension=0, tiled=True),
    )
    totals = (
        lax.psum(shares[0].astype(jnp.bfloat16), "rep").astype(jnp.float32),
        lax.psum(shares[1].astype(jnp.bfloat16), "rep").astype(jnp.float32),
        lax.psum(shares[2].astype(jnp.bfloat16), "rep").astype(jnp.float32),
        lax.psum(shares[3].astype(jnp.bfloat16), "rep").astype(jnp.float32),
        lax.psum(shares[4].astype(jnp.bfloat16), "rep").astype(jnp.float32),
        lax.psum(shares[5].astype(jnp.bfloat16), "rep").astype(jnp.float32),
        lax.psum(shares[6].astype(jnp.bfloat16), "rep").astype(jnp.float32),
        lax.psum(shares[7].astype(jnp.bfloat16), "rep").astype(jnp.float32),
        lax.psum(shares[8].astype(jnp.bfloat16), "rep").astype(jnp.float32),
        lax.psum(shares[9].astype(jnp.bfloat16), "rep").astype(jnp.float32),
        lax.psum(shares[10].astype(jnp.bfloat16), "rep").astype(jnp.float32),
        lax.psum(shares[11].astype(jnp.bfloat16), "rep").astype(jnp.float32),
    )
    return (
        output,
        grad_tokens,
        totals[0],
        totals[1],
        totals[2],
        totals[3],
        totals[4],
        totals[5],
        totals[6],
        totals[7],
        totals[8],
        totals[9],
        totals[10],
        totals[11],
    )


def contract(a, b, dims):
    return lax.dot_general(a, b, dims, preferred_element_type=F32)


def matmul(a, b):
    return jnp.dot(a, b, preferred_element_type=F32)


def span(start, size):
    return pl.ds(start if isinstance(start, int) else pl.multiple_of(start, size), size)


def layer_kernel(dims, cuts, schedule, names, *args):
    r = dict(zip(names, args, strict=True))
    Z, Y, X = dims
    vec, cot = r["vec"], r["cot"]
    H0, N1, QKV, OA, H1, N2, G, DU, EB = (r[k] for k in ("H0", "N1", "QKV", "OA", "H1", "N2", "G", "DU", "EB"))
    SEG, L, V, XS, XR, OUTB, DA, VG, COL = (r[k] for k in ("SEG", "L", "V", "XS", "XR", "OUTB", "DA", "VG", "COL"))
    VGR, GM = r["VGR"], r["GM"]
    OS = XS.at[:, 0 : XS.shape[1] // 2]
    R, D = H0.shape
    half_heads = D // HD // 2
    HW = half_heads * HD
    FC = DU.shape[1]
    me = lax.axis_index("dp")
    c = lax.axis_index("rep")
    o = 1 - c
    x = lax.rem(me, X)
    y = lax.rem(me // X, Y)
    z = me // (X * Y)
    own = span(c * R, R)
    sib = span(o * R, R)

    def at(zz, yy, xx):
        return (zz * (Y * X) + yy * X + xx, c)

    def zplus(d):
        return lax.rem(z + d, Z)

    to_x, to_y, to_o = at(z, y, 1 - x), at(z, 1 - y, x), (me, o)
    to_z = [None] + [at(zplus(d), y, x) for d in range(1, Z)]
    up, down = to_z[1], to_z[Z - 1]
    z1, z2 = z + 1 - 2 * lax.rem(z, 2), lax.rem(z + 2, Z)
    to_z1, to_z2 = at(z1, y, x), at(z2, y, x)

    def remote(src, dst, ssem, rsem, to):
        return pltpu.make_async_remote_copy(
            src_ref=src, dst_ref=dst, send_sem=ssem, recv_sem=rsem, device_id=to, device_id_type=MESH
        )

    barrier = pltpu.get_barrier_semaphore()
    for to in to_z[1:] + [to_x, to_y, to_o]:
        pl.semaphore_signal(barrier, inc=1, device_id=to, device_id_type=MESH)
    W = {k: r["W" + k] for k in "jmxs"}
    blk = W["s"].shape[3]
    lnum = {k: i for i, k in enumerate("jmxset")}

    def qcols(hp, i):
        return pl.ds((3 * hp + i) * 2 * HD, 2 * HD)

    def local_copy(k, src, dst):
        pltpu.make_async_copy(src, dst, r["ls"].at[lnum[k]]).start()

    def local_wait(k, ref):
        pltpu.make_async_copy(ref, ref, r["ls"].at[lnum[k]]).wait()

    for i in range(3):
        for hp in range(half_heads // 2):
            src = r["wj"].at[:, span(i * D + c * HW + hp * 2 * HD, 2 * HD)]
            local_copy("j", src, W["j"].at[z, y, x, :, qcols(hp, i)])
    local_copy("m", r["wm"].at[:, span(c * HW, HW)], W["m"].at[z, y, x, :, span(c * HW, HW)])
    for i in range(FC // blk):
        local_copy("x", r["wx"].at[:, span(2 * blk * i + blk * c, blk)], W["x"].at[z, y, x, :, pl.ds(i * blk, blk)])
    local_copy("s", r["ws"].at[span(c * blk, blk), :], W["s"].at[z, y, x])
    local_copy("t", r["tok"], OUTB)
    local_copy("e", cot, EB.at[own, :])
    own_ref = {
        "j": W["j"].at[z, y, x],
        "m": W["m"].at[z, y, x, :, span(c * HW, HW)],
        "x": W["x"].at[z, y, x],
        "s": W["s"].at[z, y, x],
    }

    TAB = r["TAB"]
    TAB[z, y, x] = vec[...]
    pl.semaphore_wait(barrier, Z - 1 + 3)

    pair_sems = iter(range(r["ps"].shape[0]))

    def to_pair(src, dst):
        k = next(pair_sems)
        cp = remote(src, dst, r["ps"].at[k], r["pr"].at[k], to_o)
        cp.start()
        return cp

    def tab_send(ref, slot, to, src=None):
        cp = remote(src if src is not None else ref, ref, r["vs"].at[slot], r["vr"].at[slot], to)
        cp.start()
        return cp

    vcps = [tab_send(TAB.at[z, y, x], d - 1, to_z[d], vec) for d in range(1, Z)]
    order = "jmxs"
    num = {(k, p): 4 * i + p for i, k in enumerate(order) for p in range(4)}

    def gcols(k, p):
        start, size = cuts["gather"][k][p]
        return span(c * HW + start, size) if k == "m" else pl.ds(start, size)

    def block(k, p, zz, yy=slice(None), xx=slice(None)):
        return W[k].at[zz, yy, xx, :, gcols(k, p)]

    def send(ref, ssem, rsem, to):
        remote(ref, ref, ssem, rsem, to).start()

    def line_block(k, p, zz):
        return block(k, p, zz, y, x) if p < 2 else block(k, p, zz)

    def line_send(k, p, zz, way):
        n = num[k, p]
        send(line_block(k, p, zz), r["az"].at[n, way, zz], r["bz"].at[n, zz], (up, down)[way])

    def line_start(k, p):
        @pl.when(z < Z - 1)
        def _():
            line_send(k, p, z, 0)

        @pl.when(z > 0)
        def _():
            line_send(k, p, z, 1)

    def line_arrive(k, p, t, then):
        def take(zz, way, more):
            n = num[k, p]
            ref = line_block(k, p, zz)
            remote(ref, ref, r["az"].at[n, way, zz], r["bz"].at[n, zz], up).wait_recv()

            @pl.when(more)
            def _():
                line_send(k, p, zz, way)

            then(zz)

        @pl.when(z >= t)
        def _():
            take(z - t, 0, z < Z - 1)

        @pl.when(z + t < Z)
        def _():
            take(z + t, 1, z > 0)

    def spread(k, p, zz):
        n = num[k, p]
        a, b = (to_y, to_x) if p == 0 else (to_x, to_y)
        ref = block(k, p, zz, y, x)
        send(ref, r["a2"].at[n], r["b2"].at[n, zz], a)
        send(ref, r["a3"].at[n], r["b3"].at[n], b)

    def second(k, p, zz):
        n = num[k, p]
        a, b = (to_y, to_x) if p == 0 else (to_x, to_y)
        ref = block(k, p, zz, 1 - y, x) if p == 0 else block(k, p, zz, y, 1 - x)
        remote(ref, ref, r["a2"].at[n], r["b2"].at[n, zz], a).wait_recv()
        send(ref, r["a3"].at[n], r["b3"].at[n], b)

    def g_z0(k, p, t):
        line_start(k, p)

    def g_fz(k, p, t):
        if t == 0:
            spread(k, p, z)
        else:
            line_arrive(k, p, t, functools.partial(spread, k, p))

    def g_f2(k, p, t):
        if t == 0:
            second(k, p, z)
        else:

            @pl.when(z >= t)
            def _():
                second(k, p, z - t)

            @pl.when(z + t < Z)
            def _():
                second(k, p, z + t)

    def g_p0(k, p, t):
        n = num[k, p]
        a, b = (to_x, to_y) if p == 2 else (to_y, to_x)
        send(block(k, p, z, y, x), r["a2"].at[n], r["b2"].at[n, 0], a)
        send(block(k, p, z, y, x), r["a3"].at[n], r["b3"].at[n], b)

    def g_p1(k, p, t):
        n = num[k, p]
        a, b = (to_x, to_y) if p == 2 else (to_y, to_x)
        ref = block(k, p, z, y, 1 - x) if p == 2 else block(k, p, z, 1 - y, x)
        remote(ref, ref, r["a2"].at[n], r["b2"].at[n, 0], a).wait_recv()
        send(ref, r["a3"].at[n], r["b3"].at[n], b)

    def g_p2(k, p, t):
        n = num[k, p]
        ref = block(k, p, z, 1 - y) if p == 2 else block(k, p, z, slice(None), 1 - x)
        remote(ref, ref, r["a3"].at[n], r["b3"].at[n], to_y if p == 2 else to_x).wait_recv()
        line_start(k, p)

    def g_pz(k, p, t):
        line_arrive(k, p, t, lambda zz: None)

    def gather_wait(k):
        for p in (0, 1):
            n = num[k, p]
            ref = block(k, p, slice(None), slice(None), 0) if p == 0 else block(k, p, slice(None), 0)
            remote(ref, ref, r["a3"].at[n], r["b3"].at[n], to_x if p == 0 else to_y).wait_recv()

    def gather_done(k):
        for p in range(4):
            if not cuts["gather"][k][p][1]:
                continue
            n = num[k, p]
            every = slice(None)
            if p < 2:
                done = [(block(k, p, every, 0, 0), "a2"), (block(k, p, every, every, 0), "a3")]
            else:
                done = [(block(k, p, 0, 0, 0), "a2"), (block(k, p, 0, 0), "a3")]
            for ref, s in done:
                remote(ref, ref, r[s].at[n], r["b3"].at[n], to_x).wait_send()
            for t in range(Z):
                ref = line_block(k, p, t)

                @pl.when((z < Z - 1) & (t <= z))
                def _():
                    remote(ref, ref, r["az"].at[n, 0, t], r["bz"].at[n, t], up).wait_send()

                @pl.when((z > 0) & (t >= z))
                def _():
                    remote(ref, ref, r["az"].at[n, 1, t], r["bz"].at[n, t], down).wait_send()

    GS, GX, GJ = r["GS"], W["s"], W["x"]
    grad = {"s": GS, "t": GS, "x": GX, "u": GX, "m": GM, "j": GJ, "k": GJ, "l": GJ}
    gorder = "stxumjkl"
    gnum = {(k, p): 4 * i + p for i, k in enumerate(gorder) for p in range(4)}
    outs = {k: r["o" + v] for k, v in zip(gorder, "ssxxmjjj", strict=True)}

    def gslice(k, p):
        row, rows, begin, size = cuts["reduce"][k][p]
        return pl.ds(row, rows), span(c * HW + begin, size) if k == "m" else pl.ds(begin, size)

    def add_into(ref, idx, other):
        ref[idx] = (ref[idx].astype(F32) + other[...].astype(F32)).astype(BF16)

    def part(k, p, zz, yy, xx):
        return grad[k].at[(zz, yy, xx, *gslice(k, p))]

    every = slice(None)

    def part(k, p, zz, yy=every, xx=every):
        return grad[k].at[(zz, yy, xx, *gslice(k, p))]

    def buf(name, k, p):
        return r["%s%s%d" % (name, k, p)]

    def line_first(k, p, name, at_):
        n = gnum[k, p]
        return [
            remote(
                part(k, p, zz, *at_), buf(name, k, p).at[i], r["c" + name[1]].at[n, i], r["d" + name[1]].at[n, i], to_z1
            )
            for i, zz in enumerate((z1, lax.rem(z1 + 2, Z)))
        ]

    def line_last(k, p, name, at_):
        n = gnum[k, p]
        return [
            remote(
                part(k, p, z2, *at_), buf(name, k, p).at[2], r["c" + name[1]].at[n, 2], r["d" + name[1]].at[n, 2], to_z2
            )
        ]

    def s1(k, p):
        n = gnum[k, p]
        if p > 1:
            return line_first(k, p, "R1", ())
        src = part(k, p, every, every, 1 - x) if p == 0 else part(k, p, every, 1 - y)
        return [remote(src, buf("R1", k, p), r["c1"].at[n, 0], r["d1"].at[n, 0], to_x if p == 0 else to_y)]

    def s1b(k, p):
        return line_last(k, p, "R1", ()) if p > 1 else []

    def s2(k, p):
        n = gnum[k, p]
        src, to = {
            0: lambda: (part(k, p, every, 1 - y, x), to_y),
            1: lambda: (part(k, p, every, y, 1 - x), to_x),
            2: lambda: (part(k, p, z, 1 - y), to_y),
            3: lambda: (part(k, p, z, every, 1 - x), to_x),
        }[p]()
        return [remote(src, buf("R2", k, p), r["c2"].at[n], r["d2"].at[n], to)]

    def s3(k, p):
        n = gnum[k, p]
        if p < 2:
            return line_first(k, p, "R3", (y, x))
        src, to = (part(k, p, z, y, 1 - x), to_x) if p == 2 else (part(k, p, z, 1 - y, x), to_y)
        return [remote(src, buf("R3", k, p).at[0], r["c3"].at[n, 0], r["d3"].at[n, 0], to)]

    def s3b(k, p):
        return line_last(k, p, "R3", (y, x)) if p < 2 else []

    def start(copies):
        for cp in copies:
            cp.start()

    def arrived(copies):
        for cp in copies:
            cp.wait_recv()

    def r_S1(k, p, t):
        start(s1(k, p))

    def goes_and_stays(k, p):
        for q in (1, 0):
            yield q, [(1 - y if q else y, i) if p == 2 else (i, 1 - x if q else x) for i in range(2)]

    def r_A1(k, p, t):
        arrived(s1(k, p))
        R1, sl = buf("R1", k, p), gslice(k, p)
        if p > 1:
            for i in range(Y * X):
                add_into(grad[k], (z2, i // X, i % X, *sl), R1.at[1, i // X, i % X])
            start(s1b(k, p))
            return
        for q in (1, 0):
            yy = y if q == 0 else 1 - y
            xx = x if q == 0 else 1 - x

            def one(i, _):
                if p == 0:
                    add_into(grad[k], (i, yy, x, *sl), R1.at[i, yy])
                else:
                    add_into(grad[k], (i, y, xx, *sl), R1.at[i, xx])
                return 0

            lax.fori_loop(0, Z, one, 0)
            if q == 1:
                start(s2(k, p))

    def r_A2(k, p, t):
        sl = gslice(k, p)
        if p < 2:
            arrived(s2(k, p))
            R2 = buf("R2", k, p)
            for zz in (z1, lax.rem(z1 + 2, Z)):
                add_into(grad[k], (zz, y, x, *sl), R2.at[zz])
            start(s3(k, p))
            for zz in (z, z2):
                add_into(grad[k], (zz, y, x, *sl), R2.at[zz])
            return
        arrived(s1b(k, p))
        R1 = buf("R1", k, p)
        for q, places in goes_and_stays(k, p):
            for yy, xx in places:
                idx = (z, yy, xx, *sl)
                tot = grad[k][idx].astype(F32) + R1[0, yy, xx].astype(F32) + R1[2, yy, xx].astype(F32)
                grad[k][idx] = tot.astype(BF16)
            if q == 1:
                start(s2(k, p))

    def r_A3(k, p, t):
        sl = gslice(k, p)
        if p < 2:
            arrived(s3(k, p))
            add_into(grad[k], (z2, y, x, *sl), buf("R3", k, p).at[1])
            start(s3b(k, p))
            return
        arrived(s2(k, p))
        R2 = buf("R2", k, p)
        for q in (1, 0):
            yy, xx = (y, 1 - x if q else x) if p == 2 else (1 - y if q else y, x)
            add_into(grad[k], (z, yy, xx, *sl), R2.at[xx if p == 2 else yy])
            if q == 1:
                start(s3(k, p))

    def r_A4(k, p, t):
        arrived(s3b(k, p) if p < 2 else s3(k, p))
        R3 = buf("R3", k, p)
        idx = (z, y, x, *gslice(k, p))
        tot = grad[k][idx].astype(F32) + R3[0].astype(F32)
        if p < 2:
            tot = tot + R3[2].astype(F32)
        grad[k][idx] = tot.astype(BF16)

    fin_copies = []

    def r_F(k, p, t):
        i = gorder.index(k)
        row, rows, begin, size = cuts["reduce"][k][0]
        size = sum(q[3] for q in cuts["reduce"][k])
        rs = pl.ds(row, rows)
        total = grad[k].at[z, y, x, rs, span(c * HW + begin, size) if k == "m" else pl.ds(begin, size)]
        dst = outs[k].at[c, rs, pl.ds(begin, size)]
        a = pltpu.make_async_copy(total, dst, r["fl"].at[i])
        b = remote(total, dst, r["fs"].at[i], r["fr"].at[i], to_o)
        a.start()
        b.start()
        fin_copies.extend([a, b])

    TQ, TR = 256, 256
    FT = Y * X * blk // 2
    DT = Y * X * W["j"].shape[3]
    copies = {}
    lane = lax.broadcasted_iota(jnp.int32, (1, 2 * HD), 1) // HD

    def normed(h):
        center = h - jnp.mean(h, axis=-1, keepdims=True)
        inverse = lax.rsqrt(jnp.mean(center * center, axis=-1, keepdims=True) + 1e-06)
        return center * inverse, inverse

    def c_rows():
        slots = r["len"].shape[1]
        sub = lax.broadcasted_iota(jnp.int32, (slots, slots), 0)
        lan = lax.broadcasted_iota(jnp.int32, (slots, slots), 1)
        lens, dist = r["len"][...].astype(F32), r["dist"][...].astype(F32)
        ends = jnp.sum(jnp.where(lan <= sub, lens, 0.0), axis=1, keepdims=True)
        dist = jnp.sum(jnp.where(lan == sub, dist, 0.0), axis=1, keepdims=True)
        places = lax.broadcasted_iota(jnp.int32, (slots, R), 1).astype(F32)
        segment = jnp.sum(jnp.where(ends <= places, 1.0, 0.0), axis=0, keepdims=True)
        slot = lax.broadcasted_iota(jnp.int32, (slots, R), 0).astype(F32)
        ground = jnp.sum(jnp.where(slot == segment, dist, 0.0), axis=0, keepdims=True)
        alive = jnp.where(segment < slots, 1.0, 0.0)
        factor = ground / 10.0
        patch = r["patch"][...].astype(F32)
        patch = jnp.concatenate([patch[i : i + 1] for i in range(R // 128)], axis=1)
        down_ = jnp.floor((patch + 0.5) * (1.0 / 14.0))
        along = patch - 14.0 * down_
        zero = jnp.zeros_like(factor)
        rows = jnp.concatenate([segment, alive, down_ * factor, along * factor, zero, zero, zero, zero], axis=0)
        SEG[c] = rows
        COL[...] = jnp.transpose(rows)
        copies["seg"] = to_pair(SEG.at[c], SEG.at[c])

    def c_v1():
        for cp in vcps:
            cp.wait()
        copies["vy"] = tab_send(TAB.at[:, y, x], Z - 1, to_y)

    def c_v2():
        copies["vy"].wait()
        copies["vx"] = tab_send(TAB.at[:, :, x], Z, to_x)

    def c_v3():
        copies["vx"].wait()
        VG[...] = jnp.zeros_like(VG)
        count = Z * Y * X
        n, nj = D // count, 3 * D // count
        flat = TAB[...].reshape(count * 8, 128)
        table = flat.astype(BF16)
        for s_ in range(count):
            f = s_ * blk
            piece = TAB[s_ // (Y * X), s_ // X % Y, s_ % X, pl.ds(c, 1), :]
            V[8 + f // D : 9 + f // D, f % D : f % D + blk] = piece
        wide = 4 * 128
        key = lax.broadcasted_iota(jnp.int32, (128, wide), 0).astype(F32)
        row = lax.broadcasted_iota(jnp.int32, (count * 8, wide), 0).astype(F32)
        column = lax.broadcasted_iota(jnp.int32, (1, wide), 1).astype(F32)

        def spread_out(shard, entry, first):
            spot = entry + first
            line = jnp.floor((spot + 0.5) * (1.0 / 128))
            pick = jnp.where(key == spot - 128.0 * line, 1.0, 0.0).astype(BF16)
            tiled = matmul(table, pick)
            return jnp.sum(jnp.where(row == 8.0 * shard + line, tiled, 0.0), axis=0, keepdims=True)

        for a in range(0, D, wide):
            shard = jnp.floor((column + (a + 0.5)) * (1.0 / n))
            for i in range(6):
                V[i : i + 1, a : a + wide] = spread_out(shard, column + a - n * shard, 2 * blk + nj + i * n)
        for a in range(0, 3 * HW, wide):
            tile = jnp.floor((column + (a + 0.5)) * (1.0 / 128))
            hp = jnp.floor((tile + 0.5) * (1.0 / 3))
            which = tile - 3.0 * hp
            of = which * D + c.astype(F32) * HW + hp * 128.0 + (column + a - 128.0 * tile)
            shard = jnp.floor((of + 0.5) * (1.0 / nj))
            V[6 + a // D : 7 + a // D, a % D : a % D + wide] = spread_out(shard, of - nj * shard, 2 * blk)

    def c_h0():
        local_wait("t", OUTB)
        local_wait("e", EB.at[own, :])

        def rows128(i, _):
            rr, gr = span(i * 128, 128), span(c * R + i * 128, 128)
            EB[gr, :] = (EB[gr, :].astype(F32) * COL[rr, 1:2]).astype(BF16)
            Q = D // 4
            for j in (0, 1):
                angle = COL[rr, 2 + j : 3 + j] * r["freq"][...]
                at_ = 2 * j * Q
                H0[rr, at_ : at_ + Q] = OUTB[rr, at_ : at_ + Q].astype(F32) + jnp.sin(angle)
                at_ += Q
                H0[rr, at_ : at_ + Q] = OUTB[rr, at_ : at_ + Q].astype(F32) + jnp.cos(angle)
            return 0

        lax.fori_loop(0, R // 128, rows128, 0)
        copies["eb"] = to_pair(EB.at[own, :], EB.at[own, :])

    def c_ln1():
        def norm_one(i, _):
            rr, gr = span(i * 128, 128), span(c * R + i * 128, 128)
            scaled, _i = normed(H0[rr, :])
            N1[gr, :] = (scaled * V[0:1, :] + V[1:2, :]).astype(BF16)
            VG[5:6, :] += jnp.sum(EB[gr, :].astype(F32), axis=0, keepdims=True)
            return 0

        lax.fori_loop(0, R // 128, norm_one, 0)
        copies["n1"] = to_pair(N1.at[own, :], N1.at[own, :])

    def c_qkv(t):
        if t == 0:
            copies["seg"].wait()
            copies["n1"].wait()
            copies["eb"].wait()
            gather_wait("j")
        w = W["j"][:, :, :, :, t * TQ : (t + 1) * TQ].reshape(D, TQ)
        f = t * TQ
        b = V[6 + f // D : 7 + f // D, f % D : f % D + TQ]
        QKV[:, f : f + TQ] = (matmul(N1[...], w) + b).astype(BF16)

    def same_image(g):
        return jnp.transpose(SEG[g])[:, 0:1] == SEG[g, 0:1, :]

    def attend(g, hp):
        rr = span(g * R, R)
        q, k, v = (QKV[rr, qcols(hp, i)] for i in range(3))
        same = same_image(g)
        res = []
        for i in (0, 1):
            qi = jnp.where(lane == i, q.astype(F32) * HD**-0.5, 0.0).astype(BF16)
            s = jnp.where(same, contract(k, qi, LAST), NEVER)
            top = jnp.max(s, axis=0, keepdims=True)
            e = jnp.exp(s - top)
            tot = jnp.sum(e, axis=0, keepdims=True)
            L[g * half_heads + 2 * hp + i] = top + jnp.log(tot)
            pb = (e * (1.0 / tot)).astype(BF16)
            res.append(contract(v, pb, FIRST)[i * HD : (i + 1) * HD])
        return jnp.transpose(jnp.concatenate(res, axis=0)).astype(BF16)

    pairs = half_heads // 2

    def c_at(i):
        if i < pairs:
            OS[:, 2 * HD * i : 2 * HD * (i + 1)] = attend(o, i)
            if i == pairs - 1:
                copies["o"] = to_pair(OS, OA.at[:, span(c * HW, HW)])
        else:
            OA[:, span(c * HW + 2 * HD * (i - pairs), 2 * HD)] = attend(c, i - pairs)

    def c_wm():
        gather_wait("m")
        half = W["m"].at[:, :, :, :, span(c * HW, HW)]
        copies["wm"] = to_pair(half, half)

    def c_mrg():
        copies["o"].wait()
        copies["wm"].wait()
        for t in range(R // TR):
            rr = pl.ds(t * TR, TR)
            h1 = H0[rr, :] + matmul(OA[rr, :], W["m"][...].reshape(D, D)) + V[2:3, :]
            H1[rr, :] = h1
            scaled, _i = normed(h1)
            N2[span(c * R + t * TR, TR), :] = (scaled * V[3:4, :] + V[4:5, :]).astype(BF16)
        copies["n2"] = to_pair(N2.at[own, :], N2.at[own, :])

    def c_ge(t):
        if t == 0:
            copies["n2"].wait()
            gather_wait("x")
        cc = slice(t * TQ, (t + 1) * TQ)
        f = t * TQ
        b = V[8 + f // D : 9 + f // D, f % D : f % D + TQ]
        for h in range(2):
            rr = slice(h * R, (h + 1) * R)
            u = matmul(N2[rr, :], W["x"][:, :, :, :, cc].reshape(D, TQ)) + b
            cdf = 0.5 * (1.0 + lax.erf(u * 0.7071067811865476))
            G[rr, cc] = (u * cdf).astype(BF16)
            DU[rr, cc] = (cdf + u * (jnp.exp(-0.5 * u * u) * 0.3989422804014327)).astype(BF16)

    def c_gs(i):
        for t in (2 * i, 2 * i + 1):
            g = contract(G[:, t * FT : (t + 1) * FT], EB[...], FIRST)
            GS[t // Y, t % Y] = g.astype(BF16).reshape(X, blk, D)

    def c_du(i):
        if i == 0:
            gather_wait("s")
        for t in (2 * i, 2 * i + 1):
            cc = slice(t * FT, (t + 1) * FT)
            w = W["s"][t // Y, t % Y].reshape(FT, D)
            row, col = 8 + t * FT // D, t * FT % D
            for h in range(2):
                rr = slice(h * R, (h + 1) * R)
                du = (contract(EB[rr, :], w, LAST) * DU[rr, cc].astype(F32)).astype(BF16)
                DU[rr, cc] = du
                VG[row : row + 1, col : col + FT] += jnp.sum(du.astype(F32), axis=0, keepdims=True)

    def c_h2s():
        for t in range(D // TQ):
            cc = slice(t * TQ, (t + 1) * TQ)
            XS[:, cc] = matmul(G[sib, :], W["s"][:, :, :, :, cc].reshape(FC, TQ)).astype(BF16)
        copies["h2"] = to_pair(XS, OUTB)

    def c_h2o():
        copies["h2"].wait_recv()
        for t in range(D // TQ):
            cc = slice(t * TQ, (t + 1) * TQ)
            own_part = matmul(G[own, :], W["s"][:, :, :, :, cc].reshape(FC, TQ))
            OUTB[:, cc] = (
                (H1[:, cc] + own_part + OUTB[:, cc].astype(F32) + V[5:6, cc]) * COL[:, 1:2]
            ).astype(BF16)
        copies["out"] = pltpu.make_async_copy(OUTB, r["out"], r["fl"].at[len(gorder)])
        copies["out"].start()
        gather_done("s")

    def back_part(left, wk, n, name, dst):
        for t in range(Z):
            w = wk[t][:, :, :, 0:n].reshape(DT, n)
            dst[:, t * DT : (t + 1) * DT] = contract(left[sib, 0:n], w, LAST).astype(BF16)
        copies[name] = to_pair(dst, XR)

    def c_dn2s():
        back_part(DU, W["x"], FC, "dn2", DA)

    def c_gx(i):
        h, half = W["j"].shape[3], FC // 2
        for t in range(Z):
            g = contract(N2[:, t * DT : (t + 1) * DT], DU[:, i * half : (i + 1) * half], FIRST)
            GX[t, :, :, i * h : (i + 1) * h, :] = g.astype(BF16).reshape(Y, X, h, half)

    def norm_back(dy, scaled, inverse, gain, vg):
        ds_ = dy * gain
        VG[vg : vg + 1, :] += jnp.sum(dy * scaled, axis=0, keepdims=True)
        VG[vg + 1 : vg + 2, :] += jnp.sum(dy, axis=0, keepdims=True)
        cen = ds_ - jnp.mean(ds_, axis=-1, keepdims=True)
        cen = cen - scaled * jnp.mean(ds_ * scaled, axis=-1, keepdims=True)
        return cen * inverse

    def c_dn2o():
        copies["dn2"].wait()
        for t in range(R // TR):
            rr, gr = pl.ds(t * TR, TR), span(c * R + t * TR, TR)
            dy = contract(DU[gr, :], W["x"][...].reshape(D, FC), LAST) + XR[rr, :].astype(F32)
            scaled, inverse = normed(H1[rr, :])
            dh = EB[gr, :].astype(F32) + norm_back(dy, scaled, inverse, V[3:4, :], 3)
            H1[rr, :] = dh
            DA[rr, :] = dh.astype(BF16)
            VG[2:3, :] += jnp.sum(DA[rr, :].astype(F32), axis=0, keepdims=True)
        gather_done("x")

    def c_dO():
        copies["h2"].wait_send()
        cw = X * W["m"].shape[3]
        for t, base in enumerate((o, c)):
            for u in range(HW // cw):
                w = W["m"][base * (Z // 2) + u // Y, u % Y].reshape(cw, D)
                res = contract(DA[...], w, LAST).astype(BF16)
                if t == 0:
                    OS[:, u * cw : (u + 1) * cw] = res
                else:
                    G[own, 3 * HW + u * cw : 3 * HW + (u + 1) * cw] = res
            if t == 0:
                copies["do"] = to_pair(OS, G.at[own, pl.ds(3 * HW, HW)])
        gather_done("m")

    def c_gm():
        for t in range(Z):
            g = contract(OA[:, t * DT : (t + 1) * DT], DA[...], FIRST)
            GM[t] = g.astype(BF16).reshape(Y, X, W["m"].shape[3], D)
        copies["gm"] = to_pair(GM.at[:, :, :, :, span(o * HW, HW)], r["GMR"])

    def c_gma():
        copies["gm"].wait()

        def add_pair(i, _):
            for j in range(Y * X):
                idx = (i, j // X, j % X, slice(None), span(c * HW, HW))
                add_into(GM, idx, r["GMR"].at[i, j // X, j % X])
            return 0

        lax.fori_loop(0, Z, add_pair, 0)

    def attend_back(g, hp):
        rr = span(g * R, R)
        qc, kc, vc = (qcols(hp, i) for i in range(3))
        q, k, v = QKV[rr, qc], QKV[rr, kc], QKV[rr, vc]
        do = G[rr, 3 * HW + hp * 2 * HD : 3 * HW + (hp + 1) * 2 * HD]
        same = same_image(g)
        dq, dk, dv = [], [], []
        for i in (0, 1):
            qi = jnp.where(lane == i, q.astype(F32) * HD**-0.5, 0.0).astype(BF16)
            di = jnp.where(lane == i, do.astype(F32), 0.0).astype(BF16)
            s = jnp.where(same, contract(k, qi, LAST), NEVER)
            pr = jnp.exp(s - L[g * half_heads + 2 * hp + i])
            dp = contract(v, di, LAST)
            delta = jnp.sum(pr * dp, axis=0, keepdims=True)
            dsb = (pr * (dp - delta) * HD**-0.5).astype(BF16)
            dq.append(contract(k, dsb, FIRST)[i * HD : (i + 1) * HD])
            dk.append(matmul(dsb, q))
            dv.append(matmul(pr.astype(BF16), do))
        G[rr, qc] = jnp.transpose(jnp.concatenate(dq, axis=0)).astype(BF16)
        G[rr, kc] = jnp.where(lane == 0, dk[0], dk[1]).astype(BF16)
        G[rr, vc] = jnp.where(lane == 0, dv[0], dv[1]).astype(BF16)

    few = pairs // 2
    back_order = [(c, hp) for hp in range(few)] + [(o, hp) for hp in range(few)]
    back_order += [(g, hp) for hp in range(few, pairs) for g in (c, o)]

    def c_ab(i):
        if i == few:
            copies["do"].wait()
        attend_back(*back_order[i])

    def c_gj(i):
        row, rows, begin, size = cuts["reduce"]["jkl"[i]][0]
        size = sum(q[3] for q in cuts["reduce"]["jkl"[i]])
        for t in range(Z):
            g = contract(N1[:, t * DT : (t + 1) * DT], G[:, begin : begin + size], FIRST)
            GJ[t, :, :, :, begin : begin + size] = g.astype(BF16).reshape(Y, X, rows, size)

    def c_dn1s():
        back_part(G, W["j"], 3 * HW, "dn1", XS)
        for t in range(3):
            row, col = 6 + t * HW // D, t * HW % D
            VG[row : row + 1, col : col + HW] += jnp.sum(
                G[:, t * HW : (t + 1) * HW].astype(F32), axis=0, keepdims=True
            )

    def c_dn1o():
        copies["dn1"].wait()
        for t in range(R // TR):
            rr, gr = pl.ds(t * TR, TR), span(c * R + t * TR, TR)
            dy = contract(G[gr, 0 : 3 * HW], W["j"][...].reshape(D, 3 * HW), LAST) + XR[rr, :].astype(F32)
            scaled, inverse = normed(H0[rr, :])
            H1[rr, :] = H1[rr, :] + norm_back(dy, scaled, inverse, V[0:1, :], 0)
        copies["gt"] = pltpu.make_async_copy(H1, r["gt"], r["fl"].at[len(gorder) + 1])
        copies["gt"].start()
        gather_done("j")

    def vg_send(slot, to):
        cp = remote(VG, VGR.at[slot], r["gs"].at[slot], r["gr"].at[slot], to)
        cp.start()
        return cp

    def vg_add(slots):
        acc = VG[...]
        for i in slots:
            acc = acc + VGR[i]
        VG[...] = acc

    def c_vz():
        copies["gz"] = [vg_send(d - 1, to_z[d]) for d in range(1, Z)]

    def c_vx():
        for cp in copies["gz"]:
            cp.wait()
        vg_add(range(Z - 1))
        copies["gx"] = vg_send(Z - 1, to_x)

    def c_vy():
        copies["gx"].wait()
        vg_add([Z - 1])
        copies["gy"] = vg_send(Z, to_y)

    def c_vp():
        copies["gy"].wait()
        vg_add([Z])
        copies["ov"] = pltpu.make_async_copy(VG, r["ov"].at[c], r["fl"].at[len(gorder) + 2])
        copies["ov"].start()
        copies["ovr"] = to_pair(VG, r["ov"].at[c])

    def c_end():
        for k in gorder:
            for p in range(4):
                if cuts["reduce"][k][p][3]:
                    for cp in s1(k, p) + s1b(k, p) + s2(k, p) + s3(k, p) + s3b(k, p):
                        cp.wait_send()
        for cp in fin_copies + [copies[n] for n in ("out", "gt", "ov", "ovr")]:
            cp.wait()

    steps = locals()
    landed = set()
    for word in schedule:
        if word[0] == "_":
            name = word[1:].rstrip("0123456789")
            if name in ("v", "h", "ln"):
                name = word[1:]
            arg = word[1 + len(name) :]
            steps["c_" + name](*([int(arg)] if arg else []))
            continue
        op, k, p, t = word[:2], word[2], int(word[3]), int(word[4])
        if op in ("z0", "p0", "fz") and t == 0 and k not in landed:
            landed.add(k)
            local_wait(k, own_ref[k])
        steps[("r_" if op[0] in "SAF" else "g_") + op.rstrip("_")](k, p, t)


def finish_kernel(dims, names, *args):
    r = dict(zip(names, args, strict=True))
    N = dims[0] * dims[1] * dims[2]
    taken = [
        pltpu.make_async_copy(r[n], r["v_" + n], r["sem"].at[i])
        for i, n in enumerate(("out", "gt", "oj", "om", "ox", "os", "ov"))
    ]
    for cp in taken:
        cp.start()
    big = [
        pltpu.make_async_copy(r["v_" + n], r["f_" + n], r["sem"].at[7 + i]) for i, n in enumerate(("out", "gt"))
    ]
    for i, cp in enumerate(taken):
        cp.wait()
        if i < 2:
            big[i].start()
    r.update({n: r["v_" + n] for n in ("oj", "om", "ox", "os", "ov")})
    rj, D = r["f_m"].shape
    HW, P2 = D // 2, 2 * HD
    blk = r["os"].shape[1]
    half = r["ox"].shape[2]
    for core in (0, 1):
        for hp in range(HW // P2):
            for i in range(3):
                to, of = i * D + core * HW + hp * P2, (3 * hp + i) * P2
                r["f_j"][:, to : to + P2] = r["oj"][core, :, of : of + P2].astype(F32)
        r["f_m"][:, core * HW : (core + 1) * HW] = r["om"][core].astype(F32)
        for i in range(2 * half // blk):
            row, col = i * blk // half * rj, i * blk % half
            to = (2 * i + core) * blk
            r["f_x"][:, to : to + blk] = r["ox"][core, row : row + rj, col : col + blk].astype(F32)
        r["f_s"][core * blk : (core + 1) * blk, :] = r["os"][core].astype(F32)
    me = lax.axis_index("dp")
    ov = r["ov"]
    both = ov[0, 0:8, :] + ov[1, 0:8, :]

    def mine(row, n):
        return pltpu.roll(row, (N - me) * n, 1)[:, :n]

    for i, name in enumerate(("g1", "b1", "mb", "g2", "b2", "sb")):
        r["f_" + name][...] = mine(jnp.broadcast_to(both[i : i + 1], (8, D)), D // N)[0:1]
    at_ = [((3 * hp + i) * P2, core) for i in range(3) for core in (0, 1) for hp in range(HW // P2)]
    row = jnp.concatenate([ov[core, 6 + a // D : 7 + a // D, a % D : a % D + P2] for a, core in at_], axis=1)
    r["f_jb"][...] = mine(jnp.broadcast_to(row, (8, 3 * D)), 3 * D // N)[0:1]
    for core in (0, 1):
        row = jnp.concatenate([ov[core, 8 + i : 9 + i, :] for i in range(2 * half // D)], axis=1)
        r["f_xb"][:, core * blk : (core + 1) * blk] = mine(jnp.broadcast_to(row, (8, 2 * half)), blk)[0:1]
    for cp in big:
        cp.wait()


def tiled_cuts(tiles):
    starts = [sum(tiles[:p]) * 128 for p in range(4)]
    return [(start, n * 128) for start, n in zip(starts, tiles, strict=True)]


def paths(rows, row, begin, tiles):
    return [(row, rows, begin + start, size) for start, size in tiled_cuts(tiles)]


def fused_layer(dims, *args):
    (
        tokens,
        kept_patch,
        image_lengths,
        ground_distance,
        cotangent,
        norm_one_gain,
        norm_one_bias,
        joint_weight,
        joint_bias,
        merge_weight,
        merge_bias,
        norm_two_gain,
        norm_two_bias,
        expand_weight,
        expand_bias,
        shrink_weight,
        shrink_bias,
    ) = args
    Z, Y, X = dims
    N = Z * Y * X
    R, D = tokens.shape
    FF = expand_weight.shape[1]
    HW, FC, blk = D // 2, FF // 2, shrink_weight.shape[0] // 2
    rj = joint_weight.shape[0]
    pieces = [expand_bias, joint_bias, norm_one_gain, norm_one_bias, merge_bias, norm_two_gain, norm_two_bias, shrink_bias]
    vec, begin = jnp.zeros((8 * 128,), F32), 0
    for v in pieces:
        vec = vec + jnp.pad(v.astype(F32), (begin, 8 * 128 - begin - v.shape[0]))
        begin += v.shape[0]
    vec = vec.reshape(8, 128)
    quarter = D // 4
    freq = 1.0 / np.float32(10000.0) ** (np.arange(quarter, dtype=np.float32) / np.float32(quarter))

    cuts = {
        "gather": {k: tiled_cuts(tiles) for k, tiles in GATHER.items()},
        "reduce": {
            "s": paths(blk, 0, 0, REDUCE["s"]),
            "t": paths(blk, 0, D // 2, REDUCE["t"]),
            "x": paths(rj, 0, 0, REDUCE["x"]),
            "u": paths(rj, rj, 0, REDUCE["u"]),
            "m": paths(rj, 0, 0, REDUCE["m"]),
            "j": paths(rj, 0, 0, REDUCE["j"]),
            "k": paths(rj, 0, 3 * HW // 2, REDUCE["k"]),
            "l": paths(rj, 0, 9 * HW // 4, REDUCE["l"]),
        },
    }

    vm, hbm = pl.BlockSpec(memory_space=pltpu.VMEM), pl.BlockSpec(memory_space=pl.ANY)
    ins = [("patch", kept_patch.reshape(R // 128, 128), vm), ("len", image_lengths, vm), ("dist", ground_distance, vm)]
    ins += [("freq", jnp.asarray(freq[None, :], F32), vm), ("vec", vec, vm), ("tok", tokens, hbm), ("cot", cotangent, hbm)]
    ins += [("wj", joint_weight, hbm), ("wm", merge_weight, hbm), ("wx", expand_weight, hbm), ("ws", shrink_weight, hbm)]
    S = jax.ShapeDtypeStruct
    outs = [
        ("out", S((R, D), BF16), hbm),
        ("gt", S((R, D), F32), hbm),
        ("oj", S((2, rj, 3 * HW), BF16), hbm),
        ("om", S((2, rj, HW), BF16), hbm),
        ("ox", S((2, 2 * rj, FC // 2), BF16), hbm),
        ("os", S((2, blk, D), BF16), hbm),
        ("ov", S((2, 16, D), F32), hbm),
    ]
    V = pltpu.VMEM
    dma = pltpu.SemaphoreType.DMA
    scratch = [
        ("Wj", V((Z, Y, X, rj, 3 * HW), BF16)),
        ("Wm", V((Z, Y, X, rj, D), BF16)),
        ("Wx", V((Z, Y, X, rj, FC), BF16)),
        ("Ws", V((Z, Y, X, blk, D), BF16)),
        ("GS", V((Z, Y, X, blk, D), BF16)),
        ("GM", V((Z, Y, X, rj, D), BF16)),
        ("GMR", V((Z, Y, X, rj, HW), BF16)),
        ("H0", V((R, D), F32)),
        ("N1", V((2 * R, D), BF16)),
        ("QKV", V((2 * R, 3 * HW), BF16)),
        ("OA", V((R, D), BF16)),
        ("H1", V((R, D), F32)),
        ("N2", V((2 * R, D), BF16)),
        ("G", V((2 * R, FC), BF16)),
        ("DU", V((2 * R, FC), BF16)),
        ("EB", V((2 * R, D), BF16)),
        ("SEG", V((2, 8, R), F32)),
        ("COL", V((R, 8), F32)),
        ("L", V((D // HD, 1, R), F32)),
        ("V", V((16, D), F32)),
        ("TAB", V((Z, Y, X, 8, 128), F32)),
        ("VG", V((16, D), F32)),
        ("VGR", V((Z + 1, 16, D), F32)),
        ("XS", V((R, D), BF16)),
        ("XR", V((R, D), BF16)),
        ("OUTB", V((R, D), BF16)),
        ("DA", V((R, D), BF16)),
    ]
    for k, four in cuts["reduce"].items():
        for p, (_, n, _, w) in enumerate(four):
            if w:
                first = (Z, 2) if p < 2 else (3, Y, X)
                second, third = ((Z,), (3,)) if p < 2 else ((2,), (1,))
                for name, lead in (("R1", first), ("R2", second), ("R3", third)):
                    scratch.append(("%s%s%d" % (name, k, p), V((*lead, n, w), BF16)))
    for name, shape in (
        ("ps", (12,)),
        ("pr", (12,)),
        ("vs", (Z + 1,)),
        ("vr", (Z + 1,)),
        ("gs", (Z + 1,)),
        ("gr", (Z + 1,)),
        ("ls", (6,)),
        ("az", (16, 2, Z)),
        ("bz", (16, Z)),
        ("a2", (16,)),
        ("b2", (16, Z)),
        ("a3", (16,)),
        ("b3", (16,)),
        ("c1", (32, 3)),
        ("d1", (32, 3)),
        ("c2", (32,)),
        ("d2", (32,)),
        ("c3", (32, 3)),
        ("d3", (32, 3)),
        ("fl", (11,)),
        ("fs", (8,)),
        ("fr", (8,)),
    ):
        scratch.append((name, dma(shape)))
    names = [n for n, *_ in ins + outs + scratch]
    res = pl.pallas_call(
        functools.partial(layer_kernel, dims, cuts, SCHEDULE, names),
        out_shape=[s for _, s, _ in outs],
        in_specs=[s for _, _, s in ins],
        out_specs=[s for _, _, s in outs],
        scratch_shapes=[s for _, s in scratch],
        compiler_params=pltpu.CompilerParams(
            collective_id=0, has_side_effects=True, vmem_limit_bytes=VMEM_BYTES
        ),
    )(*[a for _, a, _ in ins])

    far = pl.BlockSpec(memory_space=pltpu.HBM)
    given = [(n, a, far) for (n, _, _), a in zip(outs, res, strict=True)]
    made = [("f_out", S((R, D), BF16), far), ("f_gt", S((R, D), F32), far)]
    made += [("f_" + n, S((1, D // N), F32), vm) for n in ("g1", "b1", "mb", "g2", "b2", "sb")]
    made += [("f_jb", S((1, 3 * D // N), F32), vm), ("f_xb", S((1, FF // N), F32), vm)]
    made += [("f_j", S((rj, 3 * D), F32), vm), ("f_m", S((rj, D), F32), vm)]
    made += [("f_x", S((rj, FF), F32), vm), ("f_s", S((2 * blk, D), F32), vm)]
    last = pl.pallas_call(
        functools.partial(finish_kernel, dims, [n for n, *_ in given + made] + ["v_" + n for n, *_ in outs] + ["sem"]),
        out_shape=[s for _, s, _ in made],
        in_specs=[s for _, _, s in given],
        out_specs=[s for _, _, s in made],
        scratch_shapes=[V(s.shape, s.dtype) for _, s, _ in outs] + [dma((9,))],
        compiler_params=pltpu.CompilerParams(vmem_limit_bytes=VMEM_BYTES),
    )(*[a for _, a, _ in given])
    f = {n[2:]: a for (n, *_), a in zip(made, last, strict=True)}
    g1, b1, mb, g2, b2, sb, g_jb, g_xb = (f[n].reshape(-1) for n in ("g1", "b1", "mb", "g2", "b2", "sb", "jb", "xb"))
    return f["out"], f["gt"], g1, b1, f["j"], g_jb, f["m"], mb, g2, b2, f["x"], g_xb, f["s"], sb


def layout(mesh, joint_rows, shrink_rows):
    n = mesh.shape["dp"]
    if mesh.shape["rep"] != 2 or n != 16 or joint_rows % 16 or shrink_rows % 256:
        return None
    return (n // 4, 2, 2)


def on_device(mesh, *args):
    dims = layout(mesh, args[7].shape[0], args[15].shape[0])
    if dims is None:
        return general_layer(*args)
    return fused_layer(dims, *args)


def solution(mesh):
    rows, rows2 = P(("dp", "rep")), P(("dp", "rep"), None)
    vector, matrix = P("dp"), P("dp", None)
    return jax.shard_map(
        functools.partial(on_device, mesh),
        mesh=mesh,
        in_specs=(
            rows2,
            rows,
            rows2,
            rows2,
            rows2,
            vector,
            vector,
            matrix,
            vector,
            matrix,
            vector,
            vector,
            vector,
            matrix,
            vector,
            matrix,
            vector,
        ),
        out_specs=(
            rows2,
            rows2,
            vector,
            vector,
            matrix,
            vector,
            matrix,
            vector,
            vector,
            vector,
            matrix,
            vector,
            matrix,
            vector,
        ),
        check_vma=False,
    )
```
